32 devices in a mesh: items: 16 (over z, x, core), narrow: 2 (over y).
Axes of the slice: x: 2, y: 2, z: 4, core: 2. Of those that a mesh axis runs over, the one named last changes fastest.
Arguments:
- series: bfloat16 [16, 27648], P('items'), may hold values from -6 to 6
- amplitudes: float32 [16, 5], P('items'), may hold values from -5 to 5
- periods: int32 [16, 5], P('items'), may hold values from 2 to 48, as said below
- conv_in: bfloat16 [18304, 64], replicated, may hold values from -0.25 to 0.25
- bias_in: float32 [64], replicated, may hold values from -3 to 3
- conv_out: bfloat16 [18304, 64], replicated, may hold values from -0.25 to 0.25
- bias_out: float32 [64], replicated, may hold values from -3 to 3
- norm_gain: float32 [64], replicated, may hold values from 0.5 to 1.5
- norm_bias: float32 [64], replicated, may hold values from -3 to 3
- cotangent: bfloat16 [16, 27648], P('items', 'narrow'), may hold values from -6 to 6
Outputs:
- output: bfloat16 [16, 27648], P('items', 'narrow')
- grad_series: float32 [16, 27648], P('items', 'narrow')
- grad_amplitudes: float32 [16, 5], P('items')
- grad_conv_in: float32 [18304, 64], replicated
- grad_bias_in: float32 [64], replicated
- grad_conv_out: float32 [18304, 64], replicated
- grad_bias_out: float32 [64], replicated
- grad_gain: float32 [64], replicated
- grad_norm_bias: float32 [64], replicated
The draws below stay inside these ranges and needn't reach their ends.
Inputs may be any that keep to these rules, and one draw needn't show every extreme that they name: Each item's 5 periods are distinct; some item has the period 48.
All inputs are finite; a program needn't handle non-finite values.
Results may differ from the reference program's by a relative error of at most 0.0096.
Values may be sent and summed in bfloat16 or wider, within the bound.
No kernel may reach another device: no remote copies, remote signals or barrier semaphores. Data moves between devices by JAX's collectives and lax.ppermute only.
A program may use at most 192 MiB of HBM per device.

```python
import jax
import jax.numpy as jnp
from jax import lax

D = 64
FF = 64
K = 5
TAPS = 286
STEPS = 432
PMAX = 48
ITEMS = 16
GRID = 480


def draw_periods(key, part):
    key = jax.random.fold_in(key, 11)
    first_key, second_key, third_key = jax.random.split(key, 3)
    band_width = (PMAX - 2) // K
    offsets = jax.random.randint(first_key, (ITEMS, K), 0, band_width)
    band_start = 2 + band_width * jnp.arange(K, dtype=jnp.int32)
    banded = band_start[None, :] + offsets
    chosen = jax.random.randint(second_key, (), 0, ITEMS)
    row_index = jnp.arange(ITEMS, dtype=jnp.int32)[:, None]
    col_index = jnp.arange(K, dtype=jnp.int32)[None, :]
    banded = jnp.where((row_index == chosen) & (col_index == K - 1), PMAX, banded)
    column_order = jax.vmap(lambda single: jax.random.permutation(single, K))(jax.random.split(third_key, ITEMS))
    return jnp.take_along_axis(banded, column_order, axis=1).astype(jnp.int32)


def shard_levels(own_key, extent, cuts, low, largest):
    gain = 1.0
    for dim, parts in cuts:
        draws = jax.random.uniform(jax.random.fold_in(jax.random.fold_in(own_key, 6), dim), (parts,), jnp.float32, low / len(cuts), largest / len(cuts))
        gain = gain * jnp.repeat(jnp.exp(draws), extent[dim] // parts).reshape((-1,) + (1,) * (len(extent) - 1 - dim))
    return gain


def centred(stream_key, shape, spread, bound, cuts=(), kind=jnp.bfloat16):
    entries = spread * jax.random.normal(stream_key, shape, jnp.float32)
    if cuts:
        entries = entries * shard_levels(stream_key, shape, cuts, -0.22, 0.18)
    return jnp.clip(entries, -bound, bound).astype(kind)


def setup_inputs(seed: int = 0) -> dict:
    keys = jax.random.split(jax.random.key(seed), 11)
    return {
        "series": centred(keys[0], (ITEMS, STEPS * D), 1.0, 6.0, ((0, 16),)),
        "amplitudes": centred(keys[1], (ITEMS, K), 1.0, 5.0, ((0, 16),), jnp.float32),
        "periods": draw_periods(jax.random.fold_in(keys[10], 71), 0),
        "conv_in": centred(keys[3], (TAPS * D, FF), (TAPS * D // 36) ** -0.5, 0.25),
        "bias_in": centred(keys[4], (FF,), 0.5, 3.0, (), jnp.float32),
        "conv_out": centred(keys[5], (TAPS * FF, D), (TAPS * FF // 36) ** -0.5, 0.25),
        "bias_out": centred(keys[6], (D,), 0.5, 3.0, (), jnp.float32),
        "norm_gain": jnp.clip(1.0 + 0.1 * jax.random.normal(keys[7], (D,), jnp.float32), 0.5, 1.5),
        "norm_bias": centred(keys[8], (D,), 0.5, 3.0, (), jnp.float32),
        "cotangent": centred(keys[9], (ITEMS, STEPS * D), 1.0, 6.0, ((0, 16), (1, 2))),
    }


kernel_sizes = (1, 3, 5, 7, 9, 11)
epsilon = 1e-05

@jax.custom_vjp
def low(v):
    return lax.optimization_barrier(v.astype(jnp.bfloat16)).astype(jnp.float32)

@jax.custom_vjp
def low_back(v):
    return v

def low_keep(v):
    return (low(v), None)

def low_pass(kept, grad):
    return (grad,)

def back_keep(v):
    return (v, None)

def back_low(kept, grad):
    return (low(grad),)
low.defvjp(low_keep, low_pass)
low_back.defvjp(back_keep, back_low)

def unfold(values, period, direction):
    length = values.shape[0]
    margin = 5 * PMAX + 5
    padded = jnp.pad(values, ((margin, margin), (0, 0)))
    column = jnp.arange(length, dtype=jnp.int32) % period
    shifted = {}
    for offset_row in range(-5, 6):
        begin_at = (margin - 5 + direction * offset_row * period).astype(jnp.int32)
        window = lax.dynamic_slice_in_dim(padded, begin_at, length + 10, 0)
        for offset_col in range(-5, 6):
            moved = window[5 + direction * offset_col:5 + direction * offset_col + length]
            inside = (column + direction * offset_col >= 0) & (column + direction * offset_col < period)
            shifted[offset_row, offset_col] = jnp.where(inside[:, None], moved, jnp.zeros((), values.dtype))
    pieces = []
    for kernel in kernel_sizes:
        radius = (kernel - 1) // 2
        for offset_row in range(-radius, radius + 1):
            for offset_col in range(-radius, radius + 1):
                pieces.append(shifted[offset_row, offset_col])
    return jnp.concatenate(pieces, axis=1)

def grid_mask(length, period):
    position = jnp.arange(length, dtype=jnp.int32)
    return position < (STEPS + period - 1) // period * period

def branch_forward(x_item, period, conv_in_f, bias_in_f, conv_out_f, bias_out_f):
    highest = lax.Precision.HIGHEST
    grid_input = jnp.pad(x_item, ((0, GRID - STEPS), (0, 0)))
    hidden_pre = low_back(jnp.dot(unfold(grid_input, period, 1), conv_in_f, precision=highest) / 6.0 + bias_in_f)
    active = low(jnp.where(grid_mask(GRID, period)[:, None], jax.nn.gelu(hidden_pre, approximate=False), 0.0))
    branch = jnp.dot(unfold(active, period, 1), conv_out_f, precision=highest) / 6.0 + bias_out_f
    return low(low_back(branch[:STEPS]))

def reference(series, amplitudes, periods, conv_in, bias_in, conv_out, bias_out, norm_gain, norm_bias, cotangent):

    def layer(series_f, amp_f, conv_in_f, bias_in_f, conv_out_f, bias_out_f, gain_f, shift_f):

        def one_item(item_args):
            x_flat, amp_item, period_item = item_args
            x_item = x_flat.reshape(STEPS, D)
            mixing = jax.nn.softmax(amp_item)
            merged = x_item
            for branch in range(K):
                merged = merged + mixing[branch] * branch_forward(x_item, period_item[branch], conv_in_f, bias_in_f, conv_out_f, bias_out_f)
            centered = merged - lax.optimization_barrier(jnp.mean(merged, axis=-1, keepdims=True))
            variance = lax.optimization_barrier(jnp.mean(centered * centered, axis=-1, keepdims=True))
            normed = centered * lax.rsqrt(variance + epsilon)
            return (normed * gain_f + shift_f).reshape(STEPS * D)
        return lax.map(jax.checkpoint(one_item), (series_f, amp_f, periods))
    primals = (series.astype(jnp.float32), amplitudes, conv_in.astype(jnp.float32), bias_in, conv_out.astype(jnp.float32), bias_out, norm_gain, norm_bias)
    result, pullback = jax.vjp(layer, *primals)
    grads = pullback(cotangent.astype(jnp.float32))
    return (result.astype(jnp.bfloat16), grads[0], grads[1], grads[2], grads[3], grads[4], grads[5], grads[6], grads[7])
```

```python
import functools
import math

import jax
import jax.numpy as jnp
from jax import lax
from jax.experimental import pallas as pl
from jax.experimental.pallas import tpu as pltpu
from jax.sharding import PartitionSpec as P

D = 64
FF = 64
K = 5
TAPS = 286
STEPS = 432
PMAX = 48
GRID = 480
PAIR = 448
HALF = STEPS // 2
LANES = 128
kernel_sizes = (1, 3, 5, 7, 9, 11)
epsilon = 1e-05
f32 = jnp.float32
bf16 = jnp.bfloat16

NEAR = 5 * PMAX
WIDE = 2 * FF // 2 * 6
FULL = 12 * D


def tap_index(size, row, col):
    radius = (size - 1) // 2
    first = sum(k * k for k in kernel_sizes if k < size)
    return first + (row + radius) * size + col + radius


def lane_of(rows):
    return lax.broadcasted_iota(jnp.int32, (rows, LANES), 1)


def low_half(rows):
    return lane_of(rows) < D


def both_halves(v):
    return v + pltpu.roll(v, D, 1)


def four_quarters(v):
    v = v + pltpu.roll(v, 64, 1)
    return v + pltpu.roll(v, 32, 1)


def quarter_select(parts, rows):
    lane = lane_of(rows)
    upper = jnp.where(lane < 96, parts[2], parts[3])
    lower = jnp.where(lane < 32, parts[0], parts[1])
    return jnp.where(lane < 64, lower, upper)


def rounded(v):
    return v.astype(bf16).astype(f32)


def spread_pairs(pairs, ref, start):
    rows = pairs.shape[0]
    other = pltpu.roll(pairs, D, 1)
    low = low_half(rows)
    ref[pl.ds(start, rows, stride=2), :] = jnp.where(low, pairs, other)
    ref[pl.ds(start + 1, rows, stride=2), :] = jnp.where(low, other, pairs)


def gather_pairs(ref, start, rows):
    return jnp.where(
        low_half(rows),
        ref[pl.ds(start, rows, stride=2), :],
        ref[pl.ds(start + 1, rows, stride=2), :],
    )


def combine_tile(load, rows, row, plane):
    low = low_half(rows)
    col0, col1 = 2 * plane - 5, 2 * plane - 4
    even = odd = None
    for size in kernel_sizes:
        radius = (size - 1) // 2
        in0, in1 = abs(col0) <= radius, abs(col1) <= radius
        if abs(row) > radius or not (in0 or in1):
            continue
        first = tap_index(size, row, col0)
        if first % 2 == 0:
            v = load(first // 2)
            if not in0:
                v = jnp.where(low, 0.0, v)
            if not in1:
                v = jnp.where(low, v, 0.0)
            even = v if even is None else even + v
        else:
            left = load(first // 2) if in0 else 0.0
            right = load(first // 2 + 1) if in1 else 0.0
            v = jnp.where(low, right, left)
            odd = v if odd is None else odd + v
    if odd is not None:
        odd = pltpu.roll(odd, D, 1)
        even = odd if even is None else even + odd
    return even


def column_of(period, rows, start):
    position = (lax.broadcasted_iota(jnp.int32, (rows, LANES), 0) + start).astype(f32)
    width = jnp.full((rows, LANES), period, jnp.int32).astype(f32)
    return position - jnp.floor((position + 0.5) / width) * width


def mixing_of(amp):
    shifted = jnp.exp(amp - jnp.max(amp, axis=-1, keepdims=True))
    return shifted / jnp.sum(shifted, axis=-1, keepdims=True)


def gelu_both(v):
    cdf = 0.5 * (1.0 + lax.erf(v * (1.0 / math.sqrt(2.0))))
    density = jnp.exp(-0.5 * v * v) * (1.0 / math.sqrt(2.0 * math.pi))
    return v * cdf, cdf + v * density


def forward_kernel(
    where_ref,
    periods_ref,
    amp_ref,
    x_ref,
    cot_ref,
    conv_in_ref,
    conv_out_ref,
    bias_in_ref,
    bias_out_ref,
    send_ref,
    sum_ref,
    part_ref,
    w1_ref,
    w2_ref,
    ux_ref,
    ua_ref,
    slope_ref,
    xs,
    act,
    act4,
    ys,
    ss,
    c2,
):
    side = where_ref[0]
    half = pl.multiple_of(side * 32, 32)
    for row in range(-5, 6):
        at = (row + 5) * 32
        for plane in range(6):
            lanes = slice(plane * LANES, (plane + 1) * LANES)

            def load_in(tile):
                return conv_in_ref[pl.ds(half, 32), tile * LANES : (tile + 1) * LANES].astype(f32)

            def load_out(tile):
                return conv_out_ref[:, tile * LANES : (tile + 1) * LANES].astype(f32)

            w1_ref[at : at + 32, lanes] = combine_tile(load_in, 32, row, plane).astype(bf16)
            c2[2 * at : 2 * at + 64, lanes] = combine_tile(load_out, 64, row, plane).astype(bf16)
    w1_ref[352:384, :] = jnp.zeros((32, FULL), bf16)
    c2[704:768, :] = jnp.zeros((64, FULL), bf16)
    source = lax.broadcasted_iota(jnp.int32, (FULL, WIDE), 0)
    target = lax.broadcasted_iota(jnp.int32, (FULL, WIDE), 1)
    wanted = (target // 32) * 64 + side * 32 + target % 32
    choose = (source == wanted).astype(f32).astype(bf16)
    w2_ref[...] = jnp.dot(c2[...], choose, preferred_element_type=f32).astype(bf16)

    xs[...] = jnp.zeros_like(xs)
    act[...] = jnp.zeros_like(act)
    ys[...] = jnp.zeros_like(ys)
    spread_pairs(x_ref[...].astype(f32), xs, 16)
    bias_in = jnp.concatenate([bias_in_ref[...], bias_in_ref[...]], axis=1)
    bias_in = jnp.where(side == 0, bias_in, pltpu.roll(bias_in, 96, 1))
    bias_in = four_quarters(jnp.where(lane_of(1) < 32, bias_in, 0.0))
    bias_out = jnp.concatenate([bias_out_ref[...], bias_out_ref[...]], axis=1)
    bias_out = jnp.where(side == 0, bias_out, 0.0)
    mixing = mixing_of(amp_ref[...])
    sum_ref[...] = jnp.zeros_like(sum_ref)
    step = 48

    def branch(k, carry):
        period = periods_ref[0, k]
        weight = jnp.sum(
            jnp.where(lax.broadcasted_iota(jnp.int32, (1, K), 1) == k, mixing, 0.0),
            axis=1,
            keepdims=True,
        )
        rows_used = lax.div(STEPS + period - 1, period) * period
        width = jnp.full((step, LANES), period, jnp.int32).astype(f32)
        low = low_half(step)
        lane = lane_of(step)
        for t in range(0, GRID, step):
            col = column_of(period, step, t) + jnp.where(low, 0.0, 1.0)
            for plane in range(6):
                shift = 2 * plane - 5
                moved = jnp.where(low, xs[pl.ds(16 + t + shift, step), :], xs[pl.ds(17 + t + shift, step), :])
                c = col + shift
                ux_ref[k, t : t + step, plane * LANES : (plane + 1) * LANES] = jnp.where(
                    (c >= 0.0) & (c < width), moved, 0.0
                ).astype(bf16)
        product = lax.dot_general(
            ux_ref[k], w1_ref[...], (((1,), (1,)), ((), ())), preferred_element_type=f32
        )
        for plane in range(3):
            ys[plane, NEAR : NEAR + GRID, :] = product[:, plane * LANES : (plane + 1) * LANES]
        for t in range(0, GRID + 3 * PMAX, step):
            total = ys[0, pl.ds(NEAR + t - 5 * period, step), :]
            for plane in range(1, 3):
                total = total + ys[plane, pl.ds(NEAR + t + (4 * plane - 5) * period, step), :]
            ss[t : t + step, :] = total
        for t in range(0, GRID, step):
            parts = [ss[pl.ds(t + q * period, step), :] for q in range(4)]
            hidden = four_quarters(quarter_select(parts, step)) / 6.0 + bias_in
            inside = lax.broadcasted_iota(jnp.int32, (step, LANES), 0) + t < rows_used
            active, slope = gelu_both(hidden)
            act[16 + t : 16 + t + step, :] = jnp.where(inside, rounded(active), 0.0)
            slope_ref[k, t : t + step, :] = jnp.where(inside, slope, 0.0)
        for t in range(0, 496, 16):
            parts = [act[pl.ds(8 + t + q, 16), :] for q in range(4)]
            act4[t : t + 16, :] = quarter_select(parts, 16)
        for t in range(0, GRID, step):
            col = column_of(period, step, t) + (lane // 32).astype(f32)
            for plane in range(3):
                shift = 4 * plane - 5
                c = col + shift
                ua_ref[k, t : t + step, plane * LANES : (plane + 1) * LANES] = jnp.where(
                    (c >= 0.0) & (c < width), act4[pl.ds(8 + t + shift, step), :], 0.0
                ).astype(bf16)
        product = lax.dot_general(
            ua_ref[k], w2_ref[...], (((1,), (1,)), ((), ())), preferred_element_type=f32
        )
        for plane in range(6):
            ys[plane, NEAR : NEAR + GRID, :] = product[:, plane * LANES : (plane + 1) * LANES]
        for t in range(0, GRID + PMAX, step):
            total = ys[0, pl.ds(NEAR + t - 5 * period, step), :]
            for plane in range(1, 6):
                total = total + ys[plane, pl.ds(NEAR + t + (2 * plane - 5) * period, step), :]
            ss[t : t + step, :] = total
        for t in range(0, PAIR, 56):
            own = jnp.where(low_half(56), ss[pl.ds(t, 56), :], ss[pl.ds(t + period, 56), :])
            out = both_halves(own) / 6.0 + bias_out
            part_ref[k, t : t + 56, :] = out
            sum_ref[t : t + 56, :] += weight * out
        return carry

    lax.fori_loop(0, K, branch, 0)
    send_ref[0 : PAIR // 2, :] = gather_pairs(sum_ref, 0, PAIR // 2).astype(bf16)
    send_ref[PAIR // 2 :, :] = cot_ref[...]


def backward_kernel(
    where_ref,
    periods_ref,
    amp_ref,
    x_ref,
    cot_ref,
    recv_ref,
    sum_ref,
    part_ref,
    w1_ref,
    w2_ref,
    ux_ref,
    ua_ref,
    slope_ref,
    gain_ref,
    shift_ref,
    out_ref,
    keep_ref,
    send_ref,
    own_ref,
    other_ref,
    dots_ref,
    merged,
    cot,
    outs,
    gm,
    rowed,
    gb,
    gab,
    gah,
    zs,
    vs,
    gh,
    hrow,
    dw1,
    dw2,
    zsum,
    small,
):
    side = where_ref[0]
    core = where_ref[1]
    step = 48
    spread_pairs(recv_ref[0 : PAIR // 2, :].astype(f32), merged, 0)
    spread_pairs(x_ref[...].astype(f32), outs, 0)
    mine = cot_ref[...].astype(f32)
    theirs = recv_ref[PAIR // 2 :, :].astype(f32)
    cot[...] = jnp.zeros_like(cot)
    spread_pairs(jnp.where(side == 0, mine, theirs), cot, 0)
    spread_pairs(jnp.where(side == 0, theirs, mine), cot, HALF)
    gain = jnp.concatenate([gain_ref[...], gain_ref[...]], axis=1)
    shift = jnp.concatenate([shift_ref[...], shift_ref[...]], axis=1)
    mixing = mixing_of(amp_ref[...])
    gm[...] = jnp.zeros_like(gm)
    small[...] = jnp.zeros_like(small)
    dots_ref[...] = jnp.zeros_like(dots_ref)
    rowed[...] = jnp.zeros_like(rowed)
    hrow[...] = jnp.zeros_like(hrow)
    gh[...] = jnp.zeros_like(gh)
    zs[...] = jnp.zeros_like(zs)
    zsum[...] = jnp.zeros_like(zsum)
    dw1[...] = jnp.zeros_like(dw1)
    dw2[...] = jnp.zeros_like(dw2)
    for t in range(0, PAIR, 56):
        rows = slice(t, t + 56)
        total = merged[rows, :] + outs[rows, :] + sum_ref[rows, :]
        centred = total - jnp.mean(total, axis=-1, keepdims=True)
        variance = jnp.mean(centred * centred, axis=-1, keepdims=True)
        inverse = lax.rsqrt(variance + epsilon)
        normed = centred * inverse
        outs[rows, :] = normed * gain + shift
        c = cot[rows, :]
        small[2:3, :] += jnp.sum(c * normed, axis=0, keepdims=True)
        small[3:4, :] += jnp.sum(c, axis=0, keepdims=True)
        e = c * gain
        grad = inverse * (
            e
            - jnp.mean(e, axis=-1, keepdims=True)
            - normed * jnp.mean(e * normed, axis=-1, keepdims=True)
        )
        gm[PMAX + t : PMAX + t + 56, :] = grad
        for k in range(K):
            dots_ref[k : k + 1, :] += jnp.sum(grad * part_ref[k, rows, :], axis=0, keepdims=True)
    first = pl.multiple_of(side * HALF, 8)
    out_ref[...] = gather_pairs(outs, first, 112).astype(bf16)

    def branch(k, carry):
        period = periods_ref[0, k]
        weight = jnp.sum(
            jnp.where(lax.broadcasted_iota(jnp.int32, (1, K), 1) == k, mixing, 0.0),
            axis=1,
            keepdims=True,
        )
        width = jnp.full((step, LANES), period, jnp.int32).astype(f32)
        low = low_half(step)
        lane = lane_of(step)
        for t in range(0, GRID, step):
            here = rounded(weight * gm[PMAX + t : PMAX + t + step, :])
            back = rounded(weight * gm[pl.ds(PMAX + t - period, step), :])
            small[1:2, :] += jnp.sum(here, axis=0, keepdims=True)
            rowed[NEAR + t : NEAR + t + step, :] = jnp.where(low, here, back)
        for t in range(0, GRID, step):
            for plane in range(6):
                gab[t : t + step, plane * LANES : (plane + 1) * LANES] = rowed[
                    pl.ds(NEAR + t - (2 * plane - 5) * period, step), :
                ].astype(bf16)
        product = jnp.dot(gab[...], w2_ref[...], preferred_element_type=f32)
        for t in range(0, GRID, step):
            col = column_of(period, step, t) + (lane // 32).astype(f32)
            for plane in range(3):
                c = col + (4 * plane - 5)
                zs[plane, 16 + t : 16 + t + step, :] = jnp.where(
                    (c >= 0.0) & (c < width),
                    product[t : t + step, plane * LANES : (plane + 1) * LANES],
                    0.0,
                )
        dw2[...] += lax.dot_general(
            ua_ref[k], gab[...], (((0,), (0,)), ((), ())), preferred_element_type=f32
        )
        for t in range(0, 496, 16):
            total = zs[0, pl.ds(16 - 8 + t + 5, 16), :]
            for plane in range(1, 3):
                total = total + zs[plane, pl.ds(16 - 8 + t - (4 * plane - 5), 16), :]
            vs[t : t + 16, :] = total
        for t in range(0, GRID, step):
            parts = [vs[pl.ds(8 + t - q, step), :] for q in range(4)]
            back = four_quarters(quarter_select(parts, step)) / 6.0
            grad = rounded(back * slope_ref[k, t : t + step, :])
            small[0:1, :] += jnp.sum(grad, axis=0, keepdims=True)
            gh[3 * PMAX + t : 3 * PMAX + t + step, :] = grad
        for t in range(0, GRID + 3 * PMAX, step):
            parts = [gh[pl.ds(3 * PMAX + t - q * period, step), :] for q in range(4)]
            hrow[3 * PMAX + t : 3 * PMAX + t + step, :] = quarter_select(parts, step)
        for t in range(0, GRID, step):
            for plane in range(3):
                gah[t : t + step, plane * LANES : (plane + 1) * LANES] = hrow[
                    pl.ds(3 * PMAX + t - (4 * plane - 5) * period, step), :
                ].astype(bf16)
        dw1[...] += lax.dot_general(
            gah[...], ux_ref[k], (((0,), (0,)), ((), ())), preferred_element_type=f32
        )
        product = jnp.dot(gah[...], w1_ref[...], preferred_element_type=f32)
        for t in range(0, GRID, step):
            col = column_of(period, step, t) + jnp.where(low, 0.0, 1.0)
            for plane in range(6):
                c = col + (2 * plane - 5)
                zsum[plane, 16 + t : 16 + t + step, :] += jnp.where(
                    (c >= 0.0) & (c < width),
                    product[t : t + step, plane * LANES : (plane + 1) * LANES],
                    0.0,
                )
        return carry

    lax.fori_loop(0, K, branch, 0)
    for t in range(0, 464, 16):
        total = zsum[0, pl.ds(16 - 8 + t + 5, 16), :]
        for plane in range(1, 6):
            total = total + zsum[plane, pl.ds(16 - 8 + t - (2 * plane - 5), 16), :]
        vs[t : t + 16, :] = total
    for t in range(0, PAIR, 56):
        own = jnp.where(low_half(56), vs[pl.ds(8 + t, 56), :], vs[pl.ds(8 + t - 1, 56), :])
        merged[t : t + 56, :] = both_halves(own) / 6.0
    for t in range(0, PAIR, 56):
        outs[t : t + 56, :] = merged[t : t + 56, :] + gm[PMAX + t : PMAX + t + 56, :]
    own_ref[...] = gather_pairs(outs, first, 112)
    last = pl.multiple_of((1 - side) * HALF, 8)
    other_ref[0:112, :] = gather_pairs(merged, last, 112).astype(bf16)
    dots = dots_ref[...] * 0.5
    total = jnp.broadcast_to(jnp.sum(dots, axis=1, keepdims=True), dots.shape)
    dots_ref[...] = total
    upper = rounded(total)
    other_ref[112:128, :] = jnp.concatenate([upper, total - upper], axis=0).astype(bf16)

    first_grad = dw1[...] * (1.0 / 6.0)
    second_grad = dw2[...] * (1.0 / 6.0)
    for rows in range(0, 384, 96):
        part = slice(rows, rows + 96)
        a = first_grad[part, :]
        b = second_grad[part, :]
        keep_ref[part, :] = jnp.where(core == 0, a, b).astype(bf16)
        send_ref[part, :] = jnp.where(core == 0, b, a).astype(bf16)
    spare = jnp.concatenate([small[...], jnp.zeros((8, LANES), f32)], axis=0).astype(bf16)

    @pl.when(core == 0)
    def _():
        keep_ref[352:368, 0:LANES] = spare

    @pl.when(core != 0)
    def _():
        send_ref[352:368, 0:LANES] = spare

    if keep_ref.shape[0] > 384:
        tail = jnp.zeros((keep_ref.shape[0] - 384, FULL), bf16)
        keep_ref[384:, :] = tail
        send_ref[384:, :] = tail


def final_kernel(
    places,
    block,
    where_ref,
    amp_ref,
    mine_ref,
    theirs_ref,
    own_ref,
    recv_ref,
    dots_ref,
    grad_in_ref,
    grad_out_ref,
    bias_in_ref,
    bias_out_ref,
    gain_ref,
    shift_ref,
    series_ref,
    amps_ref,
    first,
    second,
    c1,
    c1r,
    merged,
):
    core = where_ref[1]
    low = low_half(64)
    for half, target in ((0, first), (1, second)):
        for side in range(2):
            for index, place in enumerate(places[half][side]):
                if index * block >= 384:
                    continue
                a = mine_ref[place * block : (place + 1) * block, :]
                b = theirs_ref[place * block : (place + 1) * block, :]
                value = jnp.where(core == 0, a, b) if half == 0 else jnp.where(core == 0, b, a)
                target[side, index * block : (index + 1) * block, :] = value

    def expand(grad_ref):
        for tile in range(TAPS // 2):
            found = []
            for tap in (2 * tile, 2 * tile + 1):
                for size in kernel_sizes:
                    inside = tap - tap_index(size, -(size // 2), -(size // 2))
                    if 0 <= inside < size * size:
                        found.append(
                            (inside // size - size // 2 + 5, inside % size - size // 2 + 5)
                        )
            (a0, b0), (a1, b1) = found
            left = (c1 if b0 % 2 == 0 else c1r)[a0, b0 // 2]
            right = (c1 if b1 % 2 == 1 else c1r)[a1, b1 // 2]
            grad_ref[:, tile * LANES : (tile + 1) * LANES] = jnp.where(low, left, right)

    for row in range(11):
        for plane in range(6):
            lanes = slice(plane * LANES, (plane + 1) * LANES)
            for side in range(2):
                v = first[side, row * 32 : (row + 1) * 32, lanes].astype(f32)
                c1[row, plane, side * 32 : (side + 1) * 32, :] = v
                c1r[row, plane, side * 32 : (side + 1) * 32, :] = pltpu.roll(v, D, 1)
    expand(grad_in_ref)

    source = lax.broadcasted_iota(jnp.int32, (WIDE, FULL), 0)
    target = lax.broadcasted_iota(jnp.int32, (WIDE, FULL), 1)
    merge = None
    for side in range(2):
        wanted = (source // 32) * 64 + side * 32 + source % 32
        place = (target == wanted).astype(f32).astype(bf16)
        part = lax.dot_general(
            second[side], place, (((0,), (0,)), ((), ())), preferred_element_type=f32
        )
        merge = part if merge is None else merge + part
    merged[...] = merge
    for row in range(11):
        for plane in range(6):
            v = merged[row * 64 : (row + 1) * 64, plane * LANES : (plane + 1) * LANES]
            c1[row, plane] = v
            c1r[row, plane] = pltpu.roll(v, D, 1)
    expand(grad_out_ref)

    spare = first[0, 352:368, 0:LANES].astype(f32)
    other = first[1, 352:368, 0:LANES].astype(f32)
    bias_in_ref[...] = jnp.concatenate([spare[0:1, 0:32], other[0:1, 0:32]], axis=1)
    bias_out_ref[...] = spare[1:2, 0:64]
    gain_ref[...] = spare[2:3, 0:64]
    shift_ref[...] = spare[3:4, 0:64]
    series_ref[...] = own_ref[...] + recv_ref[0:112, :].astype(f32)
    tail = recv_ref[112:128, :].astype(f32)
    dots = dots_ref[...] + tail[0:8, :] + tail[8:16, :]
    mixing = mixing_of(amp_ref[...])
    pick = (
        lax.broadcasted_iota(jnp.int32, (8, K), 0) == lax.broadcasted_iota(jnp.int32, (8, K), 1)
    )
    table = jnp.sum(jnp.where(pick, dots[:, 0:K], 0.0), axis=0, keepdims=True)
    amps_ref[...] = mixing * (table - jnp.sum(mixing * table, axis=-1, keepdims=True))


def on_device(
    series,
    amplitudes,
    periods,
    conv_in,
    bias_in,
    conv_out,
    bias_out,
    norm_gain,
    norm_bias,
    cotangent,
):
    items = lax.axis_size("items")
    bits = items.bit_length() - 1
    me = lax.axis_index("items")
    side = lax.axis_index("narrow")
    core = me % 2
    where = jnp.stack([side, core]).astype(jnp.int32)
    vmem = pl.BlockSpec(memory_space=pltpu.VMEM)
    smem = pl.BlockSpec(memory_space=pltpu.SMEM)
    big = pltpu.CompilerParams(vmem_limit_bytes=58 * 1024 * 1024)
    shape = jax.ShapeDtypeStruct

    x_pairs = jnp.pad(series.reshape(HALF, LANES), ((0, 8), (0, 0)))
    cot_pairs = jnp.pad(cotangent.reshape(HALF // 2, LANES), ((0, 4), (0, 0)))
    in_flat = conv_in.T
    out_flat = conv_out.T

    send, total, part, w1, w2, ux, ua, slope = pl.pallas_call(
        forward_kernel,
        out_shape=(
            shape((PAIR // 2 + 112, LANES), bf16),
            shape((PAIR, LANES), f32),
            shape((K, PAIR, LANES), f32),
            shape((WIDE, FULL), bf16),
            shape((FULL, WIDE), bf16),
            shape((K, GRID, FULL), bf16),
            shape((K, GRID, WIDE), bf16),
            shape((K, GRID, LANES), f32),
        ),
        in_specs=[smem, smem] + [vmem] * 7,
        out_specs=[vmem] * 8,
        scratch_shapes=[
            pltpu.VMEM((512, LANES), f32),
            pltpu.VMEM((512, LANES), f32),
            pltpu.VMEM((496, LANES), f32),
            pltpu.VMEM((6, NEAR + GRID + 336, LANES), f32),
            pltpu.VMEM((GRID + 3 * PMAX, LANES), f32),
            pltpu.VMEM((FULL, FULL), bf16),
        ],
        compiler_params=big,
        name="forward",
    )(
        where,
        periods,
        amplitudes,
        x_pairs,
        cot_pairs,
        in_flat,
        out_flat,
        bias_in[None, :],
        bias_out[None, :],
    )

    def exchange(value, partner):
        pairs = []
        for item in range(items):
            for col in range(2):
                to_item, to_col = partner(item, col)
                pairs.append((item * 2 + col, to_item * 2 + to_col))
        return lax.ppermute(value, ("items", "narrow"), pairs)

    across = lambda item, col: (item, 1 - col)
    recv = exchange(send, across)

    blocks = 2 ** max(bits - 1, 0)
    block = -(-384 // (16 * blocks)) * 16
    rows = block * blocks
    out_pairs, keep, give, own, other, dots = pl.pallas_call(
        backward_kernel,
        out_shape=(
            shape((112, LANES), bf16),
            shape((rows, FULL), bf16),
            shape((rows, FULL), bf16),
            shape((112, LANES), f32),
            shape((128, LANES), bf16),
            shape((8, LANES), f32),
        ),
        in_specs=[smem, smem] + [vmem] * 13,
        out_specs=[vmem] * 6,
        scratch_shapes=[
            pltpu.VMEM((PAIR, LANES), f32),
            pltpu.VMEM((PAIR, LANES), f32),
            pltpu.VMEM((PAIR, LANES), f32),
            pltpu.VMEM((PMAX + GRID, LANES), f32),
            pltpu.VMEM((NEAR + GRID + NEAR, LANES), f32),
            pltpu.VMEM((8, LANES), f32),
            pltpu.VMEM((GRID, FULL), bf16),
            pltpu.VMEM((GRID, WIDE), bf16),
            pltpu.VMEM((3, GRID + 32, LANES), f32),
            pltpu.VMEM((GRID + 16, LANES), f32),
            pltpu.VMEM((3 * PMAX + GRID + 3 * PMAX, LANES), f32),
            pltpu.VMEM((3 * PMAX + GRID + NEAR, LANES), f32),
            pltpu.VMEM((WIDE, FULL), f32),
            pltpu.VMEM((WIDE, FULL), f32),
            pltpu.VMEM((6, GRID + 32, LANES), f32),
            pltpu.VMEM((8, LANES), f32),
        ],
        compiler_params=big,
        name="backward",
    )(
        where,
        periods,
        amplitudes,
        x_pairs,
        cot_pairs,
        recv,
        total,
        part,
        w1,
        w2,
        ux,
        ua,
        slope,
        norm_gain[None, :],
        norm_bias[None, :],
    )

    def partner_of(stage):
        def partner(item, col):
            axis = stage[item % 2]
            if axis is None:
                return (item, 1 - col)
            return (item ^ (1 << axis), col)

        return partner

    def bit_of(stage):
        values = [side if axis is None else (me >> axis) & 1 for axis in stage]
        return jnp.where(core == 0, values[0], values[1])

    received = exchange(other, across)
    order = list(range(1, bits))
    orders = (order, order[1::-1] + order[2:])
    theirs = exchange(give, lambda item, col: (item ^ 1, col)) if bits else jnp.zeros_like(give)
    acc = keep.astype(f32) + theirs.astype(f32)
    for position in range(bits - 1):
        stage = (orders[0][position], orders[1][position])
        bit = bit_of(stage)
        size = acc.shape[0] // 2
        gone = lax.dynamic_slice_in_dim(acc, (1 - bit) * size, size, 0).astype(bf16)
        stay = lax.dynamic_slice_in_dim(acc, bit * size, size, 0)
        acc = stay + exchange(gone, partner_of(stage)).astype(f32)
    mine = acc.astype(bf16)
    back = order[::-1]
    sequences = (back[:1] + [None] + back[1:], back + [None])
    for position in range(len(sequences[0])):
        stage = (sequences[0][position], sequences[1][position])
        bit = bit_of(stage)
        theirs = exchange(mine, partner_of(stage))
        mine = jnp.concatenate(
            [jnp.where(bit == 0, mine, theirs), jnp.where(bit == 0, theirs, mine)], axis=0
        )
    theirs = exchange(mine, lambda item, col: (item ^ 1, col))

    places = []
    for half in range(2):
        by_side = []
        for narrow in range(2):
            listed = []
            for index in range(blocks):
                value = {None: narrow}
                for position, axis in enumerate(orders[half]):
                    value[axis] = (index >> (len(order) - 1 - position)) & 1
                place = 0
                for position, axis in enumerate(sequences[half]):
                    place += value[axis] << position
                listed.append(place)
            by_side.append(tuple(listed))
        places.append(tuple(by_side))

    results = pl.pallas_call(
        functools.partial(final_kernel, tuple(places), block),
        out_shape=(
            shape((FF, TAPS * D), f32),
            shape((D, TAPS * FF), f32),
            shape((1, FF), f32),
            shape((1, D), f32),
            shape((1, D), f32),
            shape((1, D), f32),
            shape((112, LANES), f32),
            shape((1, K), f32),
        ),
        in_specs=[smem] + [vmem] * 6,
        out_specs=[vmem] * 8,
        scratch_shapes=[
            pltpu.VMEM((2, 384, FULL), bf16),
            pltpu.VMEM((2, 384, FULL), bf16),
            pltpu.VMEM((11, 6, 64, LANES), f32),
            pltpu.VMEM((11, 6, 64, LANES), f32),
            pltpu.VMEM((FULL, FULL), f32),
        ],
        compiler_params=big,
        name="final",
    )(where, amplitudes, mine, theirs, own, received, dots)
    grad_in, grad_out, g_bias_in, g_bias_out, g_gain, g_shift, g_series, g_amps = results
    share = HALF * D
    return (
        out_pairs[: HALF // 2].reshape(1, share),
        g_series[: HALF // 2].reshape(1, share),
        g_amps,
        grad_in.T,
        g_bias_in[0],
        grad_out.T,
        g_bias_out[0],
        g_gain[0],
        g_shift[0],
    )


def solution(mesh):
    in_specs = (
        P("items", None),
        P("items", None),
        P("items", None),
        P(),
        P(),
        P(),
        P(),
        P(),
        P(),
        P("items", "narrow"),
    )
    out_specs = (
        P("items", "narrow"),
        P("items", "narrow"),
        P("items", None),
        P(),
        P(),
        P(),
        P(),
        P(),
        P(),
    )
    return jax.shard_map(
        on_device, mesh=mesh, in_specs=in_specs, out_specs=out_specs, check_vma=False
    )
```

```python
import functools
import math

import jax
import jax.numpy as jnp
from jax import lax
from jax.experimental import pallas as pl
from jax.experimental.pallas import tpu as pltpu
from jax.sharding import PartitionSpec as P

D = 64
FF = 64
K = 5
TAPS = 286
STEPS = 432
PMAX = 48
GRID = 480
HALF = STEPS // 2
LANES = 128
kernel_sizes = (1, 3, 5, 7, 9, 11)
epsilon = 1e-05
f32 = jnp.float32
bf16 = jnp.bfloat16

PAIR = 448
FOLD = PAIR // 2
QUART = GRID // 4
NEAR = 5 * PMAX
WIDE = 12 * 32
FULL = 12 * D
HALF_IN = 1024
STEP = 48


def tap_index(size, row, col):
    radius = (size - 1) // 2
    first = sum(k * k for k in kernel_sizes if k < size)
    return first + (row + radius) * size + col + radius


def tap_place(tap):
    for size in kernel_sizes:
        inside = tap - tap_index(size, -(size // 2), -(size // 2))
        if 0 <= inside < size * size:
            return inside // size - size // 2 + 5, inside % size - size // 2 + 5
    return None


def lane_of(rows):
    return lax.broadcasted_iota(jnp.int32, (rows, LANES), 1)


def row_of(rows):
    return lax.broadcasted_iota(jnp.int32, (rows, LANES), 0)


def low_half(rows):
    return lane_of(rows) < D


def span(plane):
    return slice(plane * LANES, (plane + 1) * LANES)


def four_quarters(v):
    v = v + pltpu.roll(v, 64, 1)
    return v + pltpu.roll(v, 32, 1)


def quarter_select(parts, rows):
    lane = lane_of(rows)
    upper = jnp.where(lane < 96, parts[2], parts[3])
    lower = jnp.where(lane < 32, parts[0], parts[1])
    return jnp.where(lane < 64, lower, upper)


def pack_pieces(load, store, temp):
    rows = 24
    pieces = []
    for r in range(0, 2 * QUART, rows):

        def piece(r=r):
            low = low_half(rows)
            a, b = load(r, rows), load(2 * QUART + r, rows)
            temp[r : r + rows, :] = jnp.where(low, a, b) + pltpu.roll(jnp.where(low, b, a), 64, 1)

        pieces.append(piece)
    for r in range(0, QUART, rows):

        def piece(r=r):
            even = lane_of(rows) // 32 % 2 == 0
            a, b = temp[r : r + rows, :], temp[QUART + r : QUART + r + rows, :]
            other = jnp.where(even, pltpu.roll(a, 96, 1), pltpu.roll(b, 32, 1))
            store(r, rows, jnp.where(even, a, b) + other)

        pieces.append(piece)
    return pieces


def spread_pieces(read, target, start):
    rows = 40
    pieces = []
    for r in range(0, QUART, rows):

        def piece(r=r):
            packed = read(r, rows)
            turned = [packed if s == 0 else pltpu.roll(packed, 32 * s, 1) for s in range(4)]
            for q in range(4):
                lanes = slice(32 * q, 32 * q + 32)
                for block in range(4):
                    target[pl.ds(start(q) + block * QUART + r, rows), lanes] = turned[
                        (q - block) % 4
                    ][:, lanes]

        pieces.append(piece)
    return pieces


def rounded(v):
    return v.astype(bf16).astype(f32)


def spread_pairs(pairs, ref, start):
    rows = pairs.shape[0]
    other = pltpu.roll(pairs, D, 1)
    low = low_half(rows)
    ref[pl.ds(start, rows, stride=2), :] = jnp.where(low, pairs, other)
    ref[pl.ds(start + 1, rows, stride=2), :] = jnp.where(low, other, pairs)


def flat_pairs(ref, rows):
    return ref[...].astype(f32).reshape(rows, LANES)


def gather_pairs(ref, start, rows):
    return jnp.where(
        low_half(rows),
        ref[pl.ds(start, rows, stride=2), :],
        ref[pl.ds(start + 1, rows, stride=2), :],
    )


def combine_tile(load, rows, row, plane):
    low = low_half(rows)
    col0, col1 = 2 * plane - 5, 2 * plane - 4
    even = odd = None
    for size in kernel_sizes:
        radius = (size - 1) // 2
        in0, in1 = abs(col0) <= radius, abs(col1) <= radius
        if abs(row) > radius or not (in0 or in1):
            continue
        first = tap_index(size, row, col0)
        if first % 2 == 0:
            v = load(first // 2)
            if not in0:
                v = jnp.where(low, 0.0, v)
            if not in1:
                v = jnp.where(low, v, 0.0)
            even = v if even is None else even + v
        else:
            left = load(first // 2) if in0 else 0.0
            right = load(first // 2 + 1) if in1 else 0.0
            v = jnp.where(low, right, left)
            odd = v if odd is None else odd + v
    if odd is not None:
        odd = pltpu.roll(odd, D, 1)
        even = odd if even is None else even + odd
    return even


def widths(period):
    width = jnp.full((8, LANES), period, jnp.int32).astype(f32)
    return width, 1.0 / width


def column_of(width, inverse, rows, ahead, start):
    position = (row_of(rows) + ahead + start).astype(f32)
    many = jnp.broadcast_to(width[0:1, :], (rows, LANES))
    turns = jnp.floor((position + 0.5) * jnp.broadcast_to(inverse[0:1, :], (rows, LANES)))
    return position - turns * many


def mixing_of(amp):
    shifted = jnp.exp(amp - jnp.max(amp, axis=-1, keepdims=True))
    return shifted / jnp.sum(shifted, axis=-1, keepdims=True)


def gelu_both(v):
    cdf = 0.5 * (1.0 + lax.erf(v * (1.0 / math.sqrt(2.0))))
    density = jnp.exp(-0.5 * v * v) * (1.0 / math.sqrt(2.0 * math.pi))
    return v * cdf, cdf + v * density


def contract(a, b, dim_a, dim_b):
    return lax.dot_general(
        a, b, (((dim_a,), (dim_b,)), ((), ())), preferred_element_type=f32
    )


def together(*streams):
    lists = [list(stream) for stream in streams]
    marks = []
    for number, pieces in enumerate(lists):
        for index, piece in enumerate(pieces):
            marks.append(((index + 0.5) / len(pieces), number, piece))
    for _, _, piece in sorted(marks, key=lambda mark: mark[:2]):
        piece()


def unfold_columns(period, shifted, target):
    pieces = []
    for t in range(0, GRID, STEP):

        def piece(t=t):
            width, inverse = widths(period)
            many = jnp.broadcast_to(width[0:1, :], (STEP, LANES)).astype(bf16)
            zero = jnp.zeros((STEP, LANES), bf16)
            col = column_of(width, inverse, STEP, 0, t)
            col = (col + jnp.where(low_half(STEP), 0.0, 1.0)).astype(bf16)
            for plane in range(6):
                shift = 2 * plane - 5
                inside = (col >= jnp.asarray(-shift, bf16)) & (col < many - jnp.asarray(shift, bf16))
                target[t : t + STEP, span(plane)] = jnp.where(
                    inside, shifted[plane, t : t + STEP, :], zero
                )

        pieces.append(piece)
    return pieces


def shift_columns(xs, shifted):
    for t in range(0, GRID, STEP):
        low = low_half(STEP)
        for plane in range(6):
            at = 16 + t + 2 * plane - 5
            shifted[plane, t : t + STEP, :] = jnp.where(
                low, xs[pl.ds(at, STEP), :], xs[pl.ds(at + 1, STEP), :]
            ).astype(bf16)


def product_pieces(read, read_weight, target, start, planes, dims):
    pieces = []
    for plane in range(0, planes, 2):

        def piece(plane=plane):
            count = min(2, planes - plane)
            lanes = slice(plane * LANES, (plane + count) * LANES)
            product = contract(read(), read_weight(lanes), *dims)
            for index in range(count):
                target[plane + index, start : start + GRID, :] = product[:, span(index)]

        pieces.append(piece)
    return pieces


def weight_pieces(read, read_other, total, first):
    def piece():
        value = contract(read(), read_other(), 0, 0)
        if first:
            total[...] = value
        else:
            total[...] += value

    return [piece]


def forward_kernel(
    where_ref,
    periods_hbm,
    amp_hbm,
    x_hbm,
    cot_hbm,
    conv_in_hbm,
    conv_out_hbm,
    bias_in_hbm,
    bias_out_hbm,
    send_ref,
    total,
    part_ref,
    w1_hbm,
    w2_hbm,
    xs,
    ua_ref,
    slope_ref,
    w1_wide,
    w2_wide,
    r2,
    ux_ref,
    periods_ref,
    amp_ref,
    x_ref,
    cot_ref,
    conv_in_ref,
    conv_out_ref,
    bias_in_ref,
    bias_out_ref,
    xb,
    c2,
    act0,
    act1,
    ys0,
    ys1,
    ys2,
    zs0,
    zs1,
    ss0,
    ss1,
    st0,
    st1,
    tp0,
    tp1,
    sems,
    sent,
):
    side = where_ref[0]
    half = pl.multiple_of(side * 32, 32)
    sources = [
        (x_hbm, x_ref),
        (periods_hbm, periods_ref),
        (amp_hbm, amp_ref),
        (bias_in_hbm, bias_in_ref),
        (bias_out_hbm, bias_out_ref),
        (cot_hbm, cot_ref),
    ]
    for piece in range(2):
        rows = pl.ds(pl.multiple_of(half + 16 * piece, 16), 16)
        sources.append((conv_in_hbm.at[rows, :], conv_in_ref.at[pl.ds(16 * piece, 16), :]))
    for piece in range(4):
        rows = pl.ds(16 * piece, 16)
        sources.append((conv_out_hbm.at[rows, :], conv_out_ref.at[rows, :]))
    copies = [pltpu.make_async_copy(a, b, sems.at[i]) for i, (a, b) in enumerate(sources)]
    for copy in copies:
        copy.start()
    xs[...] = jnp.zeros_like(xs)
    for ref in (act0, act1):
        ref[...] = jnp.zeros_like(ref)
    for ref in (ys0, ys1, ys2, zs0, zs1):
        ref[:, 0:NEAR, :] = jnp.zeros((ref.shape[0], NEAR, LANES), f32)
        ref[:, NEAR + GRID :, :] = jnp.zeros((ref.shape[0], ref.shape[1] - NEAR - GRID, LANES), f32)
    source = lax.broadcasted_iota(jnp.int32, (2 * LANES, LANES), 0)
    target = lax.broadcasted_iota(jnp.int32, (2 * LANES, LANES), 1)
    wanted = (target // 32) * 64 + side * 32 + target % 32
    choose = (source == wanted).astype(f32).astype(bf16)
    w1_wide[352:384, :] = jnp.zeros((32, FULL), bf16)
    c2[704:768, :] = jnp.zeros((64, FULL), bf16)
    r2[704:768, :] = jnp.zeros((64, 2 * LANES), bf16)

    copies[0].wait()
    spread_pairs(flat_pairs(x_ref, HALF), xs, 16)
    shift_columns(xs, xb)
    for copy in copies[1:6]:
        copy.wait()
    bias_in = jnp.concatenate([bias_in_ref[...], bias_in_ref[...]], axis=1)
    bias_in = jnp.where(side == 0, bias_in, pltpu.roll(bias_in, 96, 1))
    bias_in = four_quarters(jnp.where(lane_of(1) < 32, bias_in, 0.0))
    bias_out = jnp.concatenate([bias_out_ref[...], bias_out_ref[...]], axis=1)
    bias_out = jnp.where(side == 0, bias_out, 0.0)
    mixing = mixing_of(amp_ref[...])
    leaving = []

    def leave(ref, target):
        copy = pltpu.make_async_copy(ref, target, sent.at[len(leaving)])
        copy.start()
        leaving.append(copy)

    def unfold(k):
        return unfold_columns(periods_ref[0, k], xb, ux_ref.at[k])

    def first_product(k):
        target = (ys0, ys1, ys2)[k % 3]

        def piece():
            product = contract(ux_ref[k], w1_wide[...], 1, 1)
            for plane in range(3):
                value = product[:, span(plane)]
                if plane == 1:
                    value = value + product[:, span(3)]
                target[plane, NEAR : NEAR + GRID, :] = value

        return [piece]

    def second_product(k):
        target = (zs0, zs1)[k % 2]
        pieces = []
        for plane in range(0, 6, 2):

            def piece(plane=plane):
                lanes = slice(plane * LANES, (plane + 2) * LANES)
                value = ua_ref[k]
                value = jnp.concatenate([value, value[:, span(1)]], axis=1)
                product = contract(value, w2_wide[lanes, :], 1, 1)
                for index in range(2):
                    target[plane + index, NEAR : NEAR + GRID, :] = product[:, span(index)]

            pieces.append(piece)
        return pieces

    def activate(k):
        ys, ss, act, temp = (ys0, ys1, ys2)[k % 3], (ss0, ss1)[k % 2], (act0, act1)[k % 2], (tp0, tp1)[k % 2]
        period = periods_ref[0, k]
        used = lax.div(STEPS + period - 1, period) * period
        pieces = []
        for t in range(0, GRID + 3 * PMAX, STEP):

            def piece(t=t):
                value = ys[0, pl.ds(NEAR + t - 5 * period, STEP), :]
                for plane in range(1, 3):
                    value = value + ys[plane, pl.ds(NEAR + t + (4 * plane - 5) * period, STEP), :]
                ss[t : t + STEP, :] = value

            pieces.append(piece)

        def load(r, rows):
            return quarter_select([ss[pl.ds(r + q * period, rows), :] for q in range(4)], rows)

        def store(r, rows, value):
            hidden = value * (1.0 / 6.0) + bias_in
            active, slope = gelu_both(hidden)
            position = row_of(rows) + r + QUART * (lane_of(rows) // 32)
            slope_ref[k, r : r + rows, :] = jnp.where(position < used, slope, 0.0)
            temp[r : r + rows, :] = jnp.where(position < used, active, 0.0)

        pieces += pack_pieces(load, store, temp)
        pieces += spread_pieces(lambda r, rows: temp[r : r + rows, :], act, lambda q: 16 - q)
        for t in range(0, GRID, STEP):

            def piece(t=t):
                width, inverse = widths(period)
                many = jnp.broadcast_to(width[0:1, :], (STEP, LANES)).astype(bf16)
                zero = jnp.zeros((STEP, LANES), bf16)
                col = column_of(width, inverse, STEP, 0, t) + (lane_of(STEP) // 32).astype(f32)
                col = col.astype(bf16)
                for plane in range(3):
                    shift = 4 * plane - 5
                    inside = (col >= jnp.asarray(-shift, bf16)) & (
                        col < many - jnp.asarray(shift, bf16)
                    )
                    moved = act[pl.ds(16 + t + shift, STEP), :].astype(bf16)
                    ua_ref[k, t : t + STEP, span(plane)] = jnp.where(inside, moved, zero)

            pieces.append(piece)
        return pieces

    def finish(k):
        zs, ss = (zs0, zs1)[k % 2], (st0, st1)[k % 2]
        period = periods_ref[0, k]
        weight = mixing[:, k : k + 1]
        pieces = []
        for t in range(0, GRID + PMAX, STEP):

            def piece(t=t):
                value = zs[0, pl.ds(NEAR + t - 5 * period, STEP), :]
                for plane in range(1, 6):
                    value = value + zs[plane, pl.ds(NEAR + t + (2 * plane - 5) * period, STEP), :]
                ss[t : t + STEP, :] = value

            pieces.append(piece)
        rows = 32
        for r in range(0, FOLD, rows):

            def piece(r=r):
                low = low_half(rows)
                near = jnp.where(low, ss[pl.ds(r, rows), :], ss[pl.ds(FOLD + r + period, rows), :])
                far = jnp.where(low, ss[pl.ds(FOLD + r, rows), :], ss[pl.ds(r + period, rows), :])
                out = (near + pltpu.roll(far, D, 1)) * (1.0 / 6.0) + bias_out
                part_ref[k, r : r + rows, :] = out
                if k == 0:
                    total[r : r + rows, :] = weight * out
                else:
                    total[r : r + rows, :] += weight * out

            pieces.append(piece)
        return pieces

    def combine_in():
        pieces = []
        for row in range(-5, 6):

            def piece(row=row):
                at = (row + 5) * 32
                for plane in range(6):
                    v = combine_tile(lambda tile: conv_in_ref[:, span(tile)].astype(f32), 32, row, plane)
                    w1_wide[at : at + 32, span(plane)] = v.astype(bf16)
                    if -1 <= row <= 2:
                        w1_wide[WIDE + at - 128 : WIDE + at - 96, span(plane)] = (v - rounded(v)).astype(bf16)

            pieces.append(piece)
        return pieces

    def combine_out():
        pieces = []
        for row in range(-5, 6):

            def piece(row=row):
                at = (row + 5) * 64
                for plane in range(6):
                    v = combine_tile(lambda tile: conv_out_ref[:, span(tile)].astype(f32), 64, row, plane)
                    c2[at : at + 64, span(plane)] = v.astype(bf16)
                    if plane // 2 == 1:
                        r2[at : at + 64, span(plane % 2)] = (v - rounded(v)).astype(bf16)

            pieces.append(piece)
        return pieces

    def choose_half():
        pieces = []
        for plane in range(3):

            def piece(plane=plane):
                lanes = slice(2 * plane * LANES, 2 * (plane + 1) * LANES)
                w2_wide[:, span(plane)] = jnp.dot(
                    c2[:, lanes], choose, preferred_element_type=f32
                ).astype(bf16)

            pieces.append(piece)

        def piece():
            w2_wide[:, span(3)] = jnp.dot(r2[...], choose, preferred_element_type=f32).astype(bf16)

        return pieces + [piece]

    together(unfold(0))
    together(unfold(1))
    for copy in copies[6:]:
        copy.wait()
    together(combine_in())
    leave(w1_wide.at[pl.ds(0, WIDE), :], w1_hbm)
    combining = combine_out()
    together(first_product(0), combining[:6])
    together(first_product(1), combining[6:], unfold(2))
    together(choose_half(), activate(0))
    leave(w2_wide.at[:, pl.ds(0, WIDE)], w2_hbm)
    together(first_product(2), activate(1), unfold(3))
    together(second_product(0), activate(2))
    together(first_product(3), finish(0), unfold(4))
    together(second_product(1), activate(3))
    together(first_product(4), finish(1))
    together(second_product(2), activate(4))
    together(second_product(3), finish(2))
    together(second_product(4), finish(3))
    together(finish(4))

    send_ref[0:FOLD, :] = total[...].astype(bf16)
    send_ref[FOLD:, :] = jnp.concatenate(
        [flat_pairs(cot_ref, HALF // 2), jnp.zeros((4, LANES), f32)], axis=0
    ).astype(bf16)
    for copy in leaving:
        copy.wait()


def outer_kernel(
    where_ref,
    periods_ref,
    amp_ref,
    cot_ref,
    recv_ref,
    own_ref,
    xs,
    part_ref,
    w1_hbm,
    w2_hbm,
    ua_ref,
    slope_ref,
    gain_ref,
    shift_ref,
    out_hbm,
    keep_ref,
    send_ref,
    grad_ref,
    merged_ref,
    dots_ref,
    small,
    w1_ref,
    other,
    cot,
    outs,
    gm,
    gmp,
    rw0,
    rw1,
    gb0,
    gb1,
    zs0,
    zs1,
    vs0,
    vs1,
    tp0,
    tp1,
    dw,
    packed,
    w2_ref,
    out_ref,
    sems,
    out_sem,
):
    coming = [
        pltpu.make_async_copy(w2_hbm, w2_ref, sems.at[0]),
        pltpu.make_async_copy(w1_hbm, w1_ref, sems.at[1]),
    ]
    for copy in coming:
        copy.start()
    side = where_ref[0]
    core = where_ref[1]
    mixing = mixing_of(amp_ref[...])
    small[...] = jnp.zeros_like(small)
    for ref in (rw0, rw1):
        ref[0:NEAR, :] = jnp.zeros((NEAR, LANES), f32)
        ref[NEAR + GRID :, :] = jnp.zeros((NEAR, LANES), f32)
    for ref in (zs0, zs1):
        ref[:, 0:16, :] = jnp.zeros((3, 16, LANES), f32)
        ref[:, 16 + GRID :, :] = jnp.zeros((3, 16, LANES), f32)
    gm[0:PMAX, :] = jnp.zeros((PMAX, LANES), f32)
    gm[PMAX + PAIR :, :] = jnp.zeros((GRID - PAIR, LANES), f32)

    low = low_half(FOLD)
    v = own_ref[...] + recv_ref[0:FOLD, :].astype(f32)
    turned = pltpu.roll(v, D, 1)
    other[0:FOLD, :] = jnp.where(low, v, turned)
    other[FOLD:, :] = jnp.where(low, turned, v)
    mine = flat_pairs(cot_ref, HALF // 2)
    theirs = recv_ref[FOLD:, :].astype(f32)[: HALF // 2, :]
    cot[STEPS:, :] = jnp.zeros((PAIR - STEPS, LANES), f32)
    spread_pairs(jnp.where(side == 0, mine, theirs), cot, 0)
    spread_pairs(jnp.where(side == 0, theirs, mine), cot, HALF)
    gain = jnp.concatenate([gain_ref[...], gain_ref[...]], axis=1)
    shift = jnp.concatenate([shift_ref[...], shift_ref[...]], axis=1)
    grad_gain = grad_shift = grad_bias = jnp.zeros((8, LANES), f32)

    def eights(v):
        return jnp.sum(v.reshape(-1, 8, LANES), axis=0)

    for t in range(0, PAIR, 56):
        rows = slice(t, t + 56)
        total = xs[16 + t : 16 + t + 56, :] + other[rows, :]
        centred = total - jnp.mean(total, axis=-1, keepdims=True)
        variance = jnp.mean(centred * centred, axis=-1, keepdims=True)
        inverse = lax.rsqrt(variance + epsilon)
        normed = centred * inverse
        outs[rows, :] = normed * gain + shift
        c = cot[rows, :]
        grad_gain = grad_gain + eights(c * normed)
        grad_shift = grad_shift + eights(c)
        e = c * gain
        grad = inverse * (
            e
            - jnp.mean(e, axis=-1, keepdims=True)
            - normed * jnp.mean(e * normed, axis=-1, keepdims=True)
        )
        gm[PMAX + t : PMAX + t + 56, :] = grad
        merged_ref[rows, :] = grad
        grad_bias = grad_bias + eights(grad)
    grad_bias = grad_bias * jnp.sum(mixing, axis=-1, keepdims=True)
    small[1:2, :] = jnp.sum(grad_bias, axis=0, keepdims=True)
    small[2:3, :] = jnp.sum(grad_gain, axis=0, keepdims=True)
    small[3:4, :] = jnp.sum(grad_shift, axis=0, keepdims=True)
    first = pl.multiple_of(side * HALF, 8)
    out_ref[...] = gather_pairs(outs, first, HALF // 2).reshape(1, HALF * D).astype(bf16)
    leaving = pltpu.make_async_copy(out_ref, out_hbm, out_sem)
    leaving.start()
    rows = 32
    for r in range(0, FOLD, rows):
        gmp[r : r + rows, :] = jnp.where(
            low_half(rows),
            gm[PMAX + r : PMAX + r + rows, :],
            gm[PMAX + FOLD + r : PMAX + FOLD + r + rows, :],
        )

    def unfold(k):
        rowed, gab = (rw0, rw1)[k % 2], (gb0, gb1)[k % 2]
        period = periods_ref[0, k]
        weight = mixing[:, k : k + 1]
        pieces = []
        for t in range(0, GRID, STEP):

            def piece(t=t):
                here = gm[PMAX + t : PMAX + t + STEP, :]
                back = gm[pl.ds(PMAX + t - period, STEP), :]
                rowed[NEAR + t : NEAR + t + STEP, :] = weight * jnp.where(low_half(STEP), here, back)

            pieces.append(piece)
        for t in range(0, GRID, STEP):

            def piece(t=t):
                for plane in range(6):
                    gab[t : t + STEP, span(plane)] = rowed[
                        pl.ds(NEAR + t - (2 * plane - 5) * period, STEP), :
                    ].astype(bf16)

            pieces.append(piece)
        return pieces

    def back(k):
        return product_pieces(
            lambda: (gb0, gb1)[k % 2][...], lambda lanes: w2_ref[:, lanes], (zs0, zs1)[k % 2], 16, 3, (1, 0)
        )

    def weigh(k):
        return weight_pieces(lambda: ua_ref[k], lambda: (gb0, gb1)[k % 2][...], dw, k == 0)

    def fold(k):
        zs, vs, temp = (zs0, zs1)[k % 2], (vs0, vs1)[k % 2], (tp0, tp1)[k % 2]
        period = periods_ref[0, k]
        rows = 16
        pieces = []
        for t in range(0, GRID + 16, rows):

            def piece(t=t):
                width, inverse = widths(period)
                many = jnp.broadcast_to(width[0:1, :], (rows, LANES))
                quarter = lane_of(rows) // 32
                place = column_of(width, inverse, rows, quarter, t - 8) - quarter.astype(f32)
                value = None
                for plane in range(3):
                    s = 4 * plane - 5
                    v = zs[plane, pl.ds(16 - 8 + t - s, rows), :]
                    v = jnp.where((place >= s) & (place < many + s), v, 0.0)
                    value = v if value is None else value + v
                vs[t : t + rows, :] = value

            pieces.append(piece)

        def load(r, rows):
            return quarter_select([vs[pl.ds(8 + r - q, rows), :] for q in range(4)], rows)

        def store(r, rows, value):
            grad_ref[k, r : r + rows, :] = value * slope_ref[k, r : r + rows, :] * (1.0 / 6.0)

        return pieces + pack_pieces(load, store, temp)

    together(unfold(0))
    coming[0].wait()
    for k in range(K):
        streams = [back(k)]
        if k + 1 < K:
            streams.append(unfold(k + 1))
        together(*streams)
        together(weigh(k), fold(k))
    coming[1].wait()
    leaving.wait()
    bias = None
    for k in range(K):
        v = jnp.sum(grad_ref[k], axis=0, keepdims=True)
        bias = v if bias is None else bias + v
        dots_ref[k : k + 1, :] = jnp.sum(gmp[...] * part_ref[k], axis=0, keepdims=True)
    dots_ref[K:, :] = jnp.zeros((8 - K, LANES), f32)
    small[0:1, :] = four_quarters(bias)
    count = keep_ref.shape[0]
    turned = jnp.transpose((dw[...] * (1.0 / 6.0)).astype(bf16))
    for part in range(2):
        for plane in range(3):
            for row in range(11):
                target = part * count + plane * 352 + row * 32
                source = row * 64 + part * 32
                packed[target : target + 32, :] = turned[source : source + 32, span(plane)]
        packed[part * count + 1056 : (part + 1) * count, :] = jnp.zeros((count - 1056, LANES), bf16)
    keep_ref[...] = packed[pl.ds(pl.multiple_of(core * count, 16), count), :]
    send_ref[...] = packed[pl.ds(pl.multiple_of((1 - core) * count, 16), count), :]


def unfold_rows(period, read, rowed, target, clear):
    edge = 3 * PMAX
    pieces = []
    if clear:

        def piece():
            rowed[edge : 2 * edge, :] = jnp.zeros((edge, LANES), f32)
            rowed[edge + GRID : 2 * edge + GRID, :] = jnp.zeros((edge, LANES), f32)

        pieces.append(piece)
    pieces += spread_pieces(read, rowed, lambda q: edge + q * period)
    for t in range(0, GRID, STEP):

        def piece(t=t):
            for plane in range(3):
                target[t : t + STEP, span(plane)] = rowed[
                    pl.ds(edge + t - (4 * plane - 5) * period, STEP), :
                ].astype(bf16)

        pieces.append(piece)
    return pieces


def copy_scale():
    number = row_of(48) // 4 * 2 + lane_of(48) // D
    return jnp.exp(number.astype(f32) * (math.log(2.0) / 24.0))


def inner_kernel(
    where_ref,
    periods_ref,
    grad_ref,
    small_ref,
    xs,
    keep_ref,
    send_ref,
    hr0,
    hr1,
    xb,
    gh0,
    gh1,
    ux0,
    ux1,
    dw,
    packed,
):
    core = where_ref[1]
    for ref in (hr0, hr1):
        ref[...] = jnp.zeros_like(ref)
    shift_columns(xs, xb)

    def unfold(k):
        return unfold_rows(
            periods_ref[0, k],
            lambda r, rows: grad_ref[k, r : r + rows, :],
            (hr0, hr1)[k % 2],
            (gh0, gh1)[k % 2],
            k > 1,
        )

    def again(k):
        return unfold_columns(periods_ref[0, k], xb, (ux0, ux1)[k % 2])

    def weigh(k):
        return weight_pieces(lambda: (gh0, gh1)[k % 2][...], lambda: (ux0, ux1)[k % 2][...], dw, k == 0)

    together(unfold(0), again(0))
    for k in range(K):
        streams = [weigh(k)]
        if k + 1 < K:
            streams += [unfold(k + 1), again(k + 1)]
        together(*streams)

    sixth = 1.0 / 6.0
    for part in range(2):
        at = part * HALF_IN
        for row in range(11):
            source = slice(row * 32 + part * 16, row * 32 + part * 16 + 16)
            for plane in range(5):
                target = at + plane * 176 + row * 16
                packed[target : target + 16, :] = (dw[source, span(plane)] * sixth).astype(bf16)
        for row in range(6):
            source = slice(row * 32 + part * 16, row * 32 + part * 16 + 16)
            other = slice((row + 6) * 32 + part * 16, (row + 6) * 32 + part * 16 + 16)
            v = jnp.where(low_half(16), dw[source, span(5)], pltpu.roll(dw[other, span(5)], D, 1))
            packed[at + 880 + row * 16 : at + 896 + row * 16, :] = (v * sixth).astype(bf16)
        packed[at + 976 : at + 1024, :] = (
            jnp.concatenate([small_ref[0:4, :]] * 12, axis=0) * copy_scale()
        ).astype(bf16)
    count = HALF_IN
    keep_ref[...] = packed[pl.ds(pl.multiple_of(core * count, count), count), :]
    send_ref[...] = packed[pl.ds(pl.multiple_of((1 - core) * count, count), count), :]


def series_pieces(branches, periods_ref, grad_ref, w1_ref, vs, begun, rowed, hidden, planes):
    for ref in rowed:
        ref[...] = jnp.zeros_like(ref)
    for ref in planes:
        ref[:, 0:16, :] = jnp.zeros((6, 16, LANES), f32)
        ref[:, 16 + GRID :, :] = jnp.zeros((6, 16, LANES), f32)

    def unfold(index):
        k = branches[index]
        return unfold_rows(
            periods_ref[0, k],
            lambda r, rows: grad_ref[k, r : r + rows, :],
            rowed[index % 2],
            hidden[index % 2],
            index > 1,
        )

    def back(index):
        return product_pieces(
            lambda: hidden[index % 2][...],
            lambda lanes: w1_ref[:, lanes],
            planes[index % 2],
            16,
            6,
            (1, 0),
        )

    def fold(index):
        zs = planes[index % 2]
        period = periods_ref[0, branches[index]]
        rows = 16
        pieces = []
        for t in range(0, PAIR + 16, rows):

            def piece(t=t):
                width, inverse = widths(period)
                many = jnp.broadcast_to(width[0:1, :], (rows, LANES))
                half = lane_of(rows) // D
                place = column_of(width, inverse, rows, half, t - 8) - half.astype(f32)
                value = None if begun is None or index else begun[t : t + rows, :]
                for plane in range(6):
                    s = 2 * plane - 5
                    v = zs[plane, pl.ds(16 - 8 + t - s, rows), :]
                    v = jnp.where((place >= s) & (place < many + s), v, 0.0)
                    value = v if value is None else value + v
                if index == 0:
                    vs[t : t + rows, :] = value
                else:
                    vs[t : t + rows, :] += value

            pieces.append(piece)
        return pieces

    count = len(branches)
    together(unfold(0))
    together(back(0), *([unfold(1)] if count > 1 else []))
    for index in range(count):
        streams = [fold(index)]
        if index + 1 < count:
            streams.append(back(index + 1))
        if index + 2 < count:
            streams.append(unfold(index + 2))
        together(*streams)


def series_kernel(periods_ref, grad_ref, w1_ref, vs, hr0, hr1, gh0, gh1, zs0, zs1):
    series_pieces(
        range(0, 3), periods_ref, grad_ref, w1_ref, vs, None, (hr0, hr1), (gh0, gh1), (zs0, zs1)
    )


def series_rest_kernel(
    where_ref,
    periods_ref,
    grad_ref,
    merged_ref,
    dots_ref,
    w1_ref,
    begun_ref,
    own_ref,
    other_ref,
    table_ref,
    hr0,
    hr1,
    gh0,
    gh1,
    zs0,
    zs1,
    vs,
    dx,
    outs,
):
    side = where_ref[0]
    series_pieces(
        range(3, K), periods_ref, grad_ref, w1_ref, vs, begun_ref, (hr0, hr1), (gh0, gh1), (zs0, zs1)
    )
    rows = 56
    for t in range(0, PAIR, rows):
        v = jnp.where(low_half(rows), vs[pl.ds(8 + t, rows), :], vs[pl.ds(8 + t - 1, rows), :])
        v = (v + pltpu.roll(v, D, 1)) * (1.0 / 6.0)
        dx[t : t + rows, :] = v
        outs[t : t + rows, :] = v + merged_ref[t : t + rows, :]
    own_ref[...] = gather_pairs(outs, pl.multiple_of(side * HALF, 8), HALF // 2)
    other_ref[0:112, :] = gather_pairs(dx, pl.multiple_of((1 - side) * HALF, 8), 112).astype(bf16)
    table = jnp.broadcast_to(jnp.sum(dots_ref[...], axis=1, keepdims=True), (8, LANES))
    table_ref[...] = table
    upper = table.astype(bf16).astype(f32)
    other_ref[112:128, :] = jnp.concatenate([upper, table - upper], axis=0).astype(bf16)


def rows_of(places, block, read, part, side, start, count):
    pieces = []
    while count:
        index, inside = divmod(start, block)
        take = min(count, block - inside)
        at = places[part][side][index] * block + inside
        pieces.append(read(at, take))
        start, count = start + take, count - take
    return pieces[0] if len(pieces) == 1 else jnp.concatenate(pieces, axis=0)


def half_turns():
    source = lax.broadcasted_iota(jnp.int32, (2 * LANES, 2 * LANES), 0)
    target = lax.broadcasted_iota(jnp.int32, (2 * LANES, 2 * LANES), 1)
    return (source == target // LANES * LANES + (target + D) % LANES).astype(f32).astype(bf16)


def expand(straight, turned, rows, grads, send):
    low = low_half(rows)
    copies = []
    for tile in range(TAPS // 2):
        (a0, b0), (a1, b1) = tap_place(2 * tile), tap_place(2 * tile + 1)
        left = (straight if b0 % 2 == 0 else turned)[b0 // 2, a0 * rows : (a0 + 1) * rows, :]
        right = (straight if b1 % 2 == 1 else turned)[b1 // 2, a1 * rows : (a1 + 1) * rows, :]
        grads[:, span(tile)] = jnp.where(low, left, right)
        if tile % 13 == 12:
            copies += send(tile // 13, pl.ds((tile - 12) * LANES, 13 * LANES))
    return copies


def read_half(places, block, core, part_is_mine, half_ref):
    part = core if part_is_mine else 1 - core

    def rows(side, start, count):
        def value(which):
            return rows_of(
                places, block, lambda at, take: half_ref[at : at + take, :], which, side, start, count
            )

        return jnp.where(part == 0, value(0), value(1))

    return part, rows


def expand_inner(part, rows, grad_hbm, both, straight, turned, grads, sems):
    for side in range(2):
        for row in range(11):
            at = row * 32 + side * 16
            for plane in range(5):
                both[at : at + 16, span(plane)] = rows(side, plane * 176 + row * 16, 16)
            v = rows(side, 880 + row % 6 * 16, 16)
            if row >= 6:
                v = pltpu.roll(v.astype(f32), D, 1).astype(bf16)
            both[at : at + 16, span(5)] = v
    turn = half_turns()
    for pair in range(3):
        lanes = slice(2 * pair * LANES, 2 * (pair + 1) * LANES)
        v = both[:, lanes]
        swapped = jnp.dot(v, turn, preferred_element_type=f32)
        for plane in range(2):
            straight[2 * pair + plane] = v[:, span(plane)].astype(f32)
            turned[2 * pair + plane] = swapped[:, span(plane)]

    def send(index, lanes):
        copies = []
        for side in range(2):
            target = pl.ds(pl.multiple_of(side * 32 + part * 16, 16), 16)
            copy = pltpu.make_async_copy(
                grads.at[pl.ds(side * 16, 16), lanes], grad_hbm.at[target, lanes], sems.at[2 * index + side]
            )
            copy.start()
            copies.append(copy)
        return copies

    return expand(straight, turned, 32, grads, send)


def expand_outer(part, rows, grad_hbm, both, straight, turned, grads, sems):
    for side in range(2):
        for plane in range(3):
            both[:, span(2 * plane + side)] = rows(side, plane * 352, 352)
    source = lax.broadcasted_iota(jnp.int32, (2 * LANES, 2 * LANES), 0)
    target = lax.broadcasted_iota(jnp.int32, (2 * LANES, 2 * LANES), 1)
    wanted = (target // 64) * 32 + target % 32 + LANES * (target // 32 % 2)
    place = (source == wanted).astype(f32).astype(bf16)
    other = target // LANES * LANES + (target + D) % LANES
    wanted = (other // 64) * 32 + other % 32 + LANES * (other // 32 % 2)
    place_turned = (source == wanted).astype(f32).astype(bf16)
    for pair in range(3):
        v = both[:, 2 * pair * LANES : 2 * (pair + 1) * LANES]
        for target_ref, matrix in ((straight, place), (turned, place_turned)):
            moved = jnp.dot(v, matrix, preferred_element_type=f32)
            for plane in range(2):
                target_ref[2 * pair + plane] = moved[:, span(plane)]

    def send(index, lanes):
        target = pl.ds(pl.multiple_of(part * 32, 32), 32)
        copy = pltpu.make_async_copy(grads.at[:, lanes], grad_hbm.at[target, lanes], sems.at[index])
        copy.start()
        return [copy]

    return expand(straight, turned, 32, grads, send)


def first_last_kernel(plan_out, where_ref, mine_ref, grad_hbm, *scratch):
    part, rows = read_half(*plan_out, where_ref[1], True, mine_ref)
    for copy in expand_outer(part, rows, grad_hbm, *scratch):
        copy.wait()


def second_last_kernel(
    plan_out,
    plan_in,
    where_ref,
    amp_ref,
    theirs_ref,
    mine_ref,
    own_ref,
    recv_ref,
    table_ref,
    begun_hbm,
    grad_out_hbm,
    grad_in_hbm,
    series_hbm,
    amps_hbm,
    series_ref,
    amps_ref,
    small_sems,
    *scratch,
):
    core = where_ref[1]
    gained = own_ref[...] + recv_ref[0:112, :].astype(f32)[: HALF // 2, :]
    series_ref[...] = gained.reshape(1, HALF * D)
    tail = recv_ref[112:128, :].astype(f32)
    dots = table_ref[...] + tail[0:8, :] + tail[8:16, :]
    mixing = mixing_of(amp_ref[...])
    pick = (
        lax.broadcasted_iota(jnp.int32, (8, K), 0) == lax.broadcasted_iota(jnp.int32, (8, K), 1)
    )
    table = jnp.sum(jnp.where(pick, dots[:, 0:K], 0.0), axis=0, keepdims=True)
    amps_ref[...] = mixing * (table - jnp.sum(mixing * table, axis=-1, keepdims=True))
    copies = [
        pltpu.make_async_copy(series_ref, series_hbm, small_sems.at[0]),
        pltpu.make_async_copy(amps_ref, amps_hbm, small_sems.at[1]),
    ]
    for copy in copies:
        copy.start()
    part, rows = read_half(*plan_out, core, False, theirs_ref)
    copies += expand_outer(part, rows, grad_out_hbm, *scratch[:5])
    part, rows = read_half(*plan_in, core, True, mine_ref)
    copies += expand_inner(part, rows, grad_in_hbm, *scratch[5:])
    for copy in copies:
        copy.wait()


def third_last_kernel(
    plan_in,
    where_ref,
    mine_ref,
    theirs_ref,
    begun_hbm,
    grad_hbm,
    bias_in_hbm,
    bias_out_hbm,
    gain_hbm,
    shift_hbm,
    bias_in_ref,
    bias_out_ref,
    gain_ref,
    shift_ref,
    small_sems,
    *scratch,
):
    core = where_ref[1]
    part, rows = read_half(*plan_in, core, False, theirs_ref)
    _, mine = read_half(*plan_in, core, True, mine_ref)

    def mean(side):
        both = rows(side, 976, 48).astype(f32) + mine(side, 976, 48).astype(f32)
        v = jnp.sum((both / copy_scale()).reshape(12, 4, LANES), axis=0) * (1.0 / 24.0)
        return (v + pltpu.roll(v, D, 1)) * 0.5

    spare, other = mean(0), mean(1)
    bias_in_ref[...] = jnp.concatenate([spare[0:1, 0:32], other[0:1, 0:32]], axis=1)
    bias_out_ref[...] = spare[1:2, 0:64]
    gain_ref[...] = spare[2:3, 0:64]
    shift_ref[...] = spare[3:4, 0:64]
    small = []
    for index, (source, target) in enumerate(
        (
            (bias_in_ref, bias_in_hbm),
            (bias_out_ref, bias_out_hbm),
            (gain_ref, gain_hbm),
            (shift_ref, shift_hbm),
        )
    ):
        copy = pltpu.make_async_copy(source, target, small_sems.at[index])
        copy.start()
        small.append(copy)
    copies = expand_inner(part, rows, grad_hbm, *scratch) + small
    for copy in copies:
        copy.wait()


def on_device(
    series,
    amplitudes,
    periods,
    conv_in,
    bias_in,
    conv_out,
    bias_out,
    norm_gain,
    norm_bias,
    cotangent,
):
    items = lax.axis_size("items")
    bits = items.bit_length() - 1
    me = lax.axis_index("items")
    side = lax.axis_index("narrow")
    core = me % 2
    where = jnp.stack([side, core]).astype(jnp.int32)
    vmem = pl.BlockSpec(memory_space=pltpu.VMEM)
    smem = pl.BlockSpec(memory_space=pltpu.SMEM)
    hbm = pl.BlockSpec(memory_space=pltpu.HBM)
    shape = jax.ShapeDtypeStruct

    def limit(mib):
        return pltpu.CompilerParams(vmem_limit_bytes=mib * 1024 * 1024)

    def cost(flops):
        return pl.CostEstimate(flops=flops, bytes_accessed=4 << 20, transcendentals=0)

    def stay(arrays):
        return [pltpu.with_memory_space_constraint(a, pltpu.VMEM) for a in arrays]

    def far(arrays):
        return [pltpu.with_memory_space_constraint(a, pltpu.HBM) for a in arrays]

    def two(rows, lanes, kind=f32, lead=None):
        dims = (rows, lanes) if lead is None else (lead, rows, lanes)
        return [pltpu.VMEM(dims, kind)] * 2

    margin = NEAR + GRID + 336
    halved = list(range(1, bits - 1))
    blocks = 2 ** len(halved)
    half_out = -(-1056 // (16 * blocks)) * 16 * blocks
    send, total, part, w1, w2, xs, ua, slope = pl.pallas_call(
        forward_kernel,
        out_shape=(
            pltpu.VMEM((FOLD + 112, LANES), bf16),
            pltpu.VMEM((FOLD, LANES), f32),
            pltpu.VMEM((K, FOLD, LANES), f32),
            pltpu.HBM((WIDE, FULL), bf16),
            pltpu.HBM((FULL, WIDE), bf16),
            pltpu.VMEM((512, LANES), f32),
            pltpu.VMEM((K, GRID, WIDE), bf16),
            pltpu.VMEM((K, QUART, LANES), f32),
        ),
        in_specs=[smem] + [hbm] * 8,
        out_specs=[vmem, vmem, vmem, hbm, hbm, vmem, vmem, vmem],
        scratch_shapes=[
            pltpu.VMEM((WIDE + LANES, FULL), bf16),
            pltpu.VMEM((FULL, WIDE + LANES), bf16),
            pltpu.VMEM((FULL, 2 * LANES), bf16),
            pltpu.VMEM((K, GRID, FULL), bf16),
            pltpu.SMEM((1, K), jnp.int32),
            pltpu.VMEM((1, K), f32),
            pltpu.VMEM((1, STEPS * D), bf16),
            pltpu.VMEM((1, HALF * D), bf16),
            pltpu.VMEM((32, TAPS * D), bf16),
            pltpu.VMEM((64, TAPS * D), bf16),
            pltpu.VMEM((1, FF), f32),
            pltpu.VMEM((1, D), f32),
            pltpu.VMEM((6, GRID, LANES), bf16),
            pltpu.VMEM((FULL, FULL), bf16),
            *two(512, LANES),
            *two(margin, LANES, f32, 3),
            pltpu.VMEM((3, margin, LANES), f32),
            *two(margin, LANES, f32, 6),
            *two(GRID + 3 * PMAX, LANES),
            *two(GRID + PMAX, LANES),
            *two(2 * QUART, LANES),
            pltpu.SemaphoreType.DMA((12,)),
            pltpu.SemaphoreType.DMA((2,)),
        ],
        compiler_params=limit(28),
        cost_estimate=cost(1 << 33),
        name="forward",
    )(
        where,
        *far(
            [
                periods,
                amplitudes,
                series,
                cotangent,
                conv_in.T,
                conv_out.T,
                bias_in[None, :],
                bias_out[None, :],
            ]
        ),
    )

    def exchange(value, partner):
        pairs = []
        for item in range(items):
            for col in range(2):
                to_item, to_col = partner(item, col)
                pairs.append((item * 2 + col, to_item * 2 + to_col))
        return lax.ppermute(value, ("items", "narrow"), pairs)

    across = lambda item, col: (item, 1 - col)
    chip = lambda item, col: (item ^ 1, col)
    recv = exchange(send, across)

    out, keep_out, give_out, grad, merged, dots, small, w1 = pl.pallas_call(
        outer_kernel,
        out_shape=(
            shape((1, HALF * D), bf16),
            pltpu.VMEM((half_out, LANES), bf16),
            pltpu.VMEM((half_out, LANES), bf16),
            pltpu.VMEM((K, QUART, LANES), f32),
            pltpu.VMEM((PAIR, LANES), f32),
            pltpu.VMEM((8, LANES), f32),
            pltpu.VMEM((8, LANES), f32),
            pltpu.VMEM((WIDE, FULL), bf16),
        ),
        in_specs=[smem, smem] + [vmem] * 6 + [hbm] * 2 + [vmem] * 4,
        out_specs=[hbm] + [vmem] * 7,
        scratch_shapes=[
            pltpu.VMEM((PAIR, LANES), f32),
            pltpu.VMEM((PAIR, LANES), f32),
            pltpu.VMEM((PAIR, LANES), f32),
            pltpu.VMEM((PMAX + GRID, LANES), f32),
            pltpu.VMEM((FOLD, LANES), f32),
            *two(NEAR + GRID + NEAR, LANES),
            *two(GRID, FULL, bf16),
            *two(GRID + 32, LANES, f32, 3),
            *two(GRID + 16, LANES),
            *two(2 * QUART, LANES),
            pltpu.VMEM((WIDE, FULL), f32),
            pltpu.VMEM((2 * half_out, LANES), bf16),
            pltpu.VMEM((FULL, WIDE), bf16),
            pltpu.VMEM((1, HALF * D), bf16),
            pltpu.SemaphoreType.DMA((2,)),
            pltpu.SemaphoreType.DMA,
        ],
        compiler_params=limit(16),
        cost_estimate=cost(1 << 33),
        name="outer",
    )(
        where,
        periods,
        amplitudes,
        cotangent,
        *stay([recv, total, xs, part]),
        *far([w1, w2]),
        *stay([ua, slope]),
        norm_gain[None, :],
        norm_bias[None, :],
    )

    keep_in, give_in = pl.pallas_call(
        inner_kernel,
        out_shape=(
            pltpu.VMEM((HALF_IN, LANES), bf16),
            pltpu.VMEM((HALF_IN, LANES), bf16),
        ),
        in_specs=[smem, smem] + [vmem] * 3,
        out_specs=[vmem] * 2,
        scratch_shapes=[
            *two(3 * PMAX + GRID + NEAR, LANES),
            pltpu.VMEM((6, GRID, LANES), bf16),
            *two(GRID, WIDE, bf16),
            *two(GRID, FULL, bf16),
            pltpu.VMEM((WIDE, FULL), f32),
            pltpu.VMEM((2 * HALF_IN, LANES), bf16),
        ],
        compiler_params=limit(16),
        cost_estimate=cost(1 << 33),
        name="inner",
    )(where, periods, *stay([grad, small, xs]))

    by_rows = [
        *two(3 * PMAX + GRID + NEAR, LANES),
        *two(GRID, WIDE, bf16),
        *two(GRID + 32, LANES, f32, 6),
    ]

    def series_begin(grad, w1):
        return pl.pallas_call(
            series_kernel,
            out_shape=pltpu.VMEM((GRID, LANES), f32),
            in_specs=[smem] + [vmem] * 2,
            out_specs=vmem,
            scratch_shapes=by_rows,
            compiler_params=limit(16),
            cost_estimate=cost(1 << 31),
            name="series",
        )(periods, *stay([grad, w1]))

    def series_rest(grad, w1, begun):
        return pl.pallas_call(
            series_rest_kernel,
            out_shape=(
                pltpu.VMEM((HALF // 2, LANES), f32),
                pltpu.VMEM((128, LANES), bf16),
                pltpu.VMEM((8, LANES), f32),
            ),
            in_specs=[smem, smem] + [vmem] * 5,
            out_specs=[vmem] * 3,
            scratch_shapes=[
                *by_rows,
                pltpu.VMEM((GRID, LANES), f32),
                pltpu.VMEM((PAIR, LANES), f32),
                pltpu.VMEM((PAIR, LANES), f32),
            ],
            compiler_params=limit(16),
            cost_estimate=cost(1 << 31),
            name="series_rest",
        )(where, periods, *stay([grad, merged, dots, w1, begun]))

    def partner_of(stage):
        def partner(item, col):
            axis = stage[item % 2]
            if axis is None:
                return (item, 1 - col)
            return (item ^ (1 << axis), col)

        return partner

    def bit_of(stage):
        values = [side if axis is None else (me >> axis) & 1 for axis in stage]
        return jnp.where(core == 0, values[0], values[1])

    def merge(bit, a, b):
        return jnp.concatenate([jnp.where(bit == 0, a, b), jnp.where(bit == 0, b, a)], axis=0)

    orders = (halved, halved[1::-1] + halved[2:])
    sequences = ([None] + halved[::-1], halved[::-1] + [None])

    def start_chain(keep, give):
        return keep.astype(f32) + exchange(give, chip).astype(f32)

    def halve(acc, position):
        stage = (orders[0][position], orders[1][position])
        bit = bit_of(stage)
        size = acc.shape[0] // 2
        gone = lax.dynamic_slice_in_dim(acc, (1 - bit) * size, size, 0).astype(bf16)
        kept = lax.dynamic_slice_in_dim(acc, bit * size, size, 0)
        return kept, gone, stage

    def sum_last(acc):
        mine = acc.astype(bf16)
        if bits > 1:
            theirs = exchange(mine, partner_of((bits - 1, bits - 1)))
            mine = (mine.astype(f32) + theirs.astype(f32)).astype(bf16)
        return mine

    def gather(mine, extra=None):
        came = []
        for position in range(len(sequences[0])):
            stage = (sequences[0][position], sequences[1][position])
            if extra is not None and None in stage:
                both = exchange(jnp.concatenate([mine, extra], axis=0), partner_of(stage))
                theirs = both[: mine.shape[0]]
                came.append(both[mine.shape[0] :])
            else:
                theirs = exchange(mine, partner_of(stage))
            mine = merge(bit_of(stage), mine, theirs)
        received = None if extra is None else jnp.where(core == 0, came[0], came[-1])
        return mine, exchange(mine, chip), received

    acc_out = start_chain(keep_out, give_out)
    acc_in = start_chain(keep_in, give_in)
    begun = None
    for position in range(len(halved)):
        kept_out, gone_out, stage = halve(acc_out, position)
        acc_out = kept_out + exchange(gone_out, partner_of(stage)).astype(f32)
        kept_in, gone_in, stage = halve(acc_in, position)
        if position < 2:
            gone_in, grad = lax.optimization_barrier((gone_in, grad))
        came_in = exchange(gone_in, partner_of(stage))
        if position == 0:
            begun = series_begin(grad, w1)
        if position == 1:
            own, other, table = series_rest(grad, w1, begun)
        acc_in = kept_in + came_in.astype(f32)
    if len(halved) < 1:
        begun = series_begin(grad, w1)
    if len(halved) < 2:
        own, other, table = series_rest(grad, w1, begun)
    mine_out, theirs_out, _ = gather(sum_last(acc_out))
    mine_in, theirs_in, received = gather(sum_last(acc_in), other)

    places = []
    for half in range(2):
        by_side = []
        for narrow in range(2):
            listed = []
            for index in range(blocks):
                value = {None: narrow}
                for position, axis in enumerate(orders[half]):
                    value[axis] = (index >> (len(halved) - 1 - position)) & 1
                place = 0
                for position, axis in enumerate(sequences[half]):
                    place += value[axis] << position
                listed.append(place)
            by_side.append(tuple(listed))
        places.append(tuple(by_side))
    places = tuple(places)

    plan_out = (places, half_out // blocks)
    plan_in = (places, HALF_IN // blocks)
    expanding = [
        pltpu.VMEM((352, FULL), bf16),
        pltpu.VMEM((6, 352, LANES), f32),
        pltpu.VMEM((6, 352, LANES), f32),
        pltpu.VMEM((32, TAPS * D), f32),
        pltpu.SemaphoreType.DMA((22,)),
    ]
    grad_out = pl.pallas_call(
        functools.partial(first_last_kernel, plan_out),
        out_shape=shape((D, TAPS * FF), f32),
        in_specs=[smem, vmem],
        out_specs=hbm,
        scratch_shapes=expanding,
        compiler_params=limit(16),
        cost_estimate=cost(1 << 31),
        name="first_last",
    )(where, mine_out)
    grad_out, grad_in, g_series, g_amps = pl.pallas_call(
        functools.partial(second_last_kernel, plan_out, plan_in),
        out_shape=(
            shape((D, TAPS * FF), f32),
            shape((FF, TAPS * D), f32),
            shape((1, HALF * D), f32),
            shape((1, K), f32),
        ),
        in_specs=[smem] + [vmem] * 6 + [hbm],
        out_specs=[hbm] * 4,
        input_output_aliases={7: 0},
        scratch_shapes=[
            pltpu.VMEM((1, HALF * D), f32),
            pltpu.VMEM((1, K), f32),
            pltpu.SemaphoreType.DMA((2,)),
            *expanding,
            *expanding,
        ],
        compiler_params=limit(24),
        cost_estimate=cost(1 << 32),
        name="second_last",
    )(where, amplitudes, theirs_out, mine_in, own, received, table, grad_out)
    grad_in, g_bias_in, g_bias_out, g_gain, g_shift = pl.pallas_call(
        functools.partial(third_last_kernel, plan_in),
        out_shape=(
            shape((FF, TAPS * D), f32),
            shape((1, FF), f32),
            shape((1, D), f32),
            shape((1, D), f32),
            shape((1, D), f32),
        ),
        in_specs=[smem, vmem, vmem, hbm],
        out_specs=[hbm] * 5,
        input_output_aliases={3: 0},
        scratch_shapes=[pltpu.VMEM((1, D), f32)] * 4 + [pltpu.SemaphoreType.DMA((4,))] + expanding,
        compiler_params=limit(16),
        cost_estimate=cost(1 << 31),
        name="third_last",
    )(where, mine_in, theirs_in, grad_in)
    return (
        out,
        g_series,
        g_amps,
        grad_in.T,
        g_bias_in[0],
        grad_out.T,
        g_bias_out[0],
        g_gain[0],
        g_shift[0],
    )


def solution(mesh):
    in_specs = (
        P("items", None),
        P("items", None),
        P("items", None),
        P(),
        P(),
        P(),
        P(),
        P(),
        P(),
        P("items", "narrow"),
    )
    out_specs = (
        P("items", "narrow"),
        P("items", "narrow"),
        P("items", None),
        P(),
        P(),
        P(),
        P(),
        P(),
        P(),
    )
    return jax.shard_map(
        on_device, mesh=mesh, in_specs=in_specs, out_specs=out_specs, check_vma=False
    )
```

```python
import functools
import math

import jax
import jax.numpy as jnp
from jax import lax
from jax.experimental import pallas as pl
from jax.experimental.pallas import tpu as pltpu
from jax.sharding import PartitionSpec as P

D = 64
FF = 64
K = 5
TAPS = 286
STEPS = 432
PMAX = 48
GRID = 480
HALF = STEPS // 2
LANES = 128
kernel_sizes = (1, 3, 5, 7, 9, 11)
epsilon = 1e-05
f32 = jnp.float32
bf16 = jnp.bfloat16

PAIR = 448
FOLD = PAIR // 2
QUART = GRID // 4
NEAR = 5 * PMAX
WIDE = 12 * 32
FULL = 12 * D
HALF_IN = 1024
STEP = 48


def tap_index(size, row, col):
    radius = (size - 1) // 2
    first = sum(k * k for k in kernel_sizes if k < size)
    return first + (row + radius) * size + col + radius


def tap_place(tap):
    for size in kernel_sizes:
        inside = tap - tap_index(size, -(size // 2), -(size // 2))
        if 0 <= inside < size * size:
            return inside // size - size // 2 + 5, inside % size - size // 2 + 5
    return None


def lane_of(rows):
    return lax.broadcasted_iota(jnp.int32, (rows, LANES), 1)


def row_of(rows):
    return lax.broadcasted_iota(jnp.int32, (rows, LANES), 0)


def low_half(rows):
    return lane_of(rows) < D


def span(plane):
    return slice(plane * LANES, (plane + 1) * LANES)


def four_quarters(v):
    v = v + pltpu.roll(v, 64, 1)
    return v + pltpu.roll(v, 32, 1)


def quarter_select(parts, rows):
    lane = lane_of(rows)
    upper = jnp.where(lane < 96, parts[2], parts[3])
    lower = jnp.where(lane < 32, parts[0], parts[1])
    return jnp.where(lane < 64, lower, upper)


def pack_pieces(load, store, temp):
    rows = 24
    pieces = []
    for r in range(0, 2 * QUART, rows):

        def piece(r=r):
            low = low_half(rows)
            a, b = load(r, rows), load(2 * QUART + r, rows)
            temp[r : r + rows, :] = jnp.where(low, a, b) + pltpu.roll(jnp.where(low, b, a), 64, 1)

        pieces.append(piece)
    for r in range(0, QUART, rows):

        def piece(r=r):
            even = lane_of(rows) // 32 % 2 == 0
            a, b = temp[r : r + rows, :], temp[QUART + r : QUART + r + rows, :]
            other = jnp.where(even, pltpu.roll(a, 96, 1), pltpu.roll(b, 32, 1))
            store(r, rows, jnp.where(even, a, b) + other)

        pieces.append(piece)
    return pieces


def spread_pieces(read, target, start):
    rows = 40
    pieces = []
    for r in range(0, QUART, rows):

        def piece(r=r):
            packed = read(r, rows)
            turned = [packed if s == 0 else pltpu.roll(packed, 32 * s, 1) for s in range(4)]
            for q in range(4):
                lanes = slice(32 * q, 32 * q + 32)
                for block in range(4):
                    target[pl.ds(start(q) + block * QUART + r, rows), lanes] = turned[
                        (q - block) % 4
                    ][:, lanes]

        pieces.append(piece)
    return pieces


def rounded(v):
    return v.astype(bf16).astype(f32)


def spread_pairs(pairs, ref, start):
    rows = pairs.shape[0]
    other = pltpu.roll(pairs, D, 1)
    low = low_half(rows)
    ref[pl.ds(start, rows, stride=2), :] = jnp.where(low, pairs, other)
    ref[pl.ds(start + 1, rows, stride=2), :] = jnp.where(low, other, pairs)


def flat_pairs(ref, rows):
    return ref[...].astype(f32).reshape(rows, LANES)


def gather_pairs(ref, start, rows):
    return jnp.where(
        low_half(rows),
        ref[pl.ds(start, rows, stride=2), :],
        ref[pl.ds(start + 1, rows, stride=2), :],
    )


def combine_tile(load, rows, row, plane):
    low = low_half(rows)
    col0, col1 = 2 * plane - 5, 2 * plane - 4
    even = odd = None
    for size in kernel_sizes:
        radius = (size - 1) // 2
        in0, in1 = abs(col0) <= radius, abs(col1) <= radius
        if abs(row) > radius or not (in0 or in1):
            continue
        first = tap_index(size, row, col0)
        if first % 2 == 0:
            v = load(first // 2)
            if not in0:
                v = jnp.where(low, 0.0, v)
            if not in1:
                v = jnp.where(low, v, 0.0)
            even = v if even is None else even + v
        else:
            left = load(first // 2) if in0 else 0.0
            right = load(first // 2 + 1) if in1 else 0.0
            v = jnp.where(low, right, left)
            odd = v if odd is None else odd + v
    if odd is not None:
        odd = pltpu.roll(odd, D, 1)
        even = odd if even is None else even + odd
    return even


def widths(period):
    width = jnp.full((8, LANES), period, jnp.int32).astype(f32)
    return width, 1.0 / width


def column_of(width, inverse, rows, ahead, start):
    position = (row_of(rows) + ahead + start).astype(f32)
    many = jnp.broadcast_to(width[0:1, :], (rows, LANES))
    turns = jnp.floor((position + 0.5) * jnp.broadcast_to(inverse[0:1, :], (rows, LANES)))
    return position - turns * many


def mixing_of(amp):
    shifted = jnp.exp(amp - jnp.max(amp, axis=-1, keepdims=True))
    return shifted / jnp.sum(shifted, axis=-1, keepdims=True)


def gelu_both(v):
    cdf = 0.5 * (1.0 + lax.erf(v * (1.0 / math.sqrt(2.0))))
    density = jnp.exp(-0.5 * v * v) * (1.0 / math.sqrt(2.0 * math.pi))
    return v * cdf, cdf + v * density


def contract(a, b, dim_a, dim_b):
    return lax.dot_general(
        a, b, (((dim_a,), (dim_b,)), ((), ())), preferred_element_type=f32
    )


def together(*streams):
    lists = [list(stream) for stream in streams]
    marks = []
    for number, pieces in enumerate(lists):
        for index, piece in enumerate(pieces):
            marks.append(((index + 0.5) / len(pieces), number, piece))
    for _, _, piece in sorted(marks, key=lambda mark: mark[:2]):
        piece()


def unfold_columns(period, shifted, target):
    pieces = []
    for t in range(0, GRID, STEP):

        def piece(t=t):
            width, inverse = widths(period)
            many = jnp.broadcast_to(width[0:1, :], (STEP, LANES)).astype(bf16)
            zero = jnp.zeros((STEP, LANES), bf16)
            col = column_of(width, inverse, STEP, 0, t)
            col = (col + jnp.where(low_half(STEP), 0.0, 1.0)).astype(bf16)
            for plane in range(6):
                shift = 2 * plane - 5
                inside = (col >= jnp.asarray(-shift, bf16)) & (col < many - jnp.asarray(shift, bf16))
                target[t : t + STEP, span(plane)] = jnp.where(
                    inside, shifted[plane, t : t + STEP, :], zero
                )

        pieces.append(piece)
    return pieces


def shift_columns(xs, shifted):
    for t in range(0, GRID, STEP):
        low = low_half(STEP)
        for plane in range(6):
            at = 16 + t + 2 * plane - 5
            shifted[plane, t : t + STEP, :] = jnp.where(
                low, xs[pl.ds(at, STEP), :], xs[pl.ds(at + 1, STEP), :]
            ).astype(bf16)


def product_pieces(read, read_weight, target, start, planes, dims):
    pieces = []
    for plane in range(0, planes, 2):

        def piece(plane=plane):
            count = min(2, planes - plane)
            lanes = slice(plane * LANES, (plane + count) * LANES)
            product = contract(read(), read_weight(lanes), *dims)
            for index in range(count):
                target[plane + index, start : start + GRID, :] = product[:, span(index)]

        pieces.append(piece)
    return pieces


def weight_pieces(read, read_other, total, first):
    def piece():
        value = contract(read(), read_other(), 0, 0)
        if first:
            total[...] = value
        else:
            total[...] += value

    return [piece]


def forward_kernel(
    where_ref,
    periods_hbm,
    amp_hbm,
    x_hbm,
    cot_hbm,
    conv_in_hbm,
    conv_out_hbm,
    bias_in_hbm,
    bias_out_hbm,
    send_ref,
    total,
    part_ref,
    w1_hbm,
    w2_ref,
    item_ref,
    ua_ref,
    slope_ref,
    w1_wide,
    w2_wide,
    r2,
    ux_ref,
    periods_ref,
    amp_ref,
    x_ref,
    cot_ref,
    conv_in_ref,
    conv_out_ref,
    bias_in_ref,
    bias_out_ref,
    xs,
    xb,
    c2,
    act0,
    act1,
    ys0,
    ys1,
    ys2,
    zs0,
    zs1,
    ss0,
    ss1,
    st0,
    st1,
    tp0,
    tp1,
    slopes,
    sems,
    sent,
):
    side = where_ref[0]
    half = pl.multiple_of(side * 32, 32)
    sources = [
        (x_hbm, x_ref),
        (periods_hbm, periods_ref),
        (amp_hbm, amp_ref),
        (bias_in_hbm, bias_in_ref),
        (bias_out_hbm, bias_out_ref),
        (cot_hbm, cot_ref),
    ]
    for piece in range(2):
        rows = pl.ds(pl.multiple_of(half + 16 * piece, 16), 16)
        sources.append((conv_in_hbm.at[rows, :], conv_in_ref.at[pl.ds(16 * piece, 16), :]))
    for piece in range(4):
        rows = pl.ds(16 * piece, 16)
        sources.append((conv_out_hbm.at[rows, :], conv_out_ref.at[rows, :]))
    copies = [pltpu.make_async_copy(a, b, sems.at[i]) for i, (a, b) in enumerate(sources)]
    for copy in copies:
        copy.start()
    xs[...] = jnp.zeros_like(xs)
    slopes[QUART:, :] = jnp.zeros((128 - QUART, LANES), f32)
    for ref in (act0, act1):
        ref[...] = jnp.zeros_like(ref)
    for refs, per_plane, ahead in (((ys0, ys1, ys2), 4, 3 * PMAX), ((zs0, zs1), 2, PMAX)):
        for plane in range(12 // per_plane):
            moved = per_plane * plane - 5
            top = -moved * PMAX if moved < 0 else 0
            bottom = ahead + (2 * moved if moved < 0 else moved * PMAX)
            for ref in refs:
                if top:
                    ref[plane, NEAR - top : NEAR, :] = jnp.zeros((top, LANES), f32)
                ref[plane, NEAR + GRID : NEAR + GRID + bottom, :] = jnp.zeros((bottom, LANES), f32)
    source = lax.broadcasted_iota(jnp.int32, (2 * LANES, LANES), 0)
    target = lax.broadcasted_iota(jnp.int32, (2 * LANES, LANES), 1)
    wanted = (target // 32) * 64 + side * 32 + target % 32
    choose = (source == wanted).astype(f32).astype(bf16)
    w1_wide[352:384, :] = jnp.zeros((32, FULL), bf16)
    c2[704:768, :] = jnp.zeros((64, FULL), bf16)
    r2[704:768, :] = jnp.zeros((64, 2 * LANES), bf16)

    copies[0].wait()
    spread_pairs(flat_pairs(x_ref, HALF), xs, 16)
    shift_columns(xs, xb)
    for copy in copies[1:6]:
        copy.wait()
    bias_in = jnp.concatenate([bias_in_ref[...], bias_in_ref[...]], axis=1)
    bias_in = jnp.where(side == 0, bias_in, pltpu.roll(bias_in, 96, 1))
    bias_in = four_quarters(jnp.where(lane_of(1) < 32, bias_in, 0.0))
    bias_out = jnp.concatenate([bias_out_ref[...], bias_out_ref[...]], axis=1)
    bias_out = jnp.where(side == 0, bias_out, 0.0)
    mixing = mixing_of(amp_ref[...])
    leaving = []

    def leave(ref, target):
        copy = pltpu.make_async_copy(ref, target, sent.at[len(leaving)])
        copy.start()
        leaving.append(copy)

    def unfold(k):
        return unfold_columns(periods_ref[0, k], xb, ux_ref.at[k])

    def first_product(k):
        target = (ys0, ys1, ys2)[k % 3]

        def piece():
            product = contract(ux_ref[k], w1_wide[...], 1, 1)
            for plane in range(3):
                value = product[:, span(plane)]
                if plane == 1:
                    value = value + product[:, span(3)]
                target[plane, NEAR : NEAR + GRID, :] = value

        return [piece]

    def second_product(k):
        target = (zs0, zs1)[k % 2]
        pieces = []
        for plane in range(0, 6, 2):

            def piece(plane=plane):
                lanes = slice(plane * LANES, (plane + 2) * LANES)
                value = ua_ref[k]
                value = jnp.concatenate([value, value[:, span(1)]], axis=1)
                product = contract(value, w2_wide[lanes, :], 1, 1)
                for index in range(2):
                    target[plane + index, NEAR : NEAR + GRID, :] = product[:, span(index)]

            pieces.append(piece)
        return pieces

    def activate(k):
        ys, ss, act, temp = (ys0, ys1, ys2)[k % 3], (ss0, ss1)[k % 2], (act0, act1)[k % 2], (tp0, tp1)[k % 2]
        period = periods_ref[0, k]
        used = lax.div(STEPS + period - 1, period) * period
        pieces = []
        for t in range(0, GRID + 3 * PMAX, STEP):

            def piece(t=t):
                value = ys[0, pl.ds(NEAR + t - 5 * period, STEP), :]
                for plane in range(1, 3):
                    value = value + ys[plane, pl.ds(NEAR + t + (4 * plane - 5) * period, STEP), :]
                ss[t : t + STEP, :] = value

            pieces.append(piece)

        def load(r, rows):
            return quarter_select([ss[pl.ds(r + q * period, rows), :] for q in range(4)], rows)

        def store(r, rows, value):
            hidden = value * (1.0 / 6.0) + bias_in
            active, slope = gelu_both(hidden)
            position = row_of(rows) + r + QUART * (lane_of(rows) // 32)
            slopes[r : r + rows, :] = jnp.where(position < used, slope, 0.0)
            temp[r : r + rows, :] = jnp.where(position < used, active, 0.0)

        def keep_slope():
            slope_ref[k] = slopes[...].astype(bf16)

        pieces += pack_pieces(load, store, temp)
        pieces.append(keep_slope)
        pieces += spread_pieces(lambda r, rows: temp[r : r + rows, :], act, lambda q: 16 - q)
        for t in range(0, GRID, STEP):

            def piece(t=t):
                width, inverse = widths(period)
                many = jnp.broadcast_to(width[0:1, :], (STEP, LANES)).astype(bf16)
                zero = jnp.zeros((STEP, LANES), bf16)
                col = column_of(width, inverse, STEP, 0, t) + (lane_of(STEP) // 32).astype(f32)
                col = col.astype(bf16)
                for plane in range(3):
                    shift = 4 * plane - 5
                    inside = (col >= jnp.asarray(-shift, bf16)) & (
                        col < many - jnp.asarray(shift, bf16)
                    )
                    moved = act[pl.ds(16 + t + shift, STEP), :].astype(bf16)
                    ua_ref[k, t : t + STEP, span(plane)] = jnp.where(inside, moved, zero)

            pieces.append(piece)
        return pieces

    def finish(k):
        zs, ss = (zs0, zs1)[k % 2], (st0, st1)[k % 2]
        period = periods_ref[0, k]
        weight = mixing[:, k : k + 1]
        pieces = []
        for t in range(0, GRID + PMAX, STEP):

            def piece(t=t):
                value = zs[0, pl.ds(NEAR + t - 5 * period, STEP), :]
                for plane in range(1, 6):
                    value = value + zs[plane, pl.ds(NEAR + t + (2 * plane - 5) * period, STEP), :]
                ss[t : t + STEP, :] = value

            pieces.append(piece)
        rows = 32
        for r in range(0, FOLD, rows):

            def piece(r=r):
                low = low_half(rows)
                near = jnp.where(low, ss[pl.ds(r, rows), :], ss[pl.ds(FOLD + r + period, rows), :])
                far = jnp.where(low, ss[pl.ds(FOLD + r, rows), :], ss[pl.ds(r + period, rows), :])
                out = (near + pltpu.roll(far, D, 1)) * (1.0 / 6.0) + bias_out
                part_ref[k, r : r + rows, :] = out
                if k == 0:
                    total[r : r + rows, :] = weight * out
                else:
                    total[r : r + rows, :] += weight * out

            pieces.append(piece)
        return pieces

    def combine_in():
        pieces = []
        for row in range(-5, 6):

            def piece(row=row):
                at = (row + 5) * 32
                for plane in range(6):
                    v = combine_tile(lambda tile: conv_in_ref[:, span(tile)].astype(f32), 32, row, plane)
                    w1_wide[at : at + 32, span(plane)] = v.astype(bf16)
                    if -1 <= row <= 2:
                        w1_wide[WIDE + at - 128 : WIDE + at - 96, span(plane)] = (v - rounded(v)).astype(bf16)

            pieces.append(piece)
        return pieces

    def combine_out():
        pieces = []
        for row in range(-5, 6):

            def piece(row=row):
                at = (row + 5) * 64
                for plane in range(6):
                    v = combine_tile(lambda tile: conv_out_ref[:, span(tile)].astype(f32), 64, row, plane)
                    c2[at : at + 64, span(plane)] = v.astype(bf16)
                    if plane // 2 == 1:
                        r2[at : at + 64, span(plane % 2)] = (v - rounded(v)).astype(bf16)

            pieces.append(piece)
        return pieces

    def choose_half():
        pieces = []
        for plane in range(3):

            def piece(plane=plane):
                lanes = slice(2 * plane * LANES, 2 * (plane + 1) * LANES)
                w2_wide[:, span(plane)] = jnp.dot(
                    c2[:, lanes], choose, preferred_element_type=f32
                ).astype(bf16)

            pieces.append(piece)

        def piece():
            w2_wide[:, span(3)] = jnp.dot(r2[...], choose, preferred_element_type=f32).astype(bf16)

        return pieces + [piece]

    together(unfold(0))
    together(unfold(1))
    for copy in copies[6:]:
        copy.wait()
    together(combine_in())
    leave(w1_wide.at[pl.ds(0, WIDE), :], w1_hbm)
    combining = combine_out()
    together(first_product(0), combining[:6])
    together(first_product(1), combining[6:], unfold(2))
    together(choose_half(), activate(0))
    w2_ref[...] = w2_wide[:, 0:WIDE]
    together(first_product(2), activate(1), unfold(3))
    together(second_product(0), activate(2))
    together(first_product(3), finish(0), unfold(4))
    together(second_product(1), activate(3))
    together(first_product(4), finish(1))
    together(second_product(2), activate(4))
    together(second_product(3), finish(2))
    together(second_product(4), finish(3))
    together(finish(4))

    send_ref[0:FOLD, :] = total[...].astype(bf16)
    item_ref[...] = xs[16 : 16 + PAIR, :].astype(bf16)
    send_ref[FOLD:, :] = jnp.concatenate(
        [flat_pairs(cot_ref, HALF // 2), jnp.zeros((4, LANES), f32)], axis=0
    ).astype(bf16)
    for copy in leaving:
        copy.wait()


def outer_kernel(
    where_ref,
    periods_ref,
    amp_ref,
    cot_ref,
    recv_ref,
    own_ref,
    item_ref,
    part_ref,
    w1_hbm,
    w2_ref,
    ua_ref,
    slope_ref,
    gain_ref,
    shift_ref,
    out_hbm,
    keep_ref,
    send_ref,
    grad_ref,
    merged_ref,
    dots_ref,
    small,
    w1_ref,
    other,
    cot,
    outs,
    gm,
    gmp,
    rw0,
    rw1,
    gb0,
    gb1,
    zs0,
    zs1,
    vs0,
    vs1,
    tp0,
    tp1,
    dw,
    packed,
    slopes,
    item,
    out_ref,
    sem,
    out_sem,
):
    coming = pltpu.make_async_copy(w1_hbm, w1_ref, sem)
    coming.start()
    slopes[...] = slope_ref[...].astype(f32)
    item[...] = item_ref[...].astype(f32)
    side = where_ref[0]
    core = where_ref[1]
    mixing = mixing_of(amp_ref[...])
    small[...] = jnp.zeros_like(small)
    for ref in (rw0, rw1):
        ref[0:NEAR, :] = jnp.zeros((NEAR, LANES), f32)
        ref[NEAR + GRID :, :] = jnp.zeros((NEAR, LANES), f32)
    for ref in (zs0, zs1):
        ref[:, 0:16, :] = jnp.zeros((3, 16, LANES), f32)
        ref[:, 16 + GRID :, :] = jnp.zeros((3, 16, LANES), f32)
    gm[0:PMAX, :] = jnp.zeros((PMAX, LANES), f32)
    gm[PMAX + PAIR :, :] = jnp.zeros((GRID - PAIR, LANES), f32)

    low = low_half(FOLD)
    v = own_ref[...] + recv_ref[0:FOLD, :].astype(f32)
    turned = pltpu.roll(v, D, 1)
    other[0:FOLD, :] = jnp.where(low, v, turned)
    other[FOLD:, :] = jnp.where(low, turned, v)
    mine = flat_pairs(cot_ref, HALF // 2)
    theirs = recv_ref[FOLD:, :].astype(f32)[: HALF // 2, :]
    cot[STEPS:, :] = jnp.zeros((PAIR - STEPS, LANES), f32)
    spread_pairs(jnp.where(side == 0, mine, theirs), cot, 0)
    spread_pairs(jnp.where(side == 0, theirs, mine), cot, HALF)
    gain = jnp.concatenate([gain_ref[...], gain_ref[...]], axis=1)
    shift = jnp.concatenate([shift_ref[...], shift_ref[...]], axis=1)
    grad_gain = grad_shift = grad_bias = jnp.zeros((8, LANES), f32)

    def eights(v):
        return jnp.sum(v.reshape(-1, 8, LANES), axis=0)

    for t in range(0, PAIR, 56):
        rows = slice(t, t + 56)
        total = item[rows, :] + other[rows, :]
        centred = total - jnp.mean(total, axis=-1, keepdims=True)
        variance = jnp.mean(centred * centred, axis=-1, keepdims=True)
        inverse = lax.rsqrt(variance + epsilon)
        normed = centred * inverse
        outs[rows, :] = normed * gain + shift
        c = cot[rows, :]
        grad_gain = grad_gain + eights(c * normed)
        grad_shift = grad_shift + eights(c)
        e = c * gain
        grad = inverse * (
            e
            - jnp.mean(e, axis=-1, keepdims=True)
            - normed * jnp.mean(e * normed, axis=-1, keepdims=True)
        )
        gm[PMAX + t : PMAX + t + 56, :] = grad
        merged_ref[rows, :] = grad
        grad_bias = grad_bias + eights(grad)
    grad_bias = grad_bias * jnp.sum(mixing, axis=-1, keepdims=True)
    small[1:2, :] = jnp.sum(grad_bias, axis=0, keepdims=True)
    small[2:3, :] = jnp.sum(grad_gain, axis=0, keepdims=True)
    small[3:4, :] = jnp.sum(grad_shift, axis=0, keepdims=True)
    first = pl.multiple_of(side * HALF, 8)
    out_ref[...] = gather_pairs(outs, first, HALF // 2).reshape(1, HALF * D).astype(bf16)
    leaving = pltpu.make_async_copy(out_ref, out_hbm, out_sem)
    leaving.start()
    rows = 32
    for r in range(0, FOLD, rows):
        gmp[r : r + rows, :] = jnp.where(
            low_half(rows),
            gm[PMAX + r : PMAX + r + rows, :],
            gm[PMAX + FOLD + r : PMAX + FOLD + r + rows, :],
        )

    def unfold(k):
        rowed, gab = (rw0, rw1)[k % 2], (gb0, gb1)[k % 2]
        period = periods_ref[0, k]
        weight = mixing[:, k : k + 1]
        pieces = []
        for t in range(0, GRID, STEP):

            def piece(t=t):
                here = gm[PMAX + t : PMAX + t + STEP, :]
                back = gm[pl.ds(PMAX + t - period, STEP), :]
                rowed[NEAR + t : NEAR + t + STEP, :] = weight * jnp.where(low_half(STEP), here, back)

            pieces.append(piece)
        for t in range(0, GRID, STEP):

            def piece(t=t):
                for plane in range(6):
                    gab[t : t + STEP, span(plane)] = rowed[
                        pl.ds(NEAR + t - (2 * plane - 5) * period, STEP), :
                    ].astype(bf16)

            pieces.append(piece)
        return pieces

    def back(k):
        return product_pieces(
            lambda: (gb0, gb1)[k % 2][...], lambda lanes: w2_ref[:, lanes], (zs0, zs1)[k % 2], 16, 3, (1, 0)
        )

    def weigh(k):
        return weight_pieces(lambda: ua_ref[k], lambda: (gb0, gb1)[k % 2][...], dw, k == 0)

    def fold(k):
        zs, vs, temp = (zs0, zs1)[k % 2], (vs0, vs1)[k % 2], (tp0, tp1)[k % 2]
        period = periods_ref[0, k]
        rows = 16
        pieces = []
        for t in range(0, GRID + 16, rows):

            def piece(t=t):
                width, inverse = widths(period)
                many = jnp.broadcast_to(width[0:1, :], (rows, LANES))
                quarter = lane_of(rows) // 32
                place = column_of(width, inverse, rows, quarter, t - 8) - quarter.astype(f32)
                value = None
                for plane in range(3):
                    s = 4 * plane - 5
                    v = zs[plane, pl.ds(16 - 8 + t - s, rows), :]
                    v = jnp.where((place >= s) & (place < many + s), v, 0.0)
                    value = v if value is None else value + v
                vs[t : t + rows, :] = value

            pieces.append(piece)

        def load(r, rows):
            return quarter_select([vs[pl.ds(8 + r - q, rows), :] for q in range(4)], rows)

        def store(r, rows, value):
            grad_ref[k, r : r + rows, :] = value * slopes[k, r : r + rows, :] * (1.0 / 6.0)

        return pieces + pack_pieces(load, store, temp)

    together(unfold(0))
    for k in range(K):
        streams = [back(k)]
        if k + 1 < K:
            streams.append(unfold(k + 1))
        together(*streams)
        together(weigh(k), fold(k))
    coming.wait()
    leaving.wait()
    bias = None
    for k in range(K):
        v = jnp.sum(grad_ref[k], axis=0, keepdims=True)
        bias = v if bias is None else bias + v
        dots_ref[k : k + 1, :] = jnp.sum(gmp[...] * part_ref[k], axis=0, keepdims=True)
    dots_ref[K:, :] = jnp.zeros((8 - K, LANES), f32)
    small[0:1, :] = four_quarters(bias)
    count = keep_ref.shape[0]
    turned = jnp.transpose((dw[...] * (1.0 / 6.0)).astype(bf16))
    for part in range(2):
        for plane in range(3):
            for row in range(11):
                target = part * count + plane * 352 + row * 32
                source = row * 64 + part * 32
                packed[target : target + 32, :] = turned[source : source + 32, span(plane)]
        packed[part * count + 1056 : (part + 1) * count, :] = jnp.zeros((count - 1056, LANES), bf16)
    keep_ref[...] = packed[pl.ds(pl.multiple_of(core * count, 16), count), :]
    send_ref[...] = packed[pl.ds(pl.multiple_of((1 - core) * count, 16), count), :]


def unfold_rows(period, read, rowed, target, clear):
    edge = 3 * PMAX
    pieces = []
    if clear:

        def piece():
            rowed[edge : 2 * edge, :] = jnp.zeros((edge, LANES), f32)
            rowed[edge + GRID : 2 * edge + GRID, :] = jnp.zeros((edge, LANES), f32)

        pieces.append(piece)
    pieces += spread_pieces(read, rowed, lambda q: edge + q * period)
    for t in range(0, GRID, STEP):

        def piece(t=t):
            for plane in range(3):
                target[t : t + STEP, span(plane)] = rowed[
                    pl.ds(edge + t - (4 * plane - 5) * period, STEP), :
                ].astype(bf16)

        pieces.append(piece)
    return pieces


def copy_scale():
    number = row_of(48) // 4 * 2 + lane_of(48) // D
    return jnp.exp(number.astype(f32) * (math.log(2.0) / 24.0))


def inner_kernel(
    where_ref,
    periods_ref,
    grad_ref,
    small_ref,
    item_ref,
    keep_ref,
    send_ref,
    hr0,
    hr1,
    xs,
    xb,
    gh0,
    gh1,
    ux0,
    ux1,
    dw,
    packed,
):
    core = where_ref[1]
    for ref in (hr0, hr1):
        ref[...] = jnp.zeros_like(ref)
    xs[0:16, :] = jnp.zeros((16, LANES), f32)
    xs[16 : 16 + PAIR, :] = item_ref[...].astype(f32)
    xs[16 + PAIR :, :] = jnp.zeros((512 - 16 - PAIR, LANES), f32)
    shift_columns(xs, xb)

    def unfold(k):
        return unfold_rows(
            periods_ref[0, k],
            lambda r, rows: grad_ref[k, r : r + rows, :],
            (hr0, hr1)[k % 2],
            (gh0, gh1)[k % 2],
            k > 1,
        )

    def again(k):
        return unfold_columns(periods_ref[0, k], xb, (ux0, ux1)[k % 2])

    def weigh(k):
        return weight_pieces(lambda: (gh0, gh1)[k % 2][...], lambda: (ux0, ux1)[k % 2][...], dw, k == 0)

    together(unfold(0), again(0))
    for k in range(K):
        streams = [weigh(k)]
        if k + 1 < K:
            streams += [unfold(k + 1), again(k + 1)]
        together(*streams)

    sixth = 1.0 / 6.0
    for part in range(2):
        at = part * HALF_IN
        for row in range(11):
            source = slice(row * 32 + part * 16, row * 32 + part * 16 + 16)
            for plane in range(5):
                target = at + plane * 176 + row * 16
                packed[target : target + 16, :] = (dw[source, span(plane)] * sixth).astype(bf16)
        for row in range(6):
            source = slice(row * 32 + part * 16, row * 32 + part * 16 + 16)
            other = slice((row + 6) * 32 + part * 16, (row + 6) * 32 + part * 16 + 16)
            v = jnp.where(low_half(16), dw[source, span(5)], pltpu.roll(dw[other, span(5)], D, 1))
            packed[at + 880 + row * 16 : at + 896 + row * 16, :] = (v * sixth).astype(bf16)
        packed[at + 976 : at + 1024, :] = (
            jnp.concatenate([small_ref[0:4, :]] * 12, axis=0) * copy_scale()
        ).astype(bf16)
    count = HALF_IN
    keep_ref[...] = packed[pl.ds(pl.multiple_of(core * count, count), count), :]
    send_ref[...] = packed[pl.ds(pl.multiple_of((1 - core) * count, count), count), :]


def series_pieces(branches, periods_ref, grad_ref, w1_ref, vs, begun, rowed, hidden, planes):
    for ref in rowed:
        ref[...] = jnp.zeros_like(ref)
    for ref in planes:
        ref[:, 0:16, :] = jnp.zeros((6, 16, LANES), f32)
        ref[:, 16 + GRID :, :] = jnp.zeros((6, 16, LANES), f32)

    def unfold(index):
        k = branches[index]
        return unfold_rows(
            periods_ref[0, k],
            lambda r, rows: grad_ref[k, r : r + rows, :],
            rowed[index % 2],
            hidden[index % 2],
            index > 1,
        )

    def back(index):
        return product_pieces(
            lambda: hidden[index % 2][...],
            lambda lanes: w1_ref[:, lanes],
            planes[index % 2],
            16,
            6,
            (1, 0),
        )

    def fold(index):
        zs = planes[index % 2]
        period = periods_ref[0, branches[index]]
        rows = 16
        pieces = []
        for t in range(0, PAIR + 16, rows):

            def piece(t=t):
                width, inverse = widths(period)
                many = jnp.broadcast_to(width[0:1, :], (rows, LANES))
                half = lane_of(rows) // D
                place = column_of(width, inverse, rows, half, t - 8) - half.astype(f32)
                value = None if begun is None or index else begun[t : t + rows, :]
                for plane in range(6):
                    s = 2 * plane - 5
                    v = zs[plane, pl.ds(16 - 8 + t - s, rows), :]
                    v = jnp.where((place >= s) & (place < many + s), v, 0.0)
                    value = v if value is None else value + v
                if index == 0:
                    vs[t : t + rows, :] = value
                else:
                    vs[t : t + rows, :] += value

            pieces.append(piece)
        return pieces

    count = len(branches)
    together(unfold(0))
    together(back(0), *([unfold(1)] if count > 1 else []))
    for index in range(count):
        streams = [fold(index)]
        if index + 1 < count:
            streams.append(back(index + 1))
        if index + 2 < count:
            streams.append(unfold(index + 2))
        together(*streams)


def series_kernel(periods_ref, grad_ref, w1_ref, vs, hr0, hr1, gh0, gh1, zs0, zs1):
    series_pieces(
        range(0, 3), periods_ref, grad_ref, w1_ref, vs, None, (hr0, hr1), (gh0, gh1), (zs0, zs1)
    )


def series_rest_kernel(
    where_ref,
    periods_ref,
    grad_ref,
    merged_ref,
    dots_ref,
    w1_ref,
    begun_ref,
    own_ref,
    other_ref,
    table_ref,
    hr0,
    hr1,
    gh0,
    gh1,
    zs0,
    zs1,
    vs,
    dx,
    outs,
):
    side = where_ref[0]
    series_pieces(
        range(3, K), periods_ref, grad_ref, w1_ref, vs, begun_ref, (hr0, hr1), (gh0, gh1), (zs0, zs1)
    )
    rows = 56
    for t in range(0, PAIR, rows):
        v = jnp.where(low_half(rows), vs[pl.ds(8 + t, rows), :], vs[pl.ds(8 + t - 1, rows), :])
        v = (v + pltpu.roll(v, D, 1)) * (1.0 / 6.0)
        dx[t : t + rows, :] = v
        outs[t : t + rows, :] = v + merged_ref[t : t + rows, :]
    own_ref[...] = gather_pairs(outs, pl.multiple_of(side * HALF, 8), HALF // 2)
    other_ref[0:112, :] = gather_pairs(dx, pl.multiple_of((1 - side) * HALF, 8), 112).astype(bf16)
    table = jnp.broadcast_to(jnp.sum(dots_ref[...], axis=1, keepdims=True), (8, LANES))
    table_ref[...] = table
    upper = table.astype(bf16).astype(f32)
    other_ref[112:128, :] = jnp.concatenate([upper, table - upper], axis=0).astype(bf16)


def rows_of(places, block, read, part, side, start, count):
    pieces = []
    while count:
        index, inside = divmod(start, block)
        take = min(count, block - inside)
        at = places[part][side][index] * block + inside
        pieces.append(read(at, take))
        start, count = start + take, count - take
    return pieces[0] if len(pieces) == 1 else jnp.concatenate(pieces, axis=0)


def half_turns():
    source = lax.broadcasted_iota(jnp.int32, (2 * LANES, 2 * LANES), 0)
    target = lax.broadcasted_iota(jnp.int32, (2 * LANES, 2 * LANES), 1)
    return (source == target // LANES * LANES + (target + D) % LANES).astype(f32).astype(bf16)


def expand(straight, turned, rows, grads, send):
    low = low_half(rows)
    copies = []
    for tile in range(TAPS // 2):
        (a0, b0), (a1, b1) = tap_place(2 * tile), tap_place(2 * tile + 1)
        left = (straight if b0 % 2 == 0 else turned)[b0 // 2, a0 * rows : (a0 + 1) * rows, :]
        right = (straight if b1 % 2 == 1 else turned)[b1 // 2, a1 * rows : (a1 + 1) * rows, :]
        grads[:, span(tile)] = jnp.where(low, left, right)
        if tile % 13 == 12:
            copies += send(tile // 13, pl.ds((tile - 12) * LANES, 13 * LANES))
    return copies


def read_half(places, block, core, part_is_mine, half_ref):
    part = core if part_is_mine else 1 - core

    def rows(side, start, count):
        def value(which):
            return rows_of(
                places, block, lambda at, take: half_ref[at : at + take, :], which, side, start, count
            )

        return jnp.where(part == 0, value(0), value(1))

    return part, rows


def expand_inner(part, rows, grad_hbm, both, straight, turned, grads, sems):
    for side in range(2):
        for row in range(11):
            at = row * 32 + side * 16
            for plane in range(5):
                both[at : at + 16, span(plane)] = rows(side, plane * 176 + row * 16, 16)
            v = rows(side, 880 + row % 6 * 16, 16)
            if row >= 6:
                v = pltpu.roll(v.astype(f32), D, 1).astype(bf16)
            both[at : at + 16, span(5)] = v
    turn = half_turns()
    for pair in range(3):
        lanes = slice(2 * pair * LANES, 2 * (pair + 1) * LANES)
        v = both[:, lanes]
        swapped = jnp.dot(v, turn, preferred_element_type=f32)
        for plane in range(2):
            straight[2 * pair + plane] = v[:, span(plane)].astype(f32)
            turned[2 * pair + plane] = swapped[:, span(plane)]

    def send(index, lanes):
        copies = []
        for side in range(2):
            target = pl.ds(pl.multiple_of(side * 32 + part * 16, 16), 16)
            copy = pltpu.make_async_copy(
                grads.at[pl.ds(side * 16, 16), lanes], grad_hbm.at[target, lanes], sems.at[2 * index + side]
            )
            copy.start()
            copies.append(copy)
        return copies

    return expand(straight, turned, 32, grads, send)


def expand_outer(part, rows, grad_hbm, both, straight, turned, grads, sems):
    for side in range(2):
        for plane in range(3):
            both[:, span(2 * plane + side)] = rows(side, plane * 352, 352)
    source = lax.broadcasted_iota(jnp.int32, (2 * LANES, 2 * LANES), 0)
    target = lax.broadcasted_iota(jnp.int32, (2 * LANES, 2 * LANES), 1)
    wanted = (target // 64) * 32 + target % 32 + LANES * (target // 32 % 2)
    place = (source == wanted).astype(f32).astype(bf16)
    other = target // LANES * LANES + (target + D) % LANES
    wanted = (other // 64) * 32 + other % 32 + LANES * (other // 32 % 2)
    place_turned = (source == wanted).astype(f32).astype(bf16)
    for pair in range(3):
        v = both[:, 2 * pair * LANES : 2 * (pair + 1) * LANES]
        for target_ref, matrix in ((straight, place), (turned, place_turned)):
            moved = jnp.dot(v, matrix, preferred_element_type=f32)
            for plane in range(2):
                target_ref[2 * pair + plane] = moved[:, span(plane)]

    def send(index, lanes):
        target = pl.ds(pl.multiple_of(part * 32, 32), 32)
        copy = pltpu.make_async_copy(grads.at[:, lanes], grad_hbm.at[target, lanes], sems.at[index])
        copy.start()
        return [copy]

    return expand(straight, turned, 32, grads, send)


def first_last_kernel(plan_out, where_ref, mine_ref, grad_hbm, *scratch):
    part, rows = read_half(*plan_out, where_ref[1], True, mine_ref)
    for copy in expand_outer(part, rows, grad_hbm, *scratch):
        copy.wait()


def second_last_kernel(
    plan_out,
    plan_in,
    where_ref,
    amp_ref,
    theirs_ref,
    mine_ref,
    own_ref,
    recv_ref,
    table_ref,
    begun_hbm,
    grad_out_hbm,
    grad_in_hbm,
    series_hbm,
    amps_hbm,
    series_ref,
    amps_ref,
    small_sems,
    *scratch,
):
    core = where_ref[1]
    gained = own_ref[...] + recv_ref[0:112, :].astype(f32)[: HALF // 2, :]
    series_ref[...] = gained.reshape(1, HALF * D)
    tail = recv_ref[112:128, :].astype(f32)
    dots = table_ref[...] + tail[0:8, :] + tail[8:16, :]
    mixing = mixing_of(amp_ref[...])
    pick = (
        lax.broadcasted_iota(jnp.int32, (8, K), 0) == lax.broadcasted_iota(jnp.int32, (8, K), 1)
    )
    table = jnp.sum(jnp.where(pick, dots[:, 0:K], 0.0), axis=0, keepdims=True)
    amps_ref[...] = mixing * (table - jnp.sum(mixing * table, axis=-1, keepdims=True))
    copies = [
        pltpu.make_async_copy(series_ref, series_hbm, small_sems.at[0]),
        pltpu.make_async_copy(amps_ref, amps_hbm, small_sems.at[1]),
    ]
    for copy in copies:
        copy.start()
    part, rows = read_half(*plan_out, core, False, theirs_ref)
    copies += expand_outer(part, rows, grad_out_hbm, *scratch[:5])
    part, rows = read_half(*plan_in, core, True, mine_ref)
    copies += expand_inner(part, rows, grad_in_hbm, *scratch[5:])
    for copy in copies:
        copy.wait()


def third_last_kernel(
    plan_in,
    where_ref,
    mine_ref,
    theirs_ref,
    begun_hbm,
    grad_hbm,
    bias_in_hbm,
    bias_out_hbm,
    gain_hbm,
    shift_hbm,
    bias_in_ref,
    bias_out_ref,
    gain_ref,
    shift_ref,
    small_sems,
    *scratch,
):
    core = where_ref[1]
    part, rows = read_half(*plan_in, core, False, theirs_ref)
    _, mine = read_half(*plan_in, core, True, mine_ref)

    def mean(side):
        both = rows(side, 976, 48).astype(f32) + mine(side, 976, 48).astype(f32)
        v = jnp.sum((both / copy_scale()).reshape(12, 4, LANES), axis=0) * (1.0 / 24.0)
        return (v + pltpu.roll(v, D, 1)) * 0.5

    spare, other = mean(0), mean(1)
    bias_in_ref[...] = jnp.concatenate([spare[0:1, 0:32], other[0:1, 0:32]], axis=1)
    bias_out_ref[...] = spare[1:2, 0:64]
    gain_ref[...] = spare[2:3, 0:64]
    shift_ref[...] = spare[3:4, 0:64]
    small = []
    for index, (source, target) in enumerate(
        (
            (bias_in_ref, bias_in_hbm),
            (bias_out_ref, bias_out_hbm),
            (gain_ref, gain_hbm),
            (shift_ref, shift_hbm),
        )
    ):
        copy = pltpu.make_async_copy(source, target, small_sems.at[index])
        copy.start()
        small.append(copy)
    copies = expand_inner(part, rows, grad_hbm, *scratch) + small
    for copy in copies:
        copy.wait()


def on_device(
    series,
    amplitudes,
    periods,
    conv_in,
    bias_in,
    conv_out,
    bias_out,
    norm_gain,
    norm_bias,
    cotangent,
):
    items = lax.axis_size("items")
    bits = items.bit_length() - 1
    me = lax.axis_index("items")
    side = lax.axis_index("narrow")
    core = me % 2
    where = jnp.stack([side, core]).astype(jnp.int32)
    vmem = pl.BlockSpec(memory_space=pltpu.VMEM)
    smem = pl.BlockSpec(memory_space=pltpu.SMEM)
    hbm = pl.BlockSpec(memory_space=pltpu.HBM)
    shape = jax.ShapeDtypeStruct

    def limit(mib):
        return pltpu.CompilerParams(vmem_limit_bytes=mib * 1024 * 1024)

    def cost(flops):
        return pl.CostEstimate(flops=flops, bytes_accessed=4 << 20, transcendentals=0)

    def stay(arrays):
        return [pltpu.with_memory_space_constraint(a, pltpu.VMEM) for a in arrays]

    def far(arrays):
        return [pltpu.with_memory_space_constraint(a, pltpu.HBM) for a in arrays]

    def two(rows, lanes, kind=f32, lead=None):
        dims = (rows, lanes) if lead is None else (lead, rows, lanes)
        return [pltpu.VMEM(dims, kind)] * 2

    margin = NEAR + GRID + 336
    halved = list(range(1, bits - 1))
    blocks = 2 ** len(halved)
    half_out = -(-1056 // (16 * blocks)) * 16 * blocks
    send, total, part, w1, w2, xs, ua, slope = pl.pallas_call(
        forward_kernel,
        out_shape=(
            pltpu.VMEM((FOLD + 112, LANES), bf16),
            pltpu.VMEM((FOLD, LANES), f32),
            pltpu.VMEM((K, FOLD, LANES), f32),
            pltpu.HBM((WIDE, FULL), bf16),
            pltpu.VMEM((FULL, WIDE), bf16),
            pltpu.VMEM((PAIR, LANES), bf16),
            pltpu.VMEM((K, GRID, WIDE), bf16),
            pltpu.VMEM((K, 128, LANES), bf16),
        ),
        in_specs=[smem] + [hbm] * 8,
        out_specs=[vmem, vmem, vmem, hbm, vmem, vmem, vmem, vmem],
        scratch_shapes=[
            pltpu.VMEM((WIDE + LANES, FULL), bf16),
            pltpu.VMEM((FULL, WIDE + LANES), bf16),
            pltpu.VMEM((FULL, 2 * LANES), bf16),
            pltpu.VMEM((K, GRID, FULL), bf16),
            pltpu.SMEM((1, K), jnp.int32),
            pltpu.VMEM((1, K), f32),
            pltpu.VMEM((1, STEPS * D), bf16),
            pltpu.VMEM((1, HALF * D), bf16),
            pltpu.VMEM((32, TAPS * D), bf16),
            pltpu.VMEM((64, TAPS * D), bf16),
            pltpu.VMEM((1, FF), f32),
            pltpu.VMEM((1, D), f32),
            pltpu.VMEM((512, LANES), f32),
            pltpu.VMEM((6, GRID, LANES), bf16),
            pltpu.VMEM((FULL, FULL), bf16),
            *two(512, LANES),
            *two(margin, LANES, f32, 3),
            pltpu.VMEM((3, margin, LANES), f32),
            *two(margin, LANES, f32, 6),
            *two(GRID + 3 * PMAX, LANES),
            *two(GRID + PMAX, LANES),
            *two(2 * QUART, LANES),
            pltpu.VMEM((128, LANES), f32),
            pltpu.SemaphoreType.DMA((12,)),
            pltpu.SemaphoreType.DMA((1,)),
        ],
        compiler_params=limit(28),
        cost_estimate=cost(1 << 33),
        name="forward",
    )(
        where,
        *far(
            [
                periods,
                amplitudes,
                series,
                cotangent,
                conv_in.T,
                conv_out.T,
                bias_in[None, :],
                bias_out[None, :],
            ]
        ),
    )

    def exchange(value, partner):
        pairs = []
        for item in range(items):
            for col in range(2):
                to_item, to_col = partner(item, col)
                pairs.append((item * 2 + col, to_item * 2 + to_col))
        return lax.ppermute(value, ("items", "narrow"), pairs)

    across = lambda item, col: (item, 1 - col)
    chip = lambda item, col: (item ^ 1, col)
    recv = exchange(send, across)

    out, keep_out, give_out, grad, merged, dots, small, w1 = pl.pallas_call(
        outer_kernel,
        out_shape=(
            shape((1, HALF * D), bf16),
            pltpu.VMEM((half_out, LANES), bf16),
            pltpu.VMEM((half_out, LANES), bf16),
            pltpu.VMEM((K, QUART, LANES), f32),
            pltpu.VMEM((PAIR, LANES), f32),
            pltpu.VMEM((8, LANES), f32),
            pltpu.VMEM((8, LANES), f32),
            pltpu.VMEM((WIDE, FULL), bf16),
        ),
        in_specs=[smem, smem] + [vmem] * 6 + [hbm] + [vmem] * 5,
        out_specs=[hbm] + [vmem] * 7,
        scratch_shapes=[
            pltpu.VMEM((PAIR, LANES), f32),
            pltpu.VMEM((PAIR, LANES), f32),
            pltpu.VMEM((PAIR, LANES), f32),
            pltpu.VMEM((PMAX + GRID, LANES), f32),
            pltpu.VMEM((FOLD, LANES), f32),
            *two(NEAR + GRID + NEAR, LANES),
            *two(GRID, FULL, bf16),
            *two(GRID + 32, LANES, f32, 3),
            *two(GRID + 16, LANES),
            *two(2 * QUART, LANES),
            pltpu.VMEM((WIDE, FULL), f32),
            pltpu.VMEM((2 * half_out, LANES), bf16),
            pltpu.VMEM((K, 128, LANES), f32),
            pltpu.VMEM((PAIR, LANES), f32),
            pltpu.VMEM((1, HALF * D), bf16),
            pltpu.SemaphoreType.DMA,
            pltpu.SemaphoreType.DMA,
        ],
        compiler_params=limit(16),
        cost_estimate=cost(1 << 33),
        name="outer",
    )(
        where,
        periods,
        amplitudes,
        cotangent,
        *stay([recv, total, xs, part]),
        *far([w1]),
        *stay([w2, ua, slope]),
        norm_gain[None, :],
        norm_bias[None, :],
    )

    keep_in, give_in = pl.pallas_call(
        inner_kernel,
        out_shape=(
            pltpu.VMEM((HALF_IN, LANES), bf16),
            pltpu.VMEM((HALF_IN, LANES), bf16),
        ),
        in_specs=[smem, smem] + [vmem] * 3,
        out_specs=[vmem] * 2,
        scratch_shapes=[
            *two(3 * PMAX + GRID + NEAR, LANES),
            pltpu.VMEM((512, LANES), f32),
            pltpu.VMEM((6, GRID, LANES), bf16),
            *two(GRID, WIDE, bf16),
            *two(GRID, FULL, bf16),
            pltpu.VMEM((WIDE, FULL), f32),
            pltpu.VMEM((2 * HALF_IN, LANES), bf16),
        ],
        compiler_params=limit(16),
        cost_estimate=cost(1 << 33),
        name="inner",
    )(where, periods, *stay([grad, small, xs]))

    by_rows = [
        *two(3 * PMAX + GRID + NEAR, LANES),
        *two(GRID, WIDE, bf16),
        *two(GRID + 32, LANES, f32, 6),
    ]

    def series_begin(grad, w1):
        return pl.pallas_call(
            series_kernel,
            out_shape=pltpu.VMEM((GRID, LANES), f32),
            in_specs=[smem] + [vmem] * 2,
            out_specs=vmem,
            scratch_shapes=by_rows,
            compiler_params=limit(16),
            cost_estimate=cost(1 << 31),
            name="series",
        )(periods, *stay([grad, w1]))

    def series_rest(grad, w1, begun):
        return pl.pallas_call(
            series_rest_kernel,
            out_shape=(
                pltpu.VMEM((HALF // 2, LANES), f32),
                pltpu.VMEM((128, LANES), bf16),
                pltpu.VMEM((8, LANES), f32),
            ),
            in_specs=[smem, smem] + [vmem] * 5,
            out_specs=[vmem] * 3,
            scratch_shapes=[
                *by_rows,
                pltpu.VMEM((GRID, LANES), f32),
                pltpu.VMEM((PAIR, LANES), f32),
                pltpu.VMEM((PAIR, LANES), f32),
            ],
            compiler_params=limit(16),
            cost_estimate=cost(1 << 31),
            name="series_rest",
        )(where, periods, *stay([grad, merged, dots, w1, begun]))

    def partner_of(stage):
        def partner(item, col):
            axis = stage[item % 2]
            if axis is None:
                return (item, 1 - col)
            return (item ^ (1 << axis), col)

        return partner

    def bit_of(stage):
        values = [side if axis is None else (me >> axis) & 1 for axis in stage]
        return jnp.where(core == 0, values[0], values[1])

    def merge(bit, a, b):
        return jnp.concatenate([jnp.where(bit == 0, a, b), jnp.where(bit == 0, b, a)], axis=0)

    orders = (halved, halved[1::-1] + halved[2:])
    sequences = ([None] + halved[::-1], halved[::-1] + [None])

    def start_chain(keep, give):
        return keep.astype(f32) + exchange(give, chip).astype(f32)

    def halve(acc, position):
        stage = (orders[0][position], orders[1][position])
        bit = bit_of(stage)
        size = acc.shape[0] // 2
        gone = lax.dynamic_slice_in_dim(acc, (1 - bit) * size, size, 0).astype(bf16)
        kept = lax.dynamic_slice_in_dim(acc, bit * size, size, 0)
        return kept, gone, stage

    def sum_last(acc):
        mine = acc.astype(bf16)
        if bits > 1:
            theirs = exchange(mine, partner_of((bits - 1, bits - 1)))
            mine = (mine.astype(f32) + theirs.astype(f32)).astype(bf16)
        return mine

    def gather(mine, extra=None):
        came = []
        for position in range(len(sequences[0])):
            stage = (sequences[0][position], sequences[1][position])
            if extra is not None and None in stage:
                both = exchange(jnp.concatenate([mine, extra], axis=0), partner_of(stage))
                theirs = both[: mine.shape[0]]
                came.append(both[mine.shape[0] :])
            else:
                theirs = exchange(mine, partner_of(stage))
            mine = merge(bit_of(stage), mine, theirs)
        received = None if extra is None else jnp.where(core == 0, came[0], came[-1])
        return mine, exchange(mine, chip), received

    acc_out = start_chain(keep_out, give_out)
    acc_in = start_chain(keep_in, give_in)
    begun = None
    for position in range(len(halved)):
        kept_out, gone_out, stage = halve(acc_out, position)
        acc_out = kept_out + exchange(gone_out, partner_of(stage)).astype(f32)
        kept_in, gone_in, stage = halve(acc_in, position)
        if position < 2:
            gone_in, grad = lax.optimization_barrier((gone_in, grad))
        came_in = exchange(gone_in, partner_of(stage))
        if position == 0:
            begun = series_begin(grad, w1)
        if position == 1:
            own, other, table = series_rest(grad, w1, begun)
        acc_in = kept_in + came_in.astype(f32)
    if len(halved) < 1:
        begun = series_begin(grad, w1)
    if len(halved) < 2:
        own, other, table = series_rest(grad, w1, begun)
    mine_out, theirs_out, _ = gather(sum_last(acc_out))
    mine_in, theirs_in, received = gather(sum_last(acc_in), other)

    places = []
    for half in range(2):
        by_side = []
        for narrow in range(2):
            listed = []
            for index in range(blocks):
                value = {None: narrow}
                for position, axis in enumerate(orders[half]):
                    value[axis] = (index >> (len(halved) - 1 - position)) & 1
                place = 0
                for position, axis in enumerate(sequences[half]):
                    place += value[axis] << position
                listed.append(place)
            by_side.append(tuple(listed))
        places.append(tuple(by_side))
    places = tuple(places)

    plan_out = (places, half_out // blocks)
    plan_in = (places, HALF_IN // blocks)
    expanding = [
        pltpu.VMEM((352, FULL), bf16),
        pltpu.VMEM((6, 352, LANES), f32),
        pltpu.VMEM((6, 352, LANES), f32),
        pltpu.VMEM((32, TAPS * D), f32),
        pltpu.SemaphoreType.DMA((22,)),
    ]
    grad_out = pl.pallas_call(
        functools.partial(first_last_kernel, plan_out),
        out_shape=shape((D, TAPS * FF), f32),
        in_specs=[smem, vmem],
        out_specs=hbm,
        scratch_shapes=expanding,
        compiler_params=limit(16),
        cost_estimate=cost(1 << 31),
        name="first_last",
    )(where, mine_out)
    grad_out, grad_in, g_series, g_amps = pl.pallas_call(
        functools.partial(second_last_kernel, plan_out, plan_in),
        out_shape=(
            shape((D, TAPS * FF), f32),
            shape((FF, TAPS * D), f32),
            shape((1, HALF * D), f32),
            shape((1, K), f32),
        ),
        in_specs=[smem] + [vmem] * 6 + [hbm],
        out_specs=[hbm] * 4,
        input_output_aliases={7: 0},
        scratch_shapes=[
            pltpu.VMEM((1, HALF * D), f32),
            pltpu.VMEM((1, K), f32),
            pltpu.SemaphoreType.DMA((2,)),
            *expanding,
            *expanding,
        ],
        compiler_params=limit(24),
        cost_estimate=cost(1 << 32),
        name="second_last",
    )(where, amplitudes, theirs_out, mine_in, own, received, table, grad_out)
    grad_in, g_bias_in, g_bias_out, g_gain, g_shift = pl.pallas_call(
        functools.partial(third_last_kernel, plan_in),
        out_shape=(
            shape((FF, TAPS * D), f32),
            shape((1, FF), f32),
            shape((1, D), f32),
            shape((1, D), f32),
            shape((1, D), f32),
        ),
        in_specs=[smem, vmem, vmem, hbm],
        out_specs=[hbm] * 5,
        input_output_aliases={3: 0},
        scratch_shapes=[pltpu.VMEM((1, D), f32)] * 4 + [pltpu.SemaphoreType.DMA((4,))] + expanding,
        compiler_params=limit(16),
        cost_estimate=cost(1 << 31),
        name="third_last",
    )(where, mine_in, theirs_in, grad_in)
    return (
        out,
        g_series,
        g_amps,
        grad_in.T,
        g_bias_in[0],
        grad_out.T,
        g_bias_out[0],
        g_gain[0],
        g_shift[0],
    )


def solution(mesh):
    in_specs = (
        P("items", None),
        P("items", None),
        P("items", None),
        P(),
        P(),
        P(),
        P(),
        P(),
        P(),
        P("items", "narrow"),
    )
    out_specs = (
        P("items", "narrow"),
        P("items", "narrow"),
        P("items", None),
        P(),
        P(),
        P(),
        P(),
        P(),
        P(),
    )
    return jax.shard_map(
        on_device, mesh=mesh, in_specs=in_specs, out_specs=out_specs, check_vma=False
    )
```

```python
import functools
import math

import jax
import jax.numpy as jnp
from jax import lax
from jax.experimental import pallas as pl
from jax.experimental.pallas import tpu as pltpu
from jax.sharding import PartitionSpec as P

D = 64
FF = 64
K = 5
TAPS = 286
STEPS = 432
PMAX = 48
GRID = 480
HALF = STEPS // 2
LANES = 128
kernel_sizes = (1, 3, 5, 7, 9, 11)
epsilon = 1e-05
f32 = jnp.float32
bf16 = jnp.bfloat16

PAIR = 448
FOLD = PAIR // 2
QUART = GRID // 4
NEAR = 5 * PMAX
WIDE = 12 * 32
FULL = 12 * D
HALF_IN = 1024
STEP = 48


def tap_index(size, row, col):
    radius = (size - 1) // 2
    first = sum(k * k for k in kernel_sizes if k < size)
    return first + (row + radius) * size + col + radius


def tap_place(tap):
    for size in kernel_sizes:
        inside = tap - tap_index(size, -(size // 2), -(size // 2))
        if 0 <= inside < size * size:
            return inside // size - size // 2 + 5, inside % size - size // 2 + 5
    return None


def lane_of(rows):
    return lax.broadcasted_iota(jnp.int32, (rows, LANES), 1)


def row_of(rows):
    return lax.broadcasted_iota(jnp.int32, (rows, LANES), 0)


def low_half(rows):
    return lane_of(rows) < D


def span(plane):
    return slice(plane * LANES, (plane + 1) * LANES)


def four_quarters(v):
    v = v + pltpu.roll(v, 64, 1)
    return v + pltpu.roll(v, 32, 1)


def quarter_select(parts, rows):
    lane = lane_of(rows)
    upper = jnp.where(lane < 96, parts[2], parts[3])
    lower = jnp.where(lane < 32, parts[0], parts[1])
    return jnp.where(lane < 64, lower, upper)


def pack_pieces(load, store, temp):
    rows = 24
    pieces = []
    for r in range(0, 2 * QUART, rows):

        def piece(r=r):
            low = low_half(rows)
            a, b = load(r, rows), load(2 * QUART + r, rows)
            temp[r : r + rows, :] = jnp.where(low, a, b) + pltpu.roll(jnp.where(low, b, a), 64, 1)

        pieces.append(piece)
    for r in range(0, QUART, rows):

        def piece(r=r):
            even = lane_of(rows) // 32 % 2 == 0
            a, b = temp[r : r + rows, :], temp[QUART + r : QUART + r + rows, :]
            other = jnp.where(even, pltpu.roll(a, 96, 1), pltpu.roll(b, 32, 1))
            store(r, rows, jnp.where(even, a, b) + other)

        pieces.append(piece)
    return pieces


def spread_pieces(read, target, start):
    rows = 40
    pieces = []
    for r in range(0, QUART, rows):

        def piece(r=r):
            packed = read(r, rows)
            turned = [packed if s == 0 else pltpu.roll(packed, 32 * s, 1) for s in range(4)]
            for q in range(4):
                lanes = slice(32 * q, 32 * q + 32)
                for block in range(4):
                    target[pl.ds(start(q) + block * QUART + r, rows), lanes] = turned[
                        (q - block) % 4
                    ][:, lanes]

        pieces.append(piece)
    return pieces


def rounded(v):
    return v.astype(bf16).astype(f32)


def spread_pairs(pairs, ref, start):
    rows = pairs.shape[0]
    other = pltpu.roll(pairs, D, 1)
    low = low_half(rows)
    ref[pl.ds(start, rows, stride=2), :] = jnp.where(low, pairs, other)
    ref[pl.ds(start + 1, rows, stride=2), :] = jnp.where(low, other, pairs)


def flat_pairs(ref, rows):
    return ref[...].astype(f32).reshape(rows, LANES)


def gather_pairs(ref, start, rows):
    return jnp.where(
        low_half(rows),
        ref[pl.ds(start, rows, stride=2), :],
        ref[pl.ds(start + 1, rows, stride=2), :],
    )


def combine_tile(load, rows, row, plane):
    low = low_half(rows)
    col0, col1 = 2 * plane - 5, 2 * plane - 4
    even = odd = None
    for size in kernel_sizes:
        radius = (size - 1) // 2
        in0, in1 = abs(col0) <= radius, abs(col1) <= radius
        if abs(row) > radius or not (in0 or in1):
            continue
        first = tap_index(size, row, col0)
        if first % 2 == 0:
            v = load(first // 2)
            if not in0:
                v = jnp.where(low, 0.0, v)
            if not in1:
                v = jnp.where(low, v, 0.0)
            even = v if even is None else even + v
        else:
            left = load(first // 2) if in0 else 0.0
            right = load(first // 2 + 1) if in1 else 0.0
            v = jnp.where(low, right, left)
            odd = v if odd is None else odd + v
    if odd is not None:
        odd = pltpu.roll(odd, D, 1)
        even = odd if even is None else even + odd
    return even


def widths(period):
    width = jnp.full((8, LANES), period, jnp.int32).astype(f32)
    return width, 1.0 / width


def column_of(width, inverse, rows, ahead, start):
    position = (row_of(rows) + ahead + start).astype(f32)
    many = jnp.broadcast_to(width[0:1, :], (rows, LANES))
    turns = jnp.floor((position + 0.5) * jnp.broadcast_to(inverse[0:1, :], (rows, LANES)))
    return position - turns * many


def mixing_of(amp):
    shifted = jnp.exp(amp - jnp.max(amp, axis=-1, keepdims=True))
    return shifted / jnp.sum(shifted, axis=-1, keepdims=True)


def gelu_both(v):
    cdf = 0.5 * (1.0 + lax.erf(v * (1.0 / math.sqrt(2.0))))
    density = jnp.exp(-0.5 * v * v) * (1.0 / math.sqrt(2.0 * math.pi))
    return v * cdf, cdf + v * density


def contract(a, b, dim_a, dim_b):
    return lax.dot_general(
        a, b, (((dim_a,), (dim_b,)), ((), ())), preferred_element_type=f32
    )


def together(*streams):
    lists = [list(stream) for stream in streams]
    marks = []
    for number, pieces in enumerate(lists):
        for index, piece in enumerate(pieces):
            marks.append(((index + 0.5) / len(pieces), number, piece))
    for _, _, piece in sorted(marks, key=lambda mark: mark[:2]):
        piece()


def unfold_columns(period, shifted, target):
    pieces = []
    for t in range(0, GRID, STEP):

        def piece(t=t):
            width, inverse = widths(period)
            many = jnp.broadcast_to(width[0:1, :], (STEP, LANES)).astype(bf16)
            zero = jnp.zeros((STEP, LANES), bf16)
            col = column_of(width, inverse, STEP, 0, t)
            col = (col + jnp.where(low_half(STEP), 0.0, 1.0)).astype(bf16)
            for plane in range(6):
                shift = 2 * plane - 5
                inside = (col >= jnp.asarray(-shift, bf16)) & (col < many - jnp.asarray(shift, bf16))
                target[t : t + STEP, span(plane)] = jnp.where(
                    inside, shifted[plane, t : t + STEP, :], zero
                )

        pieces.append(piece)
    return pieces


def shift_columns(xs, shifted):
    for t in range(0, GRID, STEP):
        low = low_half(STEP)
        for plane in range(6):
            at = 16 + t + 2 * plane - 5
            shifted[plane, t : t + STEP, :] = jnp.where(
                low, xs[pl.ds(at, STEP), :], xs[pl.ds(at + 1, STEP), :]
            ).astype(bf16)


def product_pieces(read, read_weight, target, start, planes, dims):
    pieces = []
    for plane in range(0, planes, 2):

        def piece(plane=plane):
            count = min(2, planes - plane)
            lanes = slice(plane * LANES, (plane + count) * LANES)
            product = contract(read(), read_weight(lanes), *dims)
            for index in range(count):
                target[plane + index, start : start + GRID, :] = product[:, span(index)]

        pieces.append(piece)
    return pieces


def weight_pieces(read, read_other, total, first):
    def piece():
        value = contract(read(), read_other(), 0, 0)
        if first:
            total[...] = value
        else:
            total[...] += value

    return [piece]


def forward_kernel(
    where_ref,
    periods_hbm,
    amp_hbm,
    x_hbm,
    cot_hbm,
    conv_in_hbm,
    conv_out_hbm,
    bias_in_hbm,
    bias_out_hbm,
    send_ref,
    total,
    part_ref,
    w1_hbm,
    w2_ref,
    item_ref,
    ua_ref,
    slope_ref,
    w1_wide,
    w2_wide,
    r2,
    ux_ref,
    periods_ref,
    amp_ref,
    x_ref,
    cot_ref,
    conv_in_ref,
    conv_out_ref,
    bias_in_ref,
    bias_out_ref,
    xs,
    xb,
    c2,
    act0,
    act1,
    ys0,
    ys1,
    ys2,
    zs0,
    zs1,
    ss0,
    ss1,
    st0,
    st1,
    tp0,
    tp1,
    slopes,
    sems,
    sent,
):
    side = where_ref[0]
    half = pl.multiple_of(side * 32, 32)
    sources = [
        (x_hbm, x_ref),
        (periods_hbm, periods_ref),
        (amp_hbm, amp_ref),
        (bias_in_hbm, bias_in_ref),
        (bias_out_hbm, bias_out_ref),
        (cot_hbm, cot_ref),
    ]
    for piece in range(2):
        rows = pl.ds(pl.multiple_of(half + 16 * piece, 16), 16)
        sources.append((conv_in_hbm.at[rows, :], conv_in_ref.at[pl.ds(16 * piece, 16), :]))
    for piece in range(4):
        rows = pl.ds(16 * piece, 16)
        sources.append((conv_out_hbm.at[rows, :], conv_out_ref.at[rows, :]))
    copies = [pltpu.make_async_copy(a, b, sems.at[i]) for i, (a, b) in enumerate(sources)]
    for copy in copies:
        copy.start()
    xs[...] = jnp.zeros_like(xs)
    slopes[QUART:, :] = jnp.zeros((128 - QUART, LANES), f32)
    for ref in (act0, act1):
        ref[...] = jnp.zeros_like(ref)
    for refs, per_plane, ahead in (((ys0, ys1, ys2), 4, 3 * PMAX), ((zs0, zs1), 2, PMAX)):
        for plane in range(12 // per_plane):
            moved = per_plane * plane - 5
            top = -moved * PMAX if moved < 0 else 0
            bottom = ahead + (2 * moved if moved < 0 else moved * PMAX)
            for ref in refs:
                if top:
                    ref[plane, NEAR - top : NEAR, :] = jnp.zeros((top, LANES), f32)
                ref[plane, NEAR + GRID : NEAR + GRID + bottom, :] = jnp.zeros((bottom, LANES), f32)
    source = lax.broadcasted_iota(jnp.int32, (2 * LANES, LANES), 0)
    target = lax.broadcasted_iota(jnp.int32, (2 * LANES, LANES), 1)
    wanted = (target // 32) * 64 + side * 32 + target % 32
    choose = (source == wanted).astype(f32).astype(bf16)
    w1_wide[352:384, :] = jnp.zeros((32, FULL), bf16)
    c2[704:768, :] = jnp.zeros((64, FULL), bf16)
    r2[704:768, :] = jnp.zeros((64, 2 * LANES), bf16)

    copies[0].wait()
    spread_pairs(flat_pairs(x_ref, HALF), xs, 16)
    shift_columns(xs, xb)
    for copy in copies[1:6]:
        copy.wait()
    bias_in = jnp.concatenate([bias_in_ref[...], bias_in_ref[...]], axis=1)
    bias_in = jnp.where(side == 0, bias_in, pltpu.roll(bias_in, 96, 1))
    bias_in = four_quarters(jnp.where(lane_of(1) < 32, bias_in, 0.0))
    bias_out = jnp.concatenate([bias_out_ref[...], bias_out_ref[...]], axis=1)
    bias_out = jnp.where(side == 0, bias_out, 0.0)
    mixing = mixing_of(amp_ref[...])
    leaving = []

    def leave(ref, target):
        copy = pltpu.make_async_copy(ref, target, sent.at[len(leaving)])
        copy.start()
        leaving.append(copy)

    def unfold(k):
        return unfold_columns(periods_ref[0, k], xb, ux_ref.at[k])

    def first_product(k):
        target = (ys0, ys1, ys2)[k % 3]

        def piece():
            product = contract(ux_ref[k], w1_wide[...], 1, 1)
            for plane in range(3):
                value = product[:, span(plane)]
                if plane == 1:
                    value = value + product[:, span(3)]
                target[plane, NEAR : NEAR + GRID, :] = value

        return [piece]

    def second_product(k):
        target = (zs0, zs1)[k % 2]
        pieces = []
        for plane in range(0, 6, 2):

            def piece(plane=plane):
                lanes = slice(plane * LANES, (plane + 2) * LANES)
                value = ua_ref[k]
                value = jnp.concatenate([value, value[:, span(1)]], axis=1)
                product = contract(value, w2_wide[lanes, :], 1, 1)
                for index in range(2):
                    target[plane + index, NEAR : NEAR + GRID, :] = product[:, span(index)]

            pieces.append(piece)
        return pieces

    def activate(k):
        ys, ss, act, temp = (ys0, ys1, ys2)[k % 3], (ss0, ss1)[k % 2], (act0, act1)[k % 2], (tp0, tp1)[k % 2]
        period = periods_ref[0, k]
        used = lax.div(STEPS + period - 1, period) * period
        pieces = []
        for t in range(0, GRID + 3 * PMAX, STEP):

            def piece(t=t):
                value = ys[0, pl.ds(NEAR + t - 5 * period, STEP), :]
                for plane in range(1, 3):
                    value = value + ys[plane, pl.ds(NEAR + t + (4 * plane - 5) * period, STEP), :]
                ss[t : t + STEP, :] = value

            pieces.append(piece)

        def load(r, rows):
            return quarter_select([ss[pl.ds(r + q * period, rows), :] for q in range(4)], rows)

        def store(r, rows, value):
            hidden = value * (1.0 / 6.0) + bias_in
            active, slope = gelu_both(hidden)
            position = row_of(rows) + r + QUART * (lane_of(rows) // 32)
            slopes[r : r + rows, :] = jnp.where(position < used, slope, 0.0)
            temp[r : r + rows, :] = jnp.where(position < used, active, 0.0)

        def keep_slope():
            slope_ref[k] = slopes[...].astype(bf16)

        pieces += pack_pieces(load, store, temp)
        pieces.append(keep_slope)
        pieces += spread_pieces(lambda r, rows: temp[r : r + rows, :], act, lambda q: 16 - q)
        for t in range(0, GRID, STEP):

            def piece(t=t):
                width, inverse = widths(period)
                many = jnp.broadcast_to(width[0:1, :], (STEP, LANES)).astype(bf16)
                zero = jnp.zeros((STEP, LANES), bf16)
                col = column_of(width, inverse, STEP, 0, t) + (lane_of(STEP) // 32).astype(f32)
                col = col.astype(bf16)
                for plane in range(3):
                    shift = 4 * plane - 5
                    inside = (col >= jnp.asarray(-shift, bf16)) & (
                        col < many - jnp.asarray(shift, bf16)
                    )
                    moved = act[pl.ds(16 + t + shift, STEP), :].astype(bf16)
                    ua_ref[k, t : t + STEP, span(plane)] = jnp.where(inside, moved, zero)

            pieces.append(piece)
        return pieces

    def finish(k):
        zs, ss = (zs0, zs1)[k % 2], (st0, st1)[k % 2]
        period = periods_ref[0, k]
        weight = mixing[:, k : k + 1]
        pieces = []
        for t in range(0, GRID + PMAX, STEP):

            def piece(t=t):
                value = zs[0, pl.ds(NEAR + t - 5 * period, STEP), :]
                for plane in range(1, 6):
                    value = value + zs[plane, pl.ds(NEAR + t + (2 * plane - 5) * period, STEP), :]
                ss[t : t + STEP, :] = value

            pieces.append(piece)
        rows = 32
        for r in range(0, FOLD, rows):

            def piece(r=r):
                low = low_half(rows)
                near = jnp.where(low, ss[pl.ds(r, rows), :], ss[pl.ds(FOLD + r + period, rows), :])
                far = jnp.where(low, ss[pl.ds(FOLD + r, rows), :], ss[pl.ds(r + period, rows), :])
                out = (near + pltpu.roll(far, D, 1)) * (1.0 / 6.0) + bias_out
                part_ref[k, r : r + rows, :] = out
                if k == 0:
                    total[r : r + rows, :] = weight * out
                else:
                    total[r : r + rows, :] += weight * out

            pieces.append(piece)
        return pieces

    def combine_in():
        pieces = []
        for row in range(-5, 6):

            def piece(row=row):
                at = (row + 5) * 32
                for plane in range(6):
                    v = combine_tile(lambda tile: conv_in_ref[:, span(tile)].astype(f32), 32, row, plane)
                    w1_wide[at : at + 32, span(plane)] = v.astype(bf16)
                    if -1 <= row <= 2:
                        w1_wide[WIDE + at - 128 : WIDE + at - 96, span(plane)] = (v - rounded(v)).astype(bf16)

            pieces.append(piece)
        return pieces

    def combine_out():
        pieces = []
        for row in range(-5, 6):

            def piece(row=row):
                at = (row + 5) * 64
                for plane in range(6):
                    v = combine_tile(lambda tile: conv_out_ref[:, span(tile)].astype(f32), 64, row, plane)
                    c2[at : at + 64, span(plane)] = v.astype(bf16)
                    if plane // 2 == 1:
                        r2[at : at + 64, span(plane % 2)] = (v - rounded(v)).astype(bf16)

            pieces.append(piece)
        return pieces

    def choose_half():
        pieces = []
        for plane in range(3):

            def piece(plane=plane):
                lanes = slice(2 * plane * LANES, 2 * (plane + 1) * LANES)
                w2_wide[:, span(plane)] = jnp.dot(
                    c2[:, lanes], choose, preferred_element_type=f32
                ).astype(bf16)

            pieces.append(piece)

        def piece():
            w2_wide[:, span(3)] = jnp.dot(r2[...], choose, preferred_element_type=f32).astype(bf16)

        return pieces + [piece]

    together(unfold(0))
    together(unfold(1))
    for copy in copies[6:]:
        copy.wait()
    together(combine_in())
    leave(w1_wide.at[pl.ds(0, WIDE), :], w1_hbm)
    combining = combine_out()
    together(first_product(0), combining[:6])
    together(first_product(1), combining[6:], unfold(2))
    together(choose_half(), activate(0))
    w2_ref[...] = w2_wide[:, 0:WIDE]
    together(first_product(2), activate(1), unfold(3))
    together(second_product(0), activate(2))
    together(first_product(3), finish(0), unfold(4))
    together(second_product(1), activate(3))
    together(first_product(4), finish(1))
    together(second_product(2), activate(4))
    together(second_product(3), finish(2))
    together(second_product(4), finish(3))
    together(finish(4))

    send_ref[0:FOLD, :] = total[...].astype(bf16)
    item_ref[...] = xs[16 : 16 + PAIR, :].astype(bf16)
    send_ref[FOLD:, :] = jnp.concatenate(
        [flat_pairs(cot_ref, HALF // 2), jnp.zeros((4, LANES), f32)], axis=0
    ).astype(bf16)
    for copy in leaving:
        copy.wait()


def outer_kernel(
    where_ref,
    periods_ref,
    amp_ref,
    cot_ref,
    recv_ref,
    own_ref,
    item_ref,
    part_ref,
    w1_hbm,
    w2_ref,
    ua_ref,
    slope_ref,
    gain_ref,
    shift_ref,
    out_hbm,
    keep_ref,
    send_ref,
    grad_ref,
    merged_ref,
    dots_ref,
    small,
    w1_ref,
    other,
    cot,
    outs,
    gm,
    gmp,
    rw0,
    rw1,
    gb0,
    gb1,
    zs0,
    zs1,
    vs0,
    vs1,
    tp0,
    tp1,
    dw,
    packed,
    slopes,
    item,
    out_ref,
    sem,
    out_sem,
):
    coming = pltpu.make_async_copy(w1_hbm, w1_ref, sem)
    coming.start()
    slopes[...] = slope_ref[...].astype(f32)
    item[...] = item_ref[...].astype(f32)
    side = where_ref[0]
    core = where_ref[1]
    mixing = mixing_of(amp_ref[...])
    small[...] = jnp.zeros_like(small)
    for ref in (rw0, rw1):
        ref[0:NEAR, :] = jnp.zeros((NEAR, LANES), f32)
        ref[NEAR + GRID :, :] = jnp.zeros((NEAR, LANES), f32)
    for ref in (zs0, zs1):
        ref[:, 0:16, :] = jnp.zeros((3, 16, LANES), f32)
        ref[:, 16 + GRID :, :] = jnp.zeros((3, 16, LANES), f32)
    gm[0:PMAX, :] = jnp.zeros((PMAX, LANES), f32)
    gm[PMAX + PAIR :, :] = jnp.zeros((GRID - PAIR, LANES), f32)

    low = low_half(FOLD)
    v = own_ref[...] + recv_ref[0:FOLD, :].astype(f32)
    turned = pltpu.roll(v, D, 1)
    other[0:FOLD, :] = jnp.where(low, v, turned)
    other[FOLD:, :] = jnp.where(low, turned, v)
    mine = flat_pairs(cot_ref, HALF // 2)
    theirs = recv_ref[FOLD:, :].astype(f32)[: HALF // 2, :]
    cot[STEPS:, :] = jnp.zeros((PAIR - STEPS, LANES), f32)
    spread_pairs(jnp.where(side == 0, mine, theirs), cot, 0)
    spread_pairs(jnp.where(side == 0, theirs, mine), cot, HALF)
    gain = jnp.concatenate([gain_ref[...], gain_ref[...]], axis=1)
    shift = jnp.concatenate([shift_ref[...], shift_ref[...]], axis=1)
    grad_gain = grad_shift = grad_bias = jnp.zeros((8, LANES), f32)

    def eights(v):
        return jnp.sum(v.reshape(-1, 8, LANES), axis=0)

    for t in range(0, PAIR, 56):
        rows = slice(t, t + 56)
        total = item[rows, :] + other[rows, :]
        centred = total - jnp.mean(total, axis=-1, keepdims=True)
        variance = jnp.mean(centred * centred, axis=-1, keepdims=True)
        inverse = lax.rsqrt(variance + epsilon)
        normed = centred * inverse
        outs[rows, :] = normed * gain + shift
        c = cot[rows, :]
        grad_gain = grad_gain + eights(c * normed)
        grad_shift = grad_shift + eights(c)
        e = c * gain
        grad = inverse * (
            e
            - jnp.mean(e, axis=-1, keepdims=True)
            - normed * jnp.mean(e * normed, axis=-1, keepdims=True)
        )
        gm[PMAX + t : PMAX + t + 56, :] = grad
        merged_ref[rows, :] = grad
        grad_bias = grad_bias + eights(grad)
    grad_bias = grad_bias * jnp.sum(mixing, axis=-1, keepdims=True)
    small[1:2, :] = jnp.sum(grad_bias, axis=0, keepdims=True)
    small[2:3, :] = jnp.sum(grad_gain, axis=0, keepdims=True)
    small[3:4, :] = jnp.sum(grad_shift, axis=0, keepdims=True)
    first = pl.multiple_of(side * HALF, 8)
    out_ref[...] = gather_pairs(outs, first, HALF // 2).reshape(1, HALF * D).astype(bf16)
    leaving = pltpu.make_async_copy(out_ref, out_hbm, out_sem)
    leaving.start()
    rows = 32
    for r in range(0, FOLD, rows):
        gmp[r : r + rows, :] = jnp.where(
            low_half(rows),
            gm[PMAX + r : PMAX + r + rows, :],
            gm[PMAX + FOLD + r : PMAX + FOLD + r + rows, :],
        )

    def unfold(k):
        rowed, gab = (rw0, rw1)[k % 2], (gb0, gb1)[k % 2]
        period = periods_ref[0, k]
        weight = mixing[:, k : k + 1]
        pieces = []
        for t in range(0, GRID, STEP):

            def piece(t=t):
                here = gm[PMAX + t : PMAX + t + STEP, :]
                back = gm[pl.ds(PMAX + t - period, STEP), :]
                rowed[NEAR + t : NEAR + t + STEP, :] = weight * jnp.where(low_half(STEP), here, back)

            pieces.append(piece)
        for t in range(0, GRID, STEP):

            def piece(t=t):
                for plane in range(6):
                    gab[t : t + STEP, span(plane)] = rowed[
                        pl.ds(NEAR + t - (2 * plane - 5) * period, STEP), :
                    ].astype(bf16)

            pieces.append(piece)
        return pieces

    def back(k):
        return product_pieces(
            lambda: (gb0, gb1)[k % 2][...], lambda lanes: w2_ref[:, lanes], (zs0, zs1)[k % 2], 16, 3, (1, 0)
        )

    def weigh(k):
        return weight_pieces(lambda: ua_ref[k], lambda: (gb0, gb1)[k % 2][...], dw, k == 0)

    def fold(k):
        zs, vs, temp = (zs0, zs1)[k % 2], (vs0, vs1)[k % 2], (tp0, tp1)[k % 2]
        period = periods_ref[0, k]
        rows = 16
        pieces = []
        for t in range(0, GRID + 16, rows):

            def piece(t=t):
                width, inverse = widths(period)
                many = jnp.broadcast_to(width[0:1, :], (rows, LANES))
                quarter = lane_of(rows) // 32
                place = column_of(width, inverse, rows, quarter, t - 8) - quarter.astype(f32)
                value = None
                for plane in range(3):
                    s = 4 * plane - 5
                    v = zs[plane, pl.ds(16 - 8 + t - s, rows), :]
                    v = jnp.where((place >= s) & (place < many + s), v, 0.0)
                    value = v if value is None else value + v
                vs[t : t + rows, :] = value

            pieces.append(piece)

        def load(r, rows):
            return quarter_select([vs[pl.ds(8 + r - q, rows), :] for q in range(4)], rows)

        def store(r, rows, value):
            grad_ref[k, r : r + rows, :] = value * slopes[k, r : r + rows, :] * (1.0 / 6.0)

        return pieces + pack_pieces(load, store, temp)

    together(unfold(0))
    for k in range(K):
        streams = [back(k)]
        if k + 1 < K:
            streams.append(unfold(k + 1))
        together(*streams)
        together(weigh(k), fold(k))
    coming.wait()
    leaving.wait()
    bias = None
    for k in range(K):
        v = jnp.sum(grad_ref[k], axis=0, keepdims=True)
        bias = v if bias is None else bias + v
        dots_ref[k : k + 1, :] = jnp.sum(gmp[...] * part_ref[k], axis=0, keepdims=True)
    dots_ref[K:, :] = jnp.zeros((8 - K, LANES), f32)
    small[0:1, :] = four_quarters(bias)
    count = keep_ref.shape[0]
    turned = jnp.transpose((dw[...] * (1.0 / 6.0)).astype(bf16))
    for part in range(2):
        for plane in range(3):
            for row in range(11):
                target = part * count + plane * 352 + row * 32
                source = row * 64 + part * 32
                packed[target : target + 32, :] = turned[source : source + 32, span(plane)]
        packed[part * count + 1056 : (part + 1) * count, :] = jnp.zeros((count - 1056, LANES), bf16)
    keep_ref[...] = packed[pl.ds(pl.multiple_of(core * count, 16), count), :]
    send_ref[...] = packed[pl.ds(pl.multiple_of((1 - core) * count, 16), count), :]


def unfold_rows(period, read, rowed, target, clear):
    edge = 3 * PMAX
    pieces = []
    if clear:

        def piece():
            rowed[edge : 2 * edge, :] = jnp.zeros((edge, LANES), f32)
            rowed[edge + GRID : 2 * edge + GRID, :] = jnp.zeros((edge, LANES), f32)

        pieces.append(piece)
    pieces += spread_pieces(read, rowed, lambda q: edge + q * period)
    for t in range(0, GRID, STEP):

        def piece(t=t):
            for plane in range(3):
                target[t : t + STEP, span(plane)] = rowed[
                    pl.ds(edge + t - (4 * plane - 5) * period, STEP), :
                ].astype(bf16)

        pieces.append(piece)
    return pieces


def copy_scale():
    number = row_of(48) // 4 * 2 + lane_of(48) // D
    return jnp.exp(number.astype(f32) * (math.log(2.0) / 24.0))


def inner_kernel(
    where_ref,
    periods_ref,
    grad_ref,
    small_ref,
    item_ref,
    keep_ref,
    send_ref,
    hr0,
    hr1,
    xs,
    xb,
    gh0,
    gh1,
    ux0,
    ux1,
    dw,
    packed,
):
    core = where_ref[1]
    for ref in (hr0, hr1):
        ref[...] = jnp.zeros_like(ref)
    xs[0:16, :] = jnp.zeros((16, LANES), f32)
    xs[16 : 16 + PAIR, :] = item_ref[...].astype(f32)
    xs[16 + PAIR :, :] = jnp.zeros((512 - 16 - PAIR, LANES), f32)
    shift_columns(xs, xb)

    def unfold(k):
        return unfold_rows(
            periods_ref[0, k],
            lambda r, rows: grad_ref[k, r : r + rows, :],
            (hr0, hr1)[k % 2],
            (gh0, gh1)[k % 2],
            k > 1,
        )

    def again(k):
        return unfold_columns(periods_ref[0, k], xb, (ux0, ux1)[k % 2])

    def weigh(k):
        return weight_pieces(lambda: (gh0, gh1)[k % 2][...], lambda: (ux0, ux1)[k % 2][...], dw, k == 0)

    together(unfold(0), again(0))
    for k in range(K):
        streams = [weigh(k)]
        if k + 1 < K:
            streams += [unfold(k + 1), again(k + 1)]
        together(*streams)

    sixth = 1.0 / 6.0
    for part in range(2):
        at = part * HALF_IN
        for row in range(11):
            source = slice(row * 32 + part * 16, row * 32 + part * 16 + 16)
            for plane in range(5):
                target = at + plane * 176 + row * 16
                packed[target : target + 16, :] = (dw[source, span(plane)] * sixth).astype(bf16)
        for row in range(6):
            source = slice(row * 32 + part * 16, row * 32 + part * 16 + 16)
            other = slice((row + 6) * 32 + part * 16, (row + 6) * 32 + part * 16 + 16)
            v = jnp.where(low_half(16), dw[source, span(5)], pltpu.roll(dw[other, span(5)], D, 1))
            packed[at + 880 + row * 16 : at + 896 + row * 16, :] = (v * sixth).astype(bf16)
        packed[at + 976 : at + 1024, :] = (
            jnp.concatenate([small_ref[0:4, :]] * 12, axis=0) * copy_scale()
        ).astype(bf16)
    count = HALF_IN
    keep_ref[...] = packed[pl.ds(pl.multiple_of(core * count, count), count), :]
    send_ref[...] = packed[pl.ds(pl.multiple_of((1 - core) * count, count), count), :]


def series_pieces(branches, periods_ref, grad_ref, w1_ref, vs, begun, rowed, hidden, planes):
    for ref in rowed:
        ref[...] = jnp.zeros_like(ref)
    for ref in planes:
        ref[:, 0:16, :] = jnp.zeros((6, 16, LANES), f32)
        ref[:, 16 + GRID :, :] = jnp.zeros((6, 16, LANES), f32)

    def unfold(index):
        k = branches[index]
        return unfold_rows(
            periods_ref[0, k],
            lambda r, rows: grad_ref[k, r : r + rows, :],
            rowed[index % 2],
            hidden[index % 2],
            index > 1,
        )

    def back(index):
        return product_pieces(
            lambda: hidden[index % 2][...],
            lambda lanes: w1_ref[:, lanes],
            planes[index % 2],
            16,
            6,
            (1, 0),
        )

    def fold(index):
        zs = planes[index % 2]
        period = periods_ref[0, branches[index]]
        rows = 16
        pieces = []
        for t in range(0, PAIR + 16, rows):

            def piece(t=t):
                width, inverse = widths(period)
                many = jnp.broadcast_to(width[0:1, :], (rows, LANES))
                half = lane_of(rows) // D
                place = column_of(width, inverse, rows, half, t - 8) - half.astype(f32)
                value = None if begun is None or index else begun[t : t + rows, :]
                for plane in range(6):
                    s = 2 * plane - 5
                    v = zs[plane, pl.ds(16 - 8 + t - s, rows), :]
                    v = jnp.where((place >= s) & (place < many + s), v, 0.0)
                    value = v if value is None else value + v
                if index == 0:
                    vs[t : t + rows, :] = value
                else:
                    vs[t : t + rows, :] += value

            pieces.append(piece)
        return pieces

    count = len(branches)
    together(unfold(0))
    together(back(0), *([unfold(1)] if count > 1 else []))
    for index in range(count):
        streams = [fold(index)]
        if index + 1 < count:
            streams.append(back(index + 1))
        if index + 2 < count:
            streams.append(unfold(index + 2))
        together(*streams)


def series_kernel(periods_ref, grad_ref, w1_ref, vs, hr0, hr1, gh0, gh1, zs0, zs1):
    series_pieces(
        range(0, 3), periods_ref, grad_ref, w1_ref, vs, None, (hr0, hr1), (gh0, gh1), (zs0, zs1)
    )


def series_rest_kernel(
    where_ref,
    periods_ref,
    grad_ref,
    merged_ref,
    dots_ref,
    w1_ref,
    begun_ref,
    own_ref,
    other_ref,
    table_ref,
    hr0,
    hr1,
    gh0,
    gh1,
    zs0,
    zs1,
    vs,
    dx,
    outs,
):
    side = where_ref[0]
    series_pieces(
        range(3, K), periods_ref, grad_ref, w1_ref, vs, begun_ref, (hr0, hr1), (gh0, gh1), (zs0, zs1)
    )
    rows = 56
    for t in range(0, PAIR, rows):
        v = jnp.where(low_half(rows), vs[pl.ds(8 + t, rows), :], vs[pl.ds(8 + t - 1, rows), :])
        v = (v + pltpu.roll(v, D, 1)) * (1.0 / 6.0)
        dx[t : t + rows, :] = v
        outs[t : t + rows, :] = v + merged_ref[t : t + rows, :]
    own_ref[...] = gather_pairs(outs, pl.multiple_of(side * HALF, 8), HALF // 2)
    other_ref[0:112, :] = gather_pairs(dx, pl.multiple_of((1 - side) * HALF, 8), 112).astype(bf16)
    table = jnp.broadcast_to(jnp.sum(dots_ref[...], axis=1, keepdims=True), (8, LANES))
    table_ref[...] = table
    upper = table.astype(bf16).astype(f32)
    other_ref[112:128, :] = jnp.concatenate([upper, table - upper], axis=0).astype(bf16)


def rows_of(places, block, read, part, side, start, count):
    pieces = []
    while count:
        index, inside = divmod(start, block)
        take = min(count, block - inside)
        at = places[part][side][index] * block + inside
        pieces.append(read(at, take))
        start, count = start + take, count - take
    return pieces[0] if len(pieces) == 1 else jnp.concatenate(pieces, axis=0)


def half_turns():
    source = lax.broadcasted_iota(jnp.int32, (2 * LANES, 2 * LANES), 0)
    target = lax.broadcasted_iota(jnp.int32, (2 * LANES, 2 * LANES), 1)
    return (source == target // LANES * LANES + (target + D) % LANES).astype(f32).astype(bf16)


def expand(straight, turned, rows, grads, send):
    low = low_half(rows)
    copies = []
    for tile in range(TAPS // 2):
        (a0, b0), (a1, b1) = tap_place(2 * tile), tap_place(2 * tile + 1)
        left = (straight if b0 % 2 == 0 else turned)[b0 // 2, a0 * rows : (a0 + 1) * rows, :]
        right = (straight if b1 % 2 == 1 else turned)[b1 // 2, a1 * rows : (a1 + 1) * rows, :]
        grads[:, span(tile)] = jnp.where(low, left, right)
        if tile % 13 == 12:
            copies += send(tile // 13, pl.ds((tile - 12) * LANES, 13 * LANES))
    return copies


def read_half(places, block, core, part_is_mine, half_ref):
    part = core if part_is_mine else 1 - core

    def rows(side, start, count):
        def value(which):
            return rows_of(
                places, block, lambda at, take: half_ref[at : at + take, :], which, side, start, count
            )

        return jnp.where(part == 0, value(0), value(1))

    return part, rows


def expand_inner(part, rows, grad_hbm, both, straight, turned, grads, sems):
    for side in range(2):
        for row in range(11):
            at = row * 32 + side * 16
            for plane in range(5):
                both[at : at + 16, span(plane)] = rows(side, plane * 176 + row * 16, 16)
            v = rows(side, 880 + row % 6 * 16, 16)
            if row >= 6:
                v = pltpu.roll(v.astype(f32), D, 1).astype(bf16)
            both[at : at + 16, span(5)] = v
    turn = half_turns()
    for pair in range(3):
        lanes = slice(2 * pair * LANES, 2 * (pair + 1) * LANES)
        v = both[:, lanes]
        swapped = jnp.dot(v, turn, preferred_element_type=f32)
        for plane in range(2):
            straight[2 * pair + plane] = v[:, span(plane)].astype(f32)
            turned[2 * pair + plane] = swapped[:, span(plane)]

    def send(index, lanes):
        copies = []
        for side in range(2):
            target = pl.ds(pl.multiple_of(side * 32 + part * 16, 16), 16)
            copy = pltpu.make_async_copy(
                grads.at[pl.ds(side * 16, 16), lanes], grad_hbm.at[target, lanes], sems.at[2 * index + side]
            )
            copy.start()
            copies.append(copy)
        return copies

    return expand(straight, turned, 32, grads, send)


def expand_outer(part, rows, grad_hbm, both, straight, turned, grads, sems):
    for side in range(2):
        for plane in range(3):
            both[:, span(2 * plane + side)] = rows(side, plane * 352, 352)
    source = lax.broadcasted_iota(jnp.int32, (2 * LANES, 2 * LANES), 0)
    target = lax.broadcasted_iota(jnp.int32, (2 * LANES, 2 * LANES), 1)
    wanted = (target // 64) * 32 + target % 32 + LANES * (target // 32 % 2)
    place = (source == wanted).astype(f32).astype(bf16)
    other = target // LANES * LANES + (target + D) % LANES
    wanted = (other // 64) * 32 + other % 32 + LANES * (other // 32 % 2)
    place_turned = (source == wanted).astype(f32).astype(bf16)
    for pair in range(3):
        v = both[:, 2 * pair * LANES : 2 * (pair + 1) * LANES]
        for target_ref, matrix in ((straight, place), (turned, place_turned)):
            moved = jnp.dot(v, matrix, preferred_element_type=f32)
            for plane in range(2):
                target_ref[2 * pair + plane] = moved[:, span(plane)]

    def send(index, lanes):
        target = pl.ds(pl.multiple_of(part * 32, 32), 32)
        copy = pltpu.make_async_copy(grads.at[:, lanes], grad_hbm.at[target, lanes], sems.at[index])
        copy.start()
        return [copy]

    return expand(straight, turned, 32, grads, send)


def first_last_kernel(plan_out, where_ref, mine_ref, grad_hbm, *scratch):
    part, rows = read_half(*plan_out, where_ref[1], True, mine_ref)
    for copy in expand_outer(part, rows, grad_hbm, *scratch):
        copy.wait()


def second_last_kernel(
    plan_out,
    plan_in,
    where_ref,
    amp_ref,
    theirs_ref,
    mine_ref,
    own_ref,
    recv_ref,
    table_ref,
    begun_hbm,
    grad_out_hbm,
    grad_in_hbm,
    series_hbm,
    amps_hbm,
    series_ref,
    amps_ref,
    small_sems,
    *scratch,
):
    core = where_ref[1]
    part, rows = read_half(*plan_out, core, False, theirs_ref)
    copies = expand_outer(part, rows, grad_out_hbm, *scratch[:5])
    gained = own_ref[...] + recv_ref[0:112, :].astype(f32)[: HALF // 2, :]
    series_ref[...] = gained.reshape(1, HALF * D)
    tail = recv_ref[112:128, :].astype(f32)
    dots = table_ref[...] + tail[0:8, :] + tail[8:16, :]
    mixing = mixing_of(amp_ref[...])
    pick = (
        lax.broadcasted_iota(jnp.int32, (8, K), 0) == lax.broadcasted_iota(jnp.int32, (8, K), 1)
    )
    table = jnp.sum(jnp.where(pick, dots[:, 0:K], 0.0), axis=0, keepdims=True)
    amps_ref[...] = mixing * (table - jnp.sum(mixing * table, axis=-1, keepdims=True))
    small = [
        pltpu.make_async_copy(series_ref, series_hbm, small_sems.at[0]),
        pltpu.make_async_copy(amps_ref, amps_hbm, small_sems.at[1]),
    ]
    for copy in small:
        copy.start()
    copies += small
    part, rows = read_half(*plan_in, core, True, mine_ref)
    copies += expand_inner(part, rows, grad_in_hbm, *scratch[5:])
    for copy in copies:
        copy.wait()


def third_last_kernel(
    plan_in,
    where_ref,
    mine_ref,
    theirs_ref,
    begun_hbm,
    grad_hbm,
    bias_in_hbm,
    bias_out_hbm,
    gain_hbm,
    shift_hbm,
    bias_in_ref,
    bias_out_ref,
    gain_ref,
    shift_ref,
    small_sems,
    *scratch,
):
    core = where_ref[1]
    part, rows = read_half(*plan_in, core, False, theirs_ref)
    copies = expand_inner(part, rows, grad_hbm, *scratch)
    _, mine = read_half(*plan_in, core, True, mine_ref)

    def mean(side):
        both = rows(side, 976, 48).astype(f32) + mine(side, 976, 48).astype(f32)
        v = jnp.sum((both / copy_scale()).reshape(12, 4, LANES), axis=0) * (1.0 / 24.0)
        return (v + pltpu.roll(v, D, 1)) * 0.5

    spare, other = mean(0), mean(1)
    bias_in_ref[...] = jnp.concatenate([spare[0:1, 0:32], other[0:1, 0:32]], axis=1)
    bias_out_ref[...] = spare[1:2, 0:64]
    gain_ref[...] = spare[2:3, 0:64]
    shift_ref[...] = spare[3:4, 0:64]
    for index, (source, target) in enumerate(
        (
            (bias_in_ref, bias_in_hbm),
            (bias_out_ref, bias_out_hbm),
            (gain_ref, gain_hbm),
            (shift_ref, shift_hbm),
        )
    ):
        copy = pltpu.make_async_copy(source, target, small_sems.at[index])
        copy.start()
        copies.append(copy)
    for copy in copies:
        copy.wait()


def on_device(
    series,
    amplitudes,
    periods,
    conv_in,
    bias_in,
    conv_out,
    bias_out,
    norm_gain,
    norm_bias,
    cotangent,
):
    items = lax.axis_size("items")
    bits = items.bit_length() - 1
    me = lax.axis_index("items")
    side = lax.axis_index("narrow")
    core = me % 2
    where = jnp.stack([side, core]).astype(jnp.int32)
    vmem = pl.BlockSpec(memory_space=pltpu.VMEM)
    smem = pl.BlockSpec(memory_space=pltpu.SMEM)
    hbm = pl.BlockSpec(memory_space=pltpu.HBM)
    shape = jax.ShapeDtypeStruct

    def limit(mib):
        return pltpu.CompilerParams(vmem_limit_bytes=mib * 1024 * 1024)

    def cost(flops):
        return pl.CostEstimate(flops=flops, bytes_accessed=4 << 20, transcendentals=0)

    def stay(arrays):
        return [pltpu.with_memory_space_constraint(a, pltpu.VMEM) for a in arrays]

    def far(arrays):
        return [pltpu.with_memory_space_constraint(a, pltpu.HBM) for a in arrays]

    def two(rows, lanes, kind=f32, lead=None):
        dims = (rows, lanes) if lead is None else (lead, rows, lanes)
        return [pltpu.VMEM(dims, kind)] * 2

    margin = NEAR + GRID + 336
    halved = list(range(1, bits - 1))
    blocks = 2 ** len(halved)
    half_out = -(-1056 // (16 * blocks)) * 16 * blocks
    send, total, part, w1, w2, xs, ua, slope = pl.pallas_call(
        forward_kernel,
        out_shape=(
            pltpu.VMEM((FOLD + 112, LANES), bf16),
            pltpu.VMEM((FOLD, LANES), f32),
            pltpu.VMEM((K, FOLD, LANES), f32),
            pltpu.HBM((WIDE, FULL), bf16),
            pltpu.VMEM((FULL, WIDE), bf16),
            pltpu.VMEM((PAIR, LANES), bf16),
            pltpu.VMEM((K, GRID, WIDE), bf16),
            pltpu.VMEM((K, 128, LANES), bf16),
        ),
        in_specs=[smem] + [hbm] * 8,
        out_specs=[vmem, vmem, vmem, hbm, vmem, vmem, vmem, vmem],
        scratch_shapes=[
            pltpu.VMEM((WIDE + LANES, FULL), bf16),
            pltpu.VMEM((FULL, WIDE + LANES), bf16),
            pltpu.VMEM((FULL, 2 * LANES), bf16),
            pltpu.VMEM((K, GRID, FULL), bf16),
            pltpu.SMEM((1, K), jnp.int32),
            pltpu.VMEM((1, K), f32),
            pltpu.VMEM((1, STEPS * D), bf16),
            pltpu.VMEM((1, HALF * D), bf16),
            pltpu.VMEM((32, TAPS * D), bf16),
            pltpu.VMEM((64, TAPS * D), bf16),
            pltpu.VMEM((1, FF), f32),
            pltpu.VMEM((1, D), f32),
            pltpu.VMEM((512, LANES), f32),
            pltpu.VMEM((6, GRID, LANES), bf16),
            pltpu.VMEM((FULL, FULL), bf16),
            *two(512, LANES),
            *two(margin, LANES, f32, 3),
            pltpu.VMEM((3, margin, LANES), f32),
            *two(margin, LANES, f32, 6),
            *two(GRID + 3 * PMAX, LANES),
            *two(GRID + PMAX, LANES),
            *two(2 * QUART, LANES),
            pltpu.VMEM((128, LANES), f32),
            pltpu.SemaphoreType.DMA((12,)),
            pltpu.SemaphoreType.DMA((1,)),
        ],
        compiler_params=limit(28),
        cost_estimate=cost(1 << 33),
        name="forward",
    )(
        where,
        *far(
            [
                periods,
                amplitudes,
                series,
                cotangent,
                conv_in.T,
                conv_out.T,
                bias_in[None, :],
                bias_out[None, :],
            ]
        ),
    )

    def exchange(value, partner):
        pairs = []
        for item in range(items):
            for col in range(2):
                to_item, to_col = partner(item, col)
                pairs.append((item * 2 + col, to_item * 2 + to_col))
        return lax.ppermute(value, ("items", "narrow"), pairs)

    across = lambda item, col: (item, 1 - col)
    chip = lambda item, col: (item ^ 1, col)
    recv = exchange(send, across)

    out, keep_out, give_out, grad, merged, dots, small, w1 = pl.pallas_call(
        outer_kernel,
        out_shape=(
            shape((1, HALF * D), bf16),
            pltpu.VMEM((half_out, LANES), bf16),
            pltpu.VMEM((half_out, LANES), bf16),
            pltpu.VMEM((K, QUART, LANES), f32),
            pltpu.VMEM((PAIR, LANES), f32),
            pltpu.VMEM((8, LANES), f32),
            pltpu.VMEM((8, LANES), f32),
            pltpu.VMEM((WIDE, FULL), bf16),
        ),
        in_specs=[smem, smem] + [vmem] * 6 + [hbm] + [vmem] * 5,
        out_specs=[hbm] + [vmem] * 7,
        scratch_shapes=[
            pltpu.VMEM((PAIR, LANES), f32),
            pltpu.VMEM((PAIR, LANES), f32),
            pltpu.VMEM((PAIR, LANES), f32),
            pltpu.VMEM((PMAX + GRID, LANES), f32),
            pltpu.VMEM((FOLD, LANES), f32),
            *two(NEAR + GRID + NEAR, LANES),
            *two(GRID, FULL, bf16),
            *two(GRID + 32, LANES, f32, 3),
            *two(GRID + 16, LANES),
            *two(2 * QUART, LANES),
            pltpu.VMEM((WIDE, FULL), f32),
            pltpu.VMEM((2 * half_out, LANES), bf16),
            pltpu.VMEM((K, 128, LANES), f32),
            pltpu.VMEM((PAIR, LANES), f32),
            pltpu.VMEM((1, HALF * D), bf16),
            pltpu.SemaphoreType.DMA,
            pltpu.SemaphoreType.DMA,
        ],
        compiler_params=limit(16),
        cost_estimate=cost(1 << 33),
        name="outer",
    )(
        where,
        periods,
        amplitudes,
        cotangent,
        *stay([recv, total, xs, part]),
        *far([w1]),
        *stay([w2, ua, slope]),
        norm_gain[None, :],
        norm_bias[None, :],
    )

    keep_in, give_in = pl.pallas_call(
        inner_kernel,
        out_shape=(
            pltpu.VMEM((HALF_IN, LANES), bf16),
            pltpu.VMEM((HALF_IN, LANES), bf16),
        ),
        in_specs=[smem, smem] + [vmem] * 3,
        out_specs=[vmem] * 2,
        scratch_shapes=[
            *two(3 * PMAX + GRID + NEAR, LANES),
            pltpu.VMEM((512, LANES), f32),
            pltpu.VMEM((6, GRID, LANES), bf16),
            *two(GRID, WIDE, bf16),
            *two(GRID, FULL, bf16),
            pltpu.VMEM((WIDE, FULL), f32),
            pltpu.VMEM((2 * HALF_IN, LANES), bf16),
        ],
        compiler_params=limit(16),
        cost_estimate=cost(1 << 33),
        name="inner",
    )(where, periods, *stay([grad, small, xs]))

    by_rows = [
        *two(3 * PMAX + GRID + NEAR, LANES),
        *two(GRID, WIDE, bf16),
        *two(GRID + 32, LANES, f32, 6),
    ]

    def series_begin(grad, w1):
        return pl.pallas_call(
            series_kernel,
            out_shape=pltpu.VMEM((GRID, LANES), f32),
            in_specs=[smem] + [vmem] * 2,
            out_specs=vmem,
            scratch_shapes=by_rows,
            compiler_params=limit(16),
            cost_estimate=cost(1 << 31),
            name="series",
        )(periods, *stay([grad, w1]))

    def series_rest(grad, w1, begun):
        return pl.pallas_call(
            series_rest_kernel,
            out_shape=(
                pltpu.VMEM((HALF // 2, LANES), f32),
                pltpu.VMEM((128, LANES), bf16),
                pltpu.VMEM((8, LANES), f32),
            ),
            in_specs=[smem, smem] + [vmem] * 5,
            out_specs=[vmem] * 3,
            scratch_shapes=[
                *by_rows,
                pltpu.VMEM((GRID, LANES), f32),
                pltpu.VMEM((PAIR, LANES), f32),
                pltpu.VMEM((PAIR, LANES), f32),
            ],
            compiler_params=limit(16),
            cost_estimate=cost(1 << 31),
            name="series_rest",
        )(where, periods, *stay([grad, merged, dots, w1, begun]))

    def partner_of(stage):
        def partner(item, col):
            axis = stage[item % 2]
            if axis is None:
                return (item, 1 - col)
            return (item ^ (1 << axis), col)

        return partner

    def bit_of(stage):
        values = [side if axis is None else (me >> axis) & 1 for axis in stage]
        return jnp.where(core == 0, values[0], values[1])

    def merge(bit, a, b):
        return jnp.where(bit == 0, jnp.concatenate([a, b], axis=0), jnp.concatenate([b, a], axis=0))

    orders = (halved, halved[1::-1] + halved[2:])
    sequences = ([None] + halved[::-1], halved[::-1] + [None])

    def start_chain(keep, give):
        return keep.astype(f32) + exchange(give, chip).astype(f32)

    def halve(acc, position):
        stage = (orders[0][position], orders[1][position])
        bit = bit_of(stage)
        size = acc.shape[0] // 2
        gone = lax.dynamic_slice_in_dim(acc, (1 - bit) * size, size, 0).astype(bf16)
        kept = lax.dynamic_slice_in_dim(acc, bit * size, size, 0)
        return kept, gone, stage

    def sum_last(acc):
        mine = acc.astype(bf16)
        if bits > 1:
            theirs = exchange(mine, partner_of((bits - 1, bits - 1)))
            mine = (mine.astype(f32) + theirs.astype(f32)).astype(bf16)
        return mine

    def gather(mine, extra=None):
        came = []
        for position in range(len(sequences[0])):
            stage = (sequences[0][position], sequences[1][position])
            if extra is not None and None in stage:
                both = exchange(jnp.concatenate([mine, extra], axis=0), partner_of(stage))
                theirs = both[: mine.shape[0]]
                came.append(both[mine.shape[0] :])
            else:
                theirs = exchange(mine, partner_of(stage))
            mine = merge(bit_of(stage), mine, theirs)
        received = None if extra is None else jnp.where(core == 0, came[0], came[-1])
        return mine, exchange(mine, chip), received

    acc_out = start_chain(keep_out, give_out)
    acc_in = start_chain(keep_in, give_in)
    begun = None
    for position in range(len(halved)):
        kept_out, gone_out, stage = halve(acc_out, position)
        acc_out = kept_out + exchange(gone_out, partner_of(stage)).astype(f32)
        kept_in, gone_in, stage = halve(acc_in, position)
        if position < 2:
            gone_in, grad = lax.optimization_barrier((gone_in, grad))
        came_in = exchange(gone_in, partner_of(stage))
        if position == 0:
            begun = series_begin(grad, w1)
        if position == 1:
            own, other, table = series_rest(grad, w1, begun)
        acc_in = kept_in + came_in.astype(f32)
    if len(halved) < 1:
        begun = series_begin(grad, w1)
    if len(halved) < 2:
        own, other, table = series_rest(grad, w1, begun)
    mine_out, theirs_out, _ = gather(sum_last(acc_out))
    mine_in, theirs_in, received = gather(sum_last(acc_in), other)

    places = []
    for half in range(2):
        by_side = []
        for narrow in range(2):
            listed = []
            for index in range(blocks):
                value = {None: narrow}
                for position, axis in enumerate(orders[half]):
                    value[axis] = (index >> (len(halved) - 1 - position)) & 1
                place = 0
                for position, axis in enumerate(sequences[half]):
                    place += value[axis] << position
                listed.append(place)
            by_side.append(tuple(listed))
        places.append(tuple(by_side))
    places = tuple(places)

    plan_out = (places, half_out // blocks)
    plan_in = (places, HALF_IN // blocks)
    expanding = [
        pltpu.VMEM((352, FULL), bf16),
        pltpu.VMEM((6, 352, LANES), f32),
        pltpu.VMEM((6, 352, LANES), f32),
        pltpu.VMEM((32, TAPS * D), f32),
        pltpu.SemaphoreType.DMA((22,)),
    ]
    grad_out = pl.pallas_call(
        functools.partial(first_last_kernel, plan_out),
        out_shape=shape((D, TAPS * FF), f32),
        in_specs=[smem, vmem],
        out_specs=hbm,
        scratch_shapes=expanding,
        compiler_params=limit(16),
        cost_estimate=cost(1 << 31),
        name="first_last",
    )(where, mine_out)
    grad_out, grad_in, g_series, g_amps = pl.pallas_call(
        functools.partial(second_last_kernel, plan_out, plan_in),
        out_shape=(
            shape((D, TAPS * FF), f32),
            shape((FF, TAPS * D), f32),
            shape((1, HALF * D), f32),
            shape((1, K), f32),
        ),
        in_specs=[smem] + [vmem] * 6 + [hbm],
        out_specs=[hbm] * 4,
        input_output_aliases={7: 0},
        scratch_shapes=[
            pltpu.VMEM((1, HALF * D), f32),
            pltpu.VMEM((1, K), f32),
            pltpu.SemaphoreType.DMA((2,)),
            *expanding,
            *expanding,
        ],
        compiler_params=limit(24),
        cost_estimate=cost(1 << 32),
        name="second_last",
    )(where, amplitudes, theirs_out, mine_in, own, received, table, grad_out)
    grad_in, g_bias_in, g_bias_out, g_gain, g_shift = pl.pallas_call(
        functools.partial(third_last_kernel, plan_in),
        out_shape=(
            shape((FF, TAPS * D), f32),
            shape((1, FF), f32),
            shape((1, D), f32),
            shape((1, D), f32),
            shape((1, D), f32),
        ),
        in_specs=[smem, vmem, vmem, hbm],
        out_specs=[hbm] * 5,
        input_output_aliases={3: 0},
        scratch_shapes=[pltpu.VMEM((1, D), f32)] * 4 + [pltpu.SemaphoreType.DMA((4,))] + expanding,
        compiler_params=limit(16),
        cost_estimate=cost(1 << 31),
        name="third_last",
    )(where, mine_in, theirs_in, grad_in)
    return (
        out,
        g_series,
        g_amps,
        grad_in.T,
        g_bias_in[0],
        grad_out.T,
        g_bias_out[0],
        g_gain[0],
        g_shift[0],
    )


def solution(mesh):
    in_specs = (
        P("items", None),
        P("items", None),
        P("items", None),
        P(),
        P(),
        P(),
        P(),
        P(),
        P(),
        P("items", "narrow"),
    )
    out_specs = (
        P("items", "narrow"),
        P("items", "narrow"),
        P("items", None),
        P(),
        P(),
        P(),
        P(),
        P(),
        P(),
    )
    return jax.shard_map(
        on_device, mesh=mesh, in_specs=in_specs, out_specs=out_specs, check_vma=False
    )
```
